128 devices in a mesh: loop: 4 (over z_lo, core), dp: 32 (over x, z_hi, y).
Axes of the slice: x: 4, y: 4, z: 4 (z_hi: 2, z_lo: 2; z = z_hi * 2 + z_lo), core: 2. Of those that a mesh axis runs over, the one named last changes fastest.
Arguments:
- tokens: bfloat16 [32768, 640], P(('loop', 'dp')), may hold values from -6 to 6
- cotangent: bfloat16 [32768, 640], P(('loop', 'dp')), may hold values from -6 to 6
- doc_ids: int32 [128, 256], P(('loop', 'dp')), may hold values from 0 to 3, never falling along the last dimension, each value on 1 to 128 neighbouring positions
- doc_source: int32 [128, 4], P(('loop', 'dp')), may hold values from 0 to 7
- mixing: int32 [8], replicated, may hold values from 1 to 9
- norm_gains: float32 [2, 640], replicated, may hold values from 0.1 to 1.9
- wq: bfloat16 [640, 1024], P(None, 'dp'), may hold values from -0.25 to 0.25
- wkv: bfloat16 [640, 512], P(None, 'dp'), may hold values from -0.25 to 0.25
- wo: bfloat16 [1024, 640], P('dp'), may hold values from -0.75 to 0.75
- wgate: bfloat16 [640, 2048], P(None, 'dp'), may hold values from -0.25 to 0.25
- wup: bfloat16 [640, 2048], P(None, 'dp'), may hold values from -0.25 to 0.25
- wdown: bfloat16 [2048, 640], P('dp'), may hold values from -0.125 to 0.125
- adapt_in: bfloat16 [2, 4, 640, 256], replicated, may hold values from -0.25 to 0.25
- adapt_qkv: bfloat16 [2, 256, 1536], replicated, may hold values from -0.375 to 0.375
- adapt_ffn: bfloat16 [2, 2, 256, 2048], replicated, may hold values from -0.375 to 0.375
- adapt_attn: bfloat16 [2, 1024, 256], replicated, may hold values from -0.75 to 0.75
- adapt_down: bfloat16 [2, 2048, 256], replicated, may hold values from -0.125 to 0.125
- adapt_back: bfloat16 [2, 2, 256, 640], replicated, may hold values from -0.375 to 0.375
Outputs:
- block_out: bfloat16 [32768, 640], P(('loop', 'dp'))
- token_grad: float32 [32768, 640], P(('loop', 'dp'))
- gain_grad: float32 [2, 640], replicated
- wq_grad: float32 [640, 1024], P(None, 'dp')
- wkv_grad: float32 [640, 512], P(None, 'dp')
- wo_grad: float32 [1024, 640], P('dp')
- wgate_grad: float32 [640, 2048], P(None, 'dp')
- wup_grad: float32 [640, 2048], P(None, 'dp')
- wdown_grad: float32 [2048, 640], P('dp')
- adapt_in_grad: float32 [2, 4, 640, 256], replicated
- adapt_qkv_grad: float32 [2, 256, 1536], replicated
- adapt_ffn_grad: float32 [2, 2, 256, 2048], replicated
- adapt_attn_grad: float32 [2, 1024, 256], replicated
- adapt_down_grad: float32 [2, 2048, 256], replicated
- adapt_back_grad: float32 [2, 2, 256, 640], replicated
The draws below stay inside these ranges and needn't reach their ends.
Inputs may be any that keep to these rules, and one draw needn't show every extreme that they name: `doc_ids`: in each row, document numbers never fall; every number 0 to 3 appears, each document has 1 to 128 tokens, and one has exactly 128.
All inputs are finite; a program needn't handle non-finite values.
Results may differ from the reference program's by a relative error of at most 0.04.
Values may be sent and summed in bfloat16 or wider, within the bound.
A program may use at most 256 MiB of HBM per device.

```python
import math
import jax
import jax.numpy as jnp
import numpy as np
from jax import lax

D = 640
H = 4
HD = 256
FF = 2048
R = 256
LOOPS = 2
NDATA = 8
DOCS_DEV = 4
TOK_DEV = 256
QW = 1024
MOST_LEN = 128
TOKENS = 32768
N_LOOP = 4
N_DP = 32


def touch_ends(entries, stream_key, smallest, high):
    longest = entries.shape.index(max(entries.shape))
    spots = []
    for shift in (0, 1):
        where = [jax.random.randint(jax.random.fold_in(stream_key, axis), (), 0, length) for axis, length in enumerate(entries.shape)]
        where[longest] = (where[longest] + shift) % entries.shape[longest]
        spots.append(tuple(where))
    return entries.at[spots[0]].set(smallest).at[spots[1]].set(high)


def block_scale(stream_key, dims, split, smallest, high):
    level = 1.0
    for axis_at, parts in split:
        draws = jax.random.uniform(jax.random.fold_in(jax.random.fold_in(stream_key, 6), axis_at), (parts,), jnp.float32, smallest / len(split), high / len(split))
        level = level * jnp.repeat(jnp.exp(draws), dims[axis_at] // parts).reshape((-1,) + (1,) * (len(dims) - 1 - axis_at))
    return level


def profile(count, total, limit, lean):
    portions = [(1 << 20) // math.isqrt(rank ** lean) + 1 for rank in range(2, count + 1)]
    rest, counts = total - limit - (count - 1), [1] * (count - 1)
    while rest > 0:
        movable = [i for i in range(count - 1) if counts[i] < limit]
        mass, left = sum([portions[i] for i in movable]), rest
        for i in movable:
            extra = min(limit - counts[i], max(1, left * portions[i] // mass), rest)
            counts[i] = counts[i] + extra
            rest = rest - extra
    return np.array([limit] + counts)


def ragged_sizes(own_key, number_of, total, bound, lean):
    if number_of == 2:
        one = jax.random.randint(own_key, (), max(1, total - bound), min(bound, total - 1) + 1)
        return jnp.stack([one, total - one])
    sizes = jnp.asarray(profile(number_of, total, bound, lean), jnp.int32)
    pairs = (number_of - 1) // 2
    source_of, receiver = sizes[1:1 + 2 * pairs:2], sizes[2:2 + 2 * pairs:2]
    room = jnp.minimum(source_of - 1, bound - receiver)
    shifted = jax.random.randint(jax.random.fold_in(own_key, 1), (pairs,), 0, 1 << 20) % (room + 1)
    sizes = sizes.at[1:1 + 2 * pairs:2].set(source_of - shifted).at[2:2 + 2 * pairs:2].set(receiver + shifted)
    return sizes[jax.random.permutation(jax.random.fold_in(own_key, 2), number_of)]


def gaussian(key, shape, scale, limit, shards=(), held_as=jnp.bfloat16):
    level = block_scale(key, shape, shards, -0.22, 0.18) if shards else 1.0
    entries = jax.random.normal(key, shape, jnp.float32) * scale * level
    return jnp.minimum(jnp.maximum(entries, -limit), limit).astype(held_as)


def setup_inputs(seed: int = 0) -> dict:
    seeds = jax.random.split(jax.random.key(seed), 19)
    tokens = gaussian(seeds[0], (TOKENS, D), 1.0, 6.0, ((0, 128),))
    cotangent = gaussian(seeds[1], (TOKENS, D), 1.0, 6.0, ((0, 128),))
    doc_ids = jax.vmap(lambda own: jnp.searchsorted(jnp.cumsum(ragged_sizes(own, DOCS_DEV, TOK_DEV, MOST_LEN, 2)), jnp.arange(TOK_DEV), side="right"))(jax.random.split(seeds[2], (N_LOOP * N_DP))).reshape((N_LOOP * N_DP, TOK_DEV)).astype(jnp.int32)
    doc_source = touch_ends(jax.random.randint(seeds[3], (N_LOOP * N_DP, DOCS_DEV), 0, NDATA), jax.random.fold_in(seeds[3], 1), 0, NDATA - 1).astype(jnp.int32)
    mixing = touch_ends(jax.random.randint(seeds[4], (NDATA,), 1, 10), jax.random.fold_in(seeds[4], 1), 1, 9).astype(jnp.int32)
    norm_gains = jnp.clip(1.0 + 0.18 * jax.random.normal(seeds[5], (2, D), jnp.float32), 0.1, 1.9)
    wq = gaussian(seeds[6], (D, QW), D ** -0.5, 0.25, ((1, 32),))
    wkv = gaussian(seeds[7], (D, 2 * HD), D ** -0.5, 0.25, ((1, 32),))
    wo = gaussian(seeds[8], (QW, D), (QW // 16) ** -0.5, 0.75, ((0, 32),))
    wgate = gaussian(seeds[9], (D, FF), D ** -0.5, 0.25, ((1, 32),))
    wup = gaussian(seeds[10], (D, FF), D ** -0.5, 0.25, ((1, 32),))
    wdown = gaussian(seeds[11], (FF, D), FF ** -0.5, 0.125, ((0, 32),))
    adapt_in = gaussian(seeds[12], (LOOPS, 4, D, R), D ** -0.5, 0.25)
    adapt_qkv = gaussian(seeds[13], (LOOPS, R, QW + 2 * HD), R ** -0.5, 0.375)
    adapt_ffn = gaussian(seeds[14], (LOOPS, 2, R, FF), R ** -0.5, 0.375)
    adapt_attn = gaussian(seeds[15], (LOOPS, QW, R), (QW // 16) ** -0.5, 0.75)
    adapt_down = gaussian(seeds[16], (LOOPS, FF, R), FF ** -0.5, 0.125)
    adapt_back = gaussian(seeds[17], (LOOPS, 2, R, D), R ** -0.5, 0.375)
    return dict(tokens=tokens, cotangent=cotangent, doc_ids=doc_ids, doc_source=doc_source, mixing=mixing, norm_gains=norm_gains, wq=wq, wkv=wkv, wo=wo, wgate=wgate, wup=wup, wdown=wdown, adapt_in=adapt_in, adapt_qkv=adapt_qkv, adapt_ffn=adapt_ffn, adapt_attn=adapt_attn, adapt_down=adapt_down, adapt_back=adapt_back)


@jax.custom_vjp
def low(v):
    return lax.optimization_barrier(v.astype(jnp.bfloat16)).astype(jnp.float32)

@jax.custom_vjp
def low_back(v):
    return v

def low_keep(v):
    return (low(v), None)

def low_pass(kept, grad):
    return (grad,)

def back_keep(v):
    return (v, None)

def back_low(kept, grad):
    return (low(grad),)
low.defvjp(low_keep, low_pass)
low_back.defvjp(back_keep, back_low)
eps = 1e-06
rope_base = 10000.0
masked = -1e+30
highest = lax.Precision.HIGHEST

def matmul(left, right):
    return jnp.dot(left, right, precision=highest, preferred_element_type=jnp.float32)

def widen(array):
    return array.astype(jnp.float32)

def rotate(vector, cosine, sine):
    half = vector.shape[-1] // 2
    first_half = vector[..., :half]
    second_half = vector[..., half:]
    return jnp.concatenate([first_half * cosine - second_half * sine, second_half * cosine + first_half * sine], axis=-1)

def rms_norm(stream, gain):
    inverse = lax.rsqrt(lax.optimization_barrier(jnp.mean(stream * stream, axis=-1, keepdims=True)) + eps)
    return stream * inverse * gain

def positions(doc_row):
    index = jnp.arange(doc_row.shape[0], dtype=jnp.int32)
    starts = jnp.concatenate([jnp.ones((1,), dtype=bool), doc_row[1:] != doc_row[:-1]])
    first_index = lax.cummax(jnp.where(starts, index, 0).astype(jnp.int32), axis=0)
    return index - first_index

def layer(stream, gains, shared, adapters, cosine, sine, allowed):
    wq, wkv, wo, wgate, wup, wdown = shared
    adapt_in, adapt_qkv, adapt_ffn, adapt_attn, adapt_down, adapt_back = adapters
    normed_one = low(rms_norm(stream, gains[0]))
    lowrank_one = low(low_back(jnp.einsum('td,jdr->tjr', normed_one, adapt_in[:2], precision=highest)))
    query_pre = low_back(matmul(normed_one, wq) + matmul(lowrank_one[:, 0], adapt_qkv[:, :QW]))
    kv_pre = low_back(matmul(normed_one, wkv) + matmul(lowrank_one[:, 1], adapt_qkv[:, QW:]))
    query_rot = low(rotate(query_pre.reshape(-1, H, HD), cosine[:, None], sine[:, None]))
    key_rot = low(rotate(kv_pre[:, :HD], cosine, sine))
    values = low(kv_pre[:, HD:])
    scores = low_back(jnp.einsum('thd,sd->hts', query_rot, key_rot, precision=highest) * HD ** (-0.5))
    scores = jnp.where(allowed[None], scores, masked)
    highest_score = lax.optimization_barrier(jnp.max(scores, axis=-1, keepdims=True))
    expo = jnp.exp(scores - highest_score)
    attn_probs = low(expo / lax.optimization_barrier(jnp.sum(expo, axis=-1, keepdims=True)))
    attended = low(low_back(jnp.einsum('hts,sd->thd', attn_probs, values, precision=highest).reshape(-1, QW)))
    lowrank_o = low(low_back(matmul(attended, adapt_attn)))
    hidden = stream + low_back(matmul(attended, wo) + matmul(lowrank_o, adapt_back[0]))
    normed_two = low(rms_norm(hidden, gains[1]))
    lowrank_two = low(low_back(jnp.einsum('td,jdr->tjr', normed_two, adapt_in[2:], precision=highest)))
    gate_pre = low_back(matmul(normed_two, wgate) + matmul(lowrank_two[:, 0], adapt_ffn[0]))
    up_proj = low_back(matmul(normed_two, wup) + matmul(lowrank_two[:, 1], adapt_ffn[1]))
    mixed_act = low(jax.nn.gelu(gate_pre, approximate=True) * up_proj)
    lowrank_d = low(low_back(matmul(mixed_act, adapt_down)))
    return hidden + low_back(matmul(mixed_act, wdown) + matmul(lowrank_d, adapt_back[1]))

def reference(tokens, cotangent, doc_ids, doc_source, mixing, norm_gains, wq, wkv, wo, wgate, wup, wdown, adapt_in, adapt_qkv, adapt_ffn, adapt_attn, adapt_down, adapt_back):
    shared = tuple((widen(weight) for weight in (wq, wkv, wo, wgate, wup, wdown)))
    adapters = tuple((widen(weight) for weight in (adapt_in, adapt_qkv, adapt_ffn, adapt_attn, adapt_down, adapt_back)))
    gains = widen(norm_gains)
    mix_ratio = widen(mixing)
    scale_of = mix_ratio * NDATA / jnp.sum(mix_ratio)
    blocks = TOKENS // TOK_DEV
    block_tokens = tokens.reshape(blocks, TOK_DEV, D)
    block_cot = cotangent.reshape(blocks, TOK_DEV, D)
    half = HD // 2
    frequency = rope_base ** (-(2.0 * jnp.arange(half, dtype=jnp.float32)) / HD)

    def step(carry, inputs):
        block_x, block_c, doc_row, sources = inputs
        index = jnp.arange(TOK_DEV, dtype=jnp.int32)
        angle = positions(doc_row).astype(jnp.float32)[:, None] * frequency[None, :]
        cosine = jnp.cos(angle)
        sine = jnp.sin(angle)
        allowed = (doc_row[:, None] == doc_row[None, :]) & (index[None, :] <= index[:, None])
        token_weight = scale_of[sources[doc_row]]

        def forward(stream, gain_arg, shared_arg, adapter_arg):
            for loop_index in range(LOOPS):
                current = tuple((weight[loop_index] for weight in adapter_arg))
                stream = layer(stream, gain_arg, shared_arg, current, cosine, sine, allowed)
            return stream
        result, pull = jax.vjp(forward, widen(block_x), gains, shared, adapters)
        grad_x, grad_gain, grad_shared, grad_adapt = pull(widen(block_c) * token_weight[:, None])
        carry = jax.tree.map(lambda total, term: total + term, carry, (grad_gain, grad_shared, grad_adapt))
        return (carry, (result.astype(jnp.bfloat16), grad_x))
    start = jax.tree.map(jnp.zeros_like, (gains, shared, adapters))
    grads, (outputs, input_grads) = lax.scan(step, start, (block_tokens, block_cot, doc_ids, doc_source))
    grad_gain, grad_shared, grad_adapt = grads
    return (outputs.reshape(TOKENS, D), input_grads.reshape(TOKENS, D), grad_gain, grad_shared[0], grad_shared[1], grad_shared[2], grad_shared[3], grad_shared[4], grad_shared[5], grad_adapt[0], grad_adapt[1], grad_adapt[2], grad_adapt[3], grad_adapt[4], grad_adapt[5])
```

```python
import jax
import jax.numpy as jnp
from jax import lax
from jax.experimental import pallas as pl
from jax.experimental.pallas import tpu as pltpu
from jax.sharding import PartitionSpec as P

eps = 1e-06
rope_base = 10000.0
masked = -1e30
MESH = pl.DeviceIdType.MESH
bf16 = jnp.bfloat16
f32 = jnp.float32

ORDERS = (("x", "y", "z"), ("y", "z", "x"), ("z", "x", "y"))

CHUNKS = {
    "ffn": (0, 0, 8),
    "gate": (0, 8, 5),
    "q": (0, 13, 3),
    "in": (1, 0, 5),
    "qkv": (1, 5, 3),
    "up": (1, 8, 5),
    "o": (1, 13, 3),
    "attn": (2, 0, 2),
    "down": (2, 2, 4),
    "back": (2, 6, 3),
    "wdown": (2, 9, 5),
    "kv": (2, 14, 2),
}
STEPS = ("attn", "qkv", "ffn", "in", "down", "back", "q", "o", "wdown", "gate", "up", "kv")
GROUPS = ((0, 0, 8), (1, 0, 8), (2, 0, 9), (0, 8, 8), (1, 8, 8), (2, 9, 7))
IN_GROUP = tuple(
    tuple(
        k
        for k, name in enumerate(STEPS)
        if CHUNKS[name][0] == part and first <= CHUNKS[name][1] < first + count
    )
    for part, first, count in GROUPS
)


def place():
    lo = lax.axis_index("loop")
    dp = lax.axis_index("dp")
    return {"x": dp // 8, "y": dp % 4, "z": (dp // 4) % 2 * 2 + lo // 2, "c": lo % 2}


def device(at):
    return ((at["z"] % 2) * 2 + at["c"], at["x"] * 8 + (at["z"] // 2) * 4 + at["y"])


def moved(me, axis, by):
    return {**me, axis: (me[axis] + by) % 4}


def other_core(me):
    return {**me, "c": 1 - me["c"]}


def other_low(me):
    return {**me, "z": me["z"] + 1 - 2 * (me["z"] % 2)}


def greet(peers):
    barrier = pltpu.get_barrier_semaphore()
    for peer in peers:
        pl.semaphore_signal(barrier, inc=1, device_id=device(peer), device_id_type=MESH)
    pl.semaphore_wait(barrier, len(peers))


def sending(src, dst, send, recv, peer):
    return pltpu.make_async_remote_copy(
        src_ref=src,
        dst_ref=dst,
        send_sem=send,
        recv_sem=recv,
        device_id=device(peer),
        device_id_type=MESH,
    )


class Gather:
    def __init__(self, me, index, order, piece, region, sems):
        self.me, self.index, self.order, self.piece, self.region = me, index, order, piece, region
        self.send, self.recv, self.core_send, self.core_recv, self.local = sems
        self.sent = []
        self.due = []

    def spot(self, stage, by):
        fixed = {axis: self.me[axis] for axis in self.order[stage:]}
        fixed[self.order[stage]] = (self.me[self.order[stage]] + by) % 4
        return fixed

    def to_core(self, source, fixed, k):
        i, me = self.index, self.me
        copy = sending(
            source,
            self.region(fixed, me["c"]),
            self.core_send.at[i, k],
            self.core_recv.at[i, k],
            other_core(me),
        )
        copy.start()
        self.sent.append(copy)
        there = self.region(fixed, 1 - me["c"])
        self.due.append(
            sending(there, there, self.core_send.at[i, k], self.core_recv.at[i, k], other_core(me))
        )

    def start(self):
        fixed = self.spot(0, 0)
        self.kept = pltpu.make_async_copy(
            self.piece, self.region(fixed, self.me["c"]), self.local.at[self.index]
        )
        self.kept.start()
        self.spread(0, self.piece)
        self.to_core(self.piece, fixed, 0)

    def spread(self, stage, source=None):
        if stage == 1:
            self.kept.wait()
        here = self.region(self.spot(stage, 0), self.me["c"])
        for by in (2, 1, 3):
            copy = sending(
                here if source is None else source,
                here,
                self.send.at[self.index, stage, by - 1],
                self.recv.at[self.index, stage, 3 - by],
                moved(self.me, self.order[stage], by),
            )
            copy.start()
            self.sent.append(copy)

    def arrive(self, stage):
        for by in (1, 3, 2):
            fixed = self.spot(stage, by)
            there = self.region(fixed, self.me["c"])
            sending(
                there,
                there,
                self.send.at[self.index, stage, by - 1],
                self.recv.at[self.index, stage, by - 1],
                moved(self.me, self.order[stage], by),
            ).wait_recv()
            self.to_core(there, fixed, 1 + 3 * stage + by - 1)

    def finish(self):
        for copy in self.due:
            copy.wait_recv()
        for copy in self.sent:
            copy.wait_send()


def gather_sems(items):
    return [
        pltpu.SemaphoreType.DMA((items, 3, 3)),
        pltpu.SemaphoreType.DMA((items, 3, 3)),
        pltpu.SemaphoreType.DMA((items, 10)),
        pltpu.SemaphoreType.DMA((items, 10)),
        pltpu.SemaphoreType.DMA((items,)),
    ]


def chip_peers(me):
    return [moved(me, axis, by) for axis in ("x", "y", "z") for by in (1, 2, 3)]


WEIGHT_ITEMS = (
    (0, 0, 0, 640),
    (1, 1, 0, 640),
    (2, 2, 0, 640),
    (0, 4, 0, 384),
    (1, 3, 0, 384),
    (2, 3, 384, 640),
    (2, 4, 384, 640),
)


def weights_kernel(piece_ref, *refs):
    outs, sems = refs[:5], refs[5:]
    me = place()
    greet(chip_peers(me) + [other_core(me)])
    items = []
    for i, (part, array, low, high) in enumerate(WEIGHT_ITEMS):

        def region(fixed, core, array=array, low=low, high=high):
            every = slice(None)
            zh = fixed["z"] // 2 if "z" in fixed else every
            zl = fixed["z"] % 2 if "z" in fixed else every
            return outs[array].at[
                fixed.get("x", every), zh, fixed.get("y", every), zl, core, :, pl.ds(low, high - low)
            ]

        items.append(
            Gather(
                me,
                i,
                ORDERS[part][::-1],
                piece_ref.at[array, :, pl.ds(low, high - low)],
                region,
                sems,
            )
        )
    for item in items:
        item.start()
    for stage in range(3):
        for item in items:
            item.arrive(stage)
            if stage < 2:
                item.spread(stage + 1)
    for item in items:
        item.finish()


def gathered_weights(pieces):
    shape = jax.ShapeDtypeStruct((4, 2, 4, 2, 2, 16, 640), bf16)
    return pl.pallas_call(
        weights_kernel,
        out_shape=[shape] * 5,
        in_specs=[pl.BlockSpec(memory_space=pltpu.VMEM)],
        out_specs=[pl.BlockSpec(memory_space=pl.ANY)] * 5,
        scratch_shapes=gather_sems(len(WEIGHT_ITEMS)),
        compiler_params=pltpu.CompilerParams(collective_id=1, has_side_effects=True),
        name="weights",
    )(pieces)


NAMES = (
    ("m", 2048),
    ("gf", 640),
    ("gud", 256),
    ("ud", 256),
    ("n2", 640),
    ("ggate", 2048),
    ("gup", 2048),
    ("gu2a", 256),
    ("gu2b", 256),
    ("u2a", 256),
    ("u2b", 256),
    ("o", 1024),
    ("ga", 640),
    ("guo", 256),
    ("uo", 256),
    ("n1", 640),
    ("gqp", 1024),
    ("gkvp", 512),
    ("gu1a", 256),
    ("gu1b", 256),
    ("u1a", 256),
    ("u1b", 256),
)
NEEDS = {
    "attn": ("o", "guo"),
    "qkv": ("u1a", "gqp", "u1b", "gkvp"),
    "ffn": ("u2a", "ggate", "u2b", "gup"),
    "in": ("n1", "n2", "gu1a", "gu1b", "gu2a", "gu2b"),
    "down": ("m", "gud"),
    "back": ("uo", "ga", "ud", "gf"),
    "q": (),
    "o": (),
    "gate": (),
    "up": (),
    "wdown": (),
    "kv": (),
}
LOAD_ORDER = tuple(name for step in STEPS for name in NEEDS[step])


def crossed(left, right):
    return lax.dot_general(
        left, right, (((0,), (0,)), ((), ())), preferred_element_type=f32
    )


def chip_spot(order, x, y, z):
    at = {"x": x, "y": y, "z": z}
    return tuple(at[axis] for axis in order)


def split_spot(q):
    return (q // 16, (q // 4) % 4, q % 4)


def grads_kernel(*refs):
    count = len(NAMES)
    given = {
        (name, loop): refs[loop * count + i] for loop in range(2) for i, (name, _) in enumerate(NAMES)
    }
    gain_ref = refs[2 * count]
    all_ref, share_ref = refs[2 * count + 1 : 2 * count + 3]
    rest = refs[2 * count + 3 :]
    held = {
        (name, loop): rest[loop * count + i] for loop in range(2) for i, (name, _) in enumerate(NAMES)
    }
    rest = rest[2 * count :]
    total, from_core, to_core, got_one, got_two, got_three = rest[:6]
    (load_sem, pair_send, pair_recv, one_send, one_recv, two_send, two_recv, three_send, three_recv) = rest[6:15]
    share_send, share_recv, share_local = rest[15:18]
    spread_sems = rest[18:]

    loads = {}
    for i, name in enumerate(LOAD_ORDER):
        for loop in range(2):
            loads[name, loop] = pltpu.make_async_copy(
                given[name, loop], held[name, loop], load_sem.at[i, loop]
            )
            loads[name, loop].start()
    me = place()
    core = me["c"]
    greet(
        chip_peers(me) + [other_core(me), other_core(other_low(me))]
    )

    def put(part, spot, first, slot, tile, zero, one):
        i, j, k = spot
        own = jnp.where(core == 0, zero, one)
        away = jnp.where(core == 0, one, zero)
        total[part, i, j, k, first + tile] = own.astype(bf16)
        to_core[slot, i, j, k, tile] = away.astype(bf16)

    def shared(left, right, columns):
        return crossed(held[left, 0][:, columns], held[right, 0][...]) + crossed(
            held[left, 1][:, columns], held[right, 1][...]
        )

    def block(i, width=256):
        return pl.ds(pl.multiple_of(i * width, width), width)

    def wide_rows(name, left, right, slot):
        part, first, _ = CHUNKS[name]

        @pl.loop(0, 8)
        def _(i):
            value = shared(left, right, block(i))
            for y in range(4):
                for low in range(2):
                    row = 64 * y + 32 * low
                    for t in range(5):
                        lanes = slice(128 * t, 128 * t + 128)
                        put(
                            part,
                            chip_spot(ORDERS[part], i // 2, y, (i % 2) * 2 + low),
                            first,
                            slot,
                            t,
                            value[row : row + 16, lanes],
                            value[row + 16 : row + 32, lanes],
                        )

    def narrow_rows(name, left, right, slot):
        part, first, _ = CHUNKS[name]

        @pl.loop(0, 4)
        def _(i):
            value = shared(left, right, block(i))
            for high in range(2):
                for y in range(4):
                    for low in range(2):
                        row = 128 * high + 32 * y + 16 * low
                        for t in range(3):
                            u = min(t + 3, 4)
                            put(
                                part,
                                chip_spot(ORDERS[part], i, y, high * 2 + low),
                                first,
                                slot,
                                t,
                                value[row : row + 16, 128 * t : 128 * t + 128],
                                value[row : row + 16, 128 * u : 128 * u + 128],
                            )

    def kv_rows(slot):
        part, first, _ = CHUNKS["kv"]

        @pl.loop(0, 2)
        def _(i):
            value = shared("gkvp", "n1", block(i))
            for k in range(16):
                for low, tiles in enumerate((((0, 3), (1, 3)), ((2, 4), (2, 4)))):
                    for t, (zero, one) in enumerate(tiles):
                        put(
                            part,
                            chip_spot(ORDERS[part], 2 * i + k // 8, k % 4, (k // 4) % 2 * 2 + low),
                            first,
                            slot,
                            t,
                            value[16 * k : 16 * k + 16, 128 * zero : 128 * zero + 128],
                            value[16 * k : 16 * k + 16, 128 * one : 128 * one + 128],
                        )

    def ffn_tiles(slot):
        part, first, _ = CHUNKS["ffn"]
        for loop in range(2):
            for j, (left, right) in enumerate((("u2a", "ggate"), ("u2b", "gup"))):

                @pl.loop(0, 8)
                def _(b, loop=loop, j=j, left=left, right=right):
                    value = crossed(held[left, loop][...], held[right, loop][:, block(b)])
                    for h in range(8):
                        for t in range(2):
                            put(
                                part,
                                (b // 2, (b % 2) * 2 + h // 4, h % 4),
                                first,
                                slot,
                                (loop * 2 + j) * 2 + t,
                                value[32 * h : 32 * h + 16, 128 * t : 128 * t + 128],
                                value[32 * h + 16 : 32 * h + 32, 128 * t : 128 * t + 128],
                            )

    def in_tiles(slot):
        part, first, _ = CHUNKS["in"]
        for loop in range(2):
            for j, name in enumerate(("gu1a", "gu1b", "gu2a", "gu2b")):
                value = crossed(
                    held["n1" if j < 2 else "n2", loop][...], held[name, loop][...]
                )
                for r in range(8):
                    for t in range(5):
                        row = 80 * r + 16 * t
                        put(
                            part,
                            split_spot((loop * 4 + j) * 8 + r),
                            first,
                            slot,
                            t,
                            value[row : row + 16, :128],
                            value[row : row + 16, 128:],
                        )

    def qkv_tiles(slot):
        part, first, _ = CHUNKS["qkv"]
        for loop in range(2):
            for k in range(3):
                if k < 2:
                    right = held["gqp", loop][:, 512 * k : 512 * k + 512]
                    value = crossed(held["u1a", loop][...], right)
                else:
                    value = crossed(held["u1b", loop][...], held["gkvp", loop][...])
                for t in range(4):
                    tile = 4 * k + t
                    for h in range(8):
                        put(
                            part,
                            split_spot(loop * 32 + tile // 3 * 8 + h),
                            first,
                            slot,
                            tile % 3,
                            value[32 * h : 32 * h + 16, 128 * t : 128 * t + 128],
                            value[32 * h + 16 : 32 * h + 32, 128 * t : 128 * t + 128],
                        )

    def tall_tiles(name, left, right, slot):
        part, first, _ = CHUNKS[name]
        blocks = 4 if name == "attn" else 8
        for loop in range(2):

            @pl.loop(0, blocks)
            def _(i, loop=loop):
                value = crossed(held[left, loop][:, block(i)], held[right, loop][...])
                for h in range(8):
                    for t in range(2):
                        if name == "attn":
                            spot = (loop * 2 + i // 2, (i % 2) * 2 + h // 4, h % 4)
                            tile = t
                        else:
                            spot = (i // 2, (i % 2) * 2 + h // 4, h % 4)
                            tile = loop * 2 + t
                        put(
                            part,
                            spot,
                            first,
                            slot,
                            tile,
                            value[32 * h : 32 * h + 16, 128 * t : 128 * t + 128],
                            value[32 * h + 16 : 32 * h + 32, 128 * t : 128 * t + 128],
                        )

    def back_tiles(slot):
        part, first, _ = CHUNKS["back"]
        for loop in range(2):
            for b, (left, right) in enumerate((("uo", "ga"), ("ud", "gf"))):
                value = crossed(held[left, loop][...], held[right, loop][...])
                for g in range(16):
                    rows = slice(16 * g, 16 * g + 16)
                    q = (loop * 2 + b) * 16 + g
                    for t in range(3):
                        u = min(t + 3, 4)
                        one = value[rows, 128 * u : 128 * u + 128]
                        if q == 0 and t == 2:
                            one = gain_ref[...]
                        put(
                            part,
                            split_spot(q),
                            first,
                            slot,
                            t,
                            value[rows, 128 * t : 128 * t + 128],
                            one,
                        )

    def work(name, slot):
        if name == "ffn":
            ffn_tiles(slot)
        elif name == "in":
            in_tiles(slot)
        elif name == "qkv":
            qkv_tiles(slot)
        elif name == "attn":
            tall_tiles(name, "o", "guo", slot)
        elif name == "down":
            tall_tiles(name, "m", "gud", slot)
        elif name == "back":
            back_tiles(slot)
        elif name == "gate":
            wide_rows(name, "ggate", "n2", slot)
        elif name == "up":
            wide_rows(name, "gup", "n2", slot)
        elif name == "wdown":
            wide_rows(name, "m", "gf", slot)
        elif name == "q":
            narrow_rows(name, "gqp", "n1", slot)
        elif name == "o":
            narrow_rows(name, "o", "ga", slot)
        else:
            kv_rows(slot)

    sent = []
    pair = {}

    def combine(k):
        part, first, tiles = CHUNKS[STEPS[k]]
        axis = ORDERS[part][0]
        pair[k].wait_recv()

        @pl.loop(0, 16)
        def _(i):
            for j in range(4):
                at = (part, i // 4, i % 4, j, pl.ds(first, tiles))
                total[at] = (total[at].astype(f32) + from_core[at].astype(f32)).astype(bf16)

        for by in (2, 1, 3):
            copy = sending(
                total.at[part, (me[axis] + by) % 4, :, :, pl.ds(first, tiles)],
                got_one.at[part, 3 - by, :, :, pl.ds(first, tiles)],
                one_send.at[k, by - 1],
                one_recv.at[k, 3 - by],
                moved(me, axis, by),
            )
            copy.start()
            sent.append(copy)

    for k, name in enumerate(STEPS):
        part, first, tiles = CHUNKS[name]
        slot = k % 2
        for need in NEEDS[name]:
            loads[need, 0].wait()
            loads[need, 1].wait()
        if k >= 2:
            pair[k - 2].wait_send()
        work(name, slot)
        pair[k] = sending(
            to_core.at[slot, :, :, :, pl.ds(0, tiles)],
            from_core.at[part, :, :, :, pl.ds(first, tiles)],
            pair_send.at[k],
            pair_recv.at[k],
            other_core(me),
        )
        pair[k].start()
        if k >= 1:
            combine(k - 1)
    combine(len(STEPS) - 1)
    pair[len(STEPS) - 2].wait_send()
    pair[len(STEPS) - 1].wait_send()

    def second(g):
        part, first, tiles = GROUPS[g]
        one, two, _ = ORDERS[part]
        for k in IN_GROUP[g]:
            _, start, length = CHUNKS[STEPS[k]]
            for by in (1, 3, 2):
                there = got_one.at[part, by - 1, :, :, pl.ds(start, length)]
                sending(
                    there, there, one_send.at[k, by - 1], one_recv.at[k, by - 1], moved(me, one, by)
                ).wait_recv()

        @pl.loop(0, 16)
        def _(i):
            at = (part, me[one], i // 4, i % 4, pl.ds(first, tiles))
            value = total[at].astype(f32)
            for s in range(3):
                value += got_one[part, s, i // 4, i % 4, pl.ds(first, tiles)].astype(f32)
            total[at] = value.astype(bf16)

        for by in (2, 1, 3):
            copy = sending(
                total.at[part, me[one], (me[two] + by) % 4, :, pl.ds(first, tiles)],
                got_two.at[part, 3 - by, :, pl.ds(first, tiles)],
                two_send.at[g, by - 1],
                two_recv.at[g, 3 - by],
                moved(me, two, by),
            )
            copy.start()
            sent.append(copy)

    def third(g):
        part, first, tiles = GROUPS[g]
        one, two, three = ORDERS[part]
        for by in (1, 3, 2):
            there = got_two.at[part, by - 1, :, pl.ds(first, tiles)]
            sending(
                there, there, two_send.at[g, by - 1], two_recv.at[g, by - 1], moved(me, two, by)
            ).wait_recv()

        @pl.loop(0, 4)
        def _(i):
            at = (part, me[one], me[two], i, pl.ds(first, tiles))
            value = total[at].astype(f32)
            for s in range(3):
                value += got_two[part, s, i, pl.ds(first, tiles)].astype(f32)
            total[at] = value.astype(bf16)

        for by in (2, 1, 3):
            copy = sending(
                total.at[part, me[one], me[two], (me[three] + by) % 4, pl.ds(first, tiles)],
                got_three.at[part, 3 - by, pl.ds(first, tiles)],
                three_send.at[g, by - 1],
                three_recv.at[g, 3 - by],
                moved(me, three, by),
            )
            copy.start()
            sent.append(copy)

    def last(g):
        part, first, tiles = GROUPS[g]
        one, two, three = ORDERS[part]
        for by in (1, 3, 2):
            there = got_three.at[part, by - 1, pl.ds(first, tiles)]
            sending(
                there, there, three_send.at[g, by - 1], three_recv.at[g, by - 1], moved(me, three, by)
            ).wait_recv()
        at = (part, me[one], me[two], me[three], pl.ds(first, tiles))
        value = total[at].astype(f32)
        for s in range(3):
            value += got_three[part, s, pl.ds(first, tiles)].astype(f32)
        total[at] = value.astype(bf16)
        return total.at[at]

    gathers = []

    def start_gather(g):
        part, first, tiles = GROUPS[g]
        order = ORDERS[part]

        def region(fixed, core):
            spot = tuple(fixed.get(axis, slice(None)) for axis in order)
            return all_ref.at[(core, part, *spot, pl.ds(first, tiles))]

        gathers.append(Gather(me, part, order[::-1], last(g), region, spread_sems))
        gathers[-1].start()

    shares = []

    def share(g):
        part, first, tiles = GROUPS[g]
        mine = last(g)
        low = me["z"] % 2

        def spot(low, core):
            return share_ref.at[low * 2 + core, part, pl.ds(0, tiles)]

        local = pltpu.make_async_copy(mine, spot(low, core), share_local.at[part])
        local.start()
        shares.append(local.wait)
        for k, peer in enumerate(
            (other_low(me), other_core(me), other_core(other_low(me)))
        ):
            copy = sending(
                mine, spot(low, core), share_send.at[part, k], share_recv.at[part, k], peer
            )
            copy.start()
            sent.append(copy)
            there = spot(peer["z"] % 2, peer["c"])
            shares.append(
                sending(there, there, share_send.at[part, k], share_recv.at[part, k], peer).wait_recv
            )

    for g in range(3):
        second(g)
    for g in range(3):
        third(g)
    for g in range(3):
        start_gather(g)
    for g in range(3, 6):
        second(g)
    for item in gathers:
        item.arrive(0)
        item.spread(1)
    for g in range(3, 6):
        third(g)
    for item in gathers:
        item.arrive(1)
        item.spread(2)
    for g in range(3, 6):
        share(g)
    for item in gathers:
        item.arrive(2)
    for item in gathers:
        item.finish()
    for wait in shares:
        wait()
    for copy in sent:
        copy.wait_send()


def summed_gradients(states, gain_tile):
    operands = [states[loop][name] for loop in range(2) for name, _ in NAMES] + [gain_tile]
    anywhere = pl.BlockSpec(memory_space=pl.ANY)
    dma = pltpu.SemaphoreType.DMA
    return pl.pallas_call(
        grads_kernel,
        out_shape=[
            jax.ShapeDtypeStruct((2, 3, 4, 4, 4, 9, 16, 128), bf16),
            jax.ShapeDtypeStruct((4, 3, 8, 16, 128), bf16),
        ],
        in_specs=[anywhere] * (2 * len(NAMES)) + [pl.BlockSpec(memory_space=pltpu.VMEM)],
        out_specs=[anywhere] * 2,
        scratch_shapes=[
            pltpu.VMEM((256, width), bf16) for loop in range(2) for _, width in NAMES
        ]
        + [
            pltpu.VMEM((3, 4, 4, 4, 16, 16, 128), bf16),
            pltpu.VMEM((3, 4, 4, 4, 16, 16, 128), bf16),
            pltpu.VMEM((2, 4, 4, 4, 8, 16, 128), bf16),
            pltpu.VMEM((3, 3, 4, 4, 16, 16, 128), bf16),
            pltpu.VMEM((3, 3, 4, 16, 16, 128), bf16),
            pltpu.VMEM((3, 3, 16, 16, 128), bf16),
            dma((len(NAMES), 2)),
            dma((len(STEPS),)),
            dma((len(STEPS),)),
            dma((len(STEPS), 3)),
            dma((len(STEPS), 3)),
            dma((6, 3)),
            dma((6, 3)),
            dma((6, 3)),
            dma((6, 3)),
            dma((3, 3)),
            dma((3, 3)),
            dma((3,)),
        ]
        + gather_sems(3),
        compiler_params=pltpu.CompilerParams(
            collective_id=2, has_side_effects=True, vmem_limit_bytes=60 * 2**20
        ),
        name="grads",
    )(*operands)


def unpack_kernel(all_ref, share_ref, *outs):
    (gain, wq, wkv, wo, wgate, wup, wdown, w_in, w_qkv, w_ffn, w_attn, w_down, w_back) = outs

    def tile(core, part, q, t):
        return all_ref[core, part, q, t].astype(f32)

    for q in range(8):
        for core in range(2):
            for t in range(5):
                w_in[0, 0, 80 * q + 16 * t : 80 * q + 16 * t + 16, 128 * core : 128 * core + 128] = tile(core, 1, q, t)
            for t in range(3):
                w_qkv[0, 32 * q + 16 * core : 32 * q + 16 * core + 16, 128 * t : 128 * t + 128] = tile(core, 1, q, 5 + t)
            row = slice(32 * q + 16 * core, 32 * q + 16 * core + 16)
            for k in range(4):
                for t in range(2):
                    w_ffn[k // 2, k % 2, row, 128 * t : 128 * t + 128] = tile(core, 0, q, 2 * k + t)
            for t in range(2):
                lanes = slice(128 * t, 128 * t + 128)
                w_attn[0, row, lanes] = tile(core, 2, q, t)
                for loop in range(2):
                    w_down[loop, row, lanes] = tile(core, 2, q, 2 + loop * 2 + t)
            for t in range(3 - core):
                u = 3 * core + t
                w_back[0, 0, 16 * q : 16 * q + 16, 128 * u : 128 * u + 128] = tile(core, 2, q, 6 + t)

    @pl.when(pl.program_id(0) == 0)
    def _():
        gain[...] = tile(1, 2, 0, 8)

        def mine(low, core, part, t):
            return share_ref[low * 2 + core, part, t].astype(f32)

        def wide(part, first):
            rows = []
            for low in range(2):
                for core in range(2):
                    rows.append(jnp.concatenate([mine(low, core, part, first + t) for t in range(5)], axis=1))
            return jnp.concatenate(rows, axis=0)

        def narrow(part, first):
            rows = []
            for low in range(2):
                tiles = [mine(low, 0, part, first + t) for t in range(3)]
                tiles += [mine(low, 1, part, first + t) for t in range(2)]
                rows.append(jnp.concatenate(tiles, axis=1))
            return jnp.concatenate(rows, axis=0)

        wgate[...] = wide(0, 0).T
        wup[...] = wide(1, 0).T
        wdown[...] = wide(2, 0)
        wq[...] = narrow(0, 5).T
        wo[...] = narrow(1, 5)
        kv = [mine(0, 0, 2, 5), mine(0, 0, 2, 6), mine(1, 0, 2, 5), mine(0, 1, 2, 5), mine(1, 1, 2, 5)]
        wkv[...] = jnp.concatenate(kv, axis=1).T


def unpacked(everything, shares):
    def whole(*shape):
        return jax.ShapeDtypeStruct(shape, f32), pl.BlockSpec(shape, lambda i: (0,) * len(shape))

    def cut(shape, block, index):
        return jax.ShapeDtypeStruct(shape, f32), pl.BlockSpec(block, index)

    outs = [
        whole(16, 128),
        whole(640, 32),
        whole(640, 16),
        whole(32, 640),
        whole(640, 64),
        whole(640, 64),
        whole(64, 640),
        cut((2, 4, 640, 256), (1, 1, 640, 256), lambda i: (i // 4, i % 4, 0, 0)),
        cut((2, 256, 1536), (1, 256, 384), lambda i: (i // 4, 0, i % 4)),
        cut((2, 2, 256, 2048), (2, 2, 256, 256), lambda i: (0, 0, 0, i)),
        cut((2, 1024, 256), (1, 256, 256), lambda i: (i // 4, i % 4, 0)),
        cut((2, 2048, 256), (2, 256, 256), lambda i: (0, i, 0)),
        cut((2, 2, 256, 640), (1, 1, 128, 640), lambda i: (i // 4, (i // 2) % 2, i % 2, 0)),
    ]
    return pl.pallas_call(
        unpack_kernel,
        grid=(8,),
        out_shape=[shape for shape, _ in outs],
        in_specs=[
            pl.BlockSpec((2, 3, 8, 9, 16, 128), lambda i: (0, 0, i, 0, 0, 0)),
            pl.BlockSpec((4, 3, 8, 16, 128), lambda i: (0, 0, 0, 0, 0)),
        ],
        out_specs=[spec for _, spec in outs],
        compiler_params=pltpu.CompilerParams(vmem_limit_bytes=40 * 2**20),
        name="unpack",
    )(everything.reshape(2, 3, 64, 9, 16, 128), shares)


def product(left, right):
    return jnp.dot(left, right, preferred_element_type=f32)


def against(left, right):
    return lax.dot_general(left, right, (((1,), (1,)), ((), ())), preferred_element_type=f32)


def rotate(vector, cosine, sine):
    half = vector.shape[-1] // 2
    first_half = vector[..., :half]
    second_half = vector[..., half:]
    return jnp.concatenate(
        [first_half * cosine - second_half * sine, second_half * cosine + first_half * sine],
        axis=-1,
    )


def norm_back(grad_norm, stream, inverse, gain):
    scaled = grad_norm * gain
    grad_stream = inverse * (
        scaled - stream * inverse * inverse * jnp.mean(scaled * stream, axis=-1, keepdims=True)
    )
    return (grad_stream, jnp.sum(grad_norm * stream * inverse, axis=0))


def attention_scores(query_rot, key_rot, allowed, score_scale):
    scores = (
        jnp.einsum("thd,sd->hts", query_rot, key_rot, preferred_element_type=f32) * score_scale
    )
    return jnp.where(allowed[None], scores, masked)


def forward_loop(stream, gains, weights, adapters, cosine, sine, allowed):
    wq, wkv, wo, wgate, wup, wdown = weights
    adapt_in, adapt_qkv, adapt_ffn, adapt_attn, adapt_down, adapt_back = adapters
    row_count = stream.shape[0]
    query_width = wq.shape[0]
    head_dim = wkv.shape[0] // 2
    score_scale = head_dim ** (-0.5)
    kept = {"stream": stream}
    inv_first = lax.rsqrt(jnp.mean(stream * stream, axis=-1, keepdims=True) + eps)
    n1 = (stream * inv_first * gains[0]).astype(bf16)
    u1a = product(n1, adapt_in[0]).astype(bf16)
    u1b = product(n1, adapt_in[1]).astype(bf16)
    query_pre = against(n1, wq) + product(u1a, adapt_qkv[:, :query_width])
    kv_pre = against(n1, wkv) + product(u1b, adapt_qkv[:, query_width:])
    query_rot = rotate(
        query_pre.reshape(row_count, -1, head_dim), cosine[:, None], sine[:, None]
    ).astype(bf16)
    key_rot = rotate(kv_pre[:, :head_dim], cosine, sine).astype(bf16)
    values = kv_pre[:, head_dim:].astype(bf16)
    scores = attention_scores(query_rot, key_rot, allowed, score_scale)
    highest_score = jnp.max(scores, axis=-1, keepdims=True)
    log_total = highest_score + jnp.log(
        jnp.sum(jnp.exp(scores - highest_score), axis=-1, keepdims=True)
    )
    attn_probs = jnp.exp(scores - log_total).astype(bf16)
    attended = (
        jnp.einsum("hts,sd->thd", attn_probs, values, preferred_element_type=f32)
        .reshape(row_count, -1)
        .astype(bf16)
    )
    uo = product(attended, adapt_attn).astype(bf16)
    hidden = stream + (product(attended, wo) + product(uo, adapt_back[0]))
    inv_second = lax.rsqrt(jnp.mean(hidden * hidden, axis=-1, keepdims=True) + eps)
    n2 = (hidden * inv_second * gains[1]).astype(bf16)
    u2a = product(n2, adapt_in[2]).astype(bf16)
    u2b = product(n2, adapt_in[3]).astype(bf16)
    gate_pre = against(n2, wgate) + product(u2a, adapt_ffn[0])
    up_proj = against(n2, wup) + product(u2b, adapt_ffn[1])
    m = (jax.nn.gelu(gate_pre, approximate=True) * up_proj).astype(bf16)
    ud = product(m, adapt_down).astype(bf16)
    result = hidden + (product(m, wdown) + product(ud, adapt_back[1]))
    kept.update(
        inv_first=inv_first,
        query_rot=query_rot,
        key_rot=key_rot,
        values=values,
        log_total=log_total,
        hidden=hidden,
        inv_second=inv_second,
        gate_pre=gate_pre,
        up_proj=up_proj,
        n1=n1,
        u1a=u1a,
        u1b=u1b,
        o=attended,
        uo=uo,
        n2=n2,
        u2a=u2a,
        u2b=u2b,
        m=m,
        ud=ud,
    )
    return (result, kept)


def backward_loop(grad_out, gains, weights, adapters, cosine, sine, allowed, kept):
    wq, wkv, wo, wgate, wup, wdown = weights
    adapt_in, adapt_qkv, adapt_ffn, adapt_attn, adapt_down, adapt_back = adapters
    row_count = grad_out.shape[0]
    query_width = wq.shape[0]
    head_dim = wkv.shape[0] // 2
    score_scale = head_dim ** (-0.5)
    hidden, stream = kept["hidden"], kept["stream"]
    gf = grad_out.astype(bf16)
    gud = against(gf, adapt_back[1]).astype(bf16)
    grad_mixed = against(gf, wdown) + against(gud, adapt_down)
    activation, gelu_pull = jax.vjp(
        lambda inner: jax.nn.gelu(inner, approximate=True), kept["gate_pre"]
    )
    ggate = gelu_pull(grad_mixed * kept["up_proj"])[0].astype(bf16)
    gup = (grad_mixed * activation).astype(bf16)
    gu2a = against(ggate, adapt_ffn[0]).astype(bf16)
    gu2b = against(gup, adapt_ffn[1]).astype(bf16)
    grad_normed_two = (
        product(ggate, wgate)
        + product(gup, wup)
        + against(gu2a, adapt_in[2])
        + against(gu2b, adapt_in[3])
    )
    grad_hidden_norm, grad_gain_two = norm_back(
        grad_normed_two, hidden, kept["inv_second"], gains[1]
    )
    grad_hidden = grad_out + grad_hidden_norm
    ga = grad_hidden.astype(bf16)
    guo = against(ga, adapt_back[0]).astype(bf16)
    grad_att = (
        (against(ga, wo) + against(guo, adapt_attn)).astype(bf16).reshape(row_count, -1, head_dim)
    )
    query_rot, key_rot = kept["query_rot"], kept["key_rot"]
    scores = attention_scores(query_rot, key_rot, allowed, score_scale)
    attn_probs = jnp.exp(scores - kept["log_total"])
    grad_probs = jnp.einsum("thd,sd->hts", grad_att, kept["values"], preferred_element_type=f32)
    grad_scores = (
        attn_probs * (grad_probs - jnp.sum(attn_probs * grad_probs, axis=-1, keepdims=True))
    ).astype(bf16)
    grad_values = jnp.einsum(
        "hts,thd->sd", attn_probs.astype(bf16), grad_att, preferred_element_type=f32
    )
    grad_query = (
        jnp.einsum("hts,sd->thd", grad_scores, key_rot, preferred_element_type=f32) * score_scale
    )
    grad_key = (
        jnp.einsum("hts,thd->sd", grad_scores, query_rot, preferred_element_type=f32)
        * score_scale
    )
    gqp = (
        rotate(grad_query, cosine[:, None], -sine[:, None]).reshape(row_count, -1).astype(bf16)
    )
    gkvp = jnp.concatenate([rotate(grad_key, cosine, -sine), grad_values], axis=1).astype(bf16)
    gu1a = against(gqp, adapt_qkv[:, :query_width]).astype(bf16)
    gu1b = against(gkvp, adapt_qkv[:, query_width:]).astype(bf16)
    grad_normed_one = (
        product(gqp, wq)
        + product(gkvp, wkv)
        + against(gu1a, adapt_in[0])
        + against(gu1b, adapt_in[1])
    )
    grad_stream_norm, grad_gain_one = norm_back(
        grad_normed_one, stream, kept["inv_first"], gains[0]
    )
    grad_stream = grad_hidden + grad_stream_norm
    kept.update(
        gf=gf,
        gud=gud,
        ggate=ggate,
        gup=gup,
        gu2a=gu2a,
        gu2b=gu2b,
        ga=ga,
        guo=guo,
        gqp=gqp,
        gkvp=gkvp,
        gu1a=gu1a,
        gu1b=gu1b,
    )
    return (grad_stream, jnp.stack([grad_gain_one, grad_gain_two]))


def body(
    tokens,
    cotangent,
    doc_ids,
    doc_source,
    mixing,
    norm_gains,
    wq,
    wkv,
    wo,
    wgate,
    wup,
    wdown,
    adapt_in,
    adapt_qkv,
    adapt_ffn,
    adapt_attn,
    adapt_down,
    adapt_back,
):
    me = place()
    quarter = (me["z"] % 2) * 2 + me["c"]

    def mine(rows):
        return lax.dynamic_slice_in_dim(rows, quarter * 16, 16, axis=0)

    pieces = jnp.stack(
        [
            mine(wgate.T),
            mine(wup.T),
            mine(wdown),
            mine(jnp.concatenate([wq.T, wo], axis=0)),
            wkv.T,
        ]
    )
    full_gate, full_up, full_down, both, full_kv = gathered_weights(pieces)
    both = both.reshape(32, 2, 32, 640)
    weights = (
        both[:, 0].reshape(1024, 640),
        full_kv.reshape(32, 4, 16, 640)[:, 0].reshape(512, 640),
        both[:, 1].reshape(1024, 640),
        full_gate.reshape(2048, 640),
        full_up.reshape(2048, 640),
        full_down.reshape(2048, 640),
    )
    adapter_args = (adapt_in, adapt_qkv, adapt_ffn, adapt_attn, adapt_down, adapt_back)
    loop_count = adapt_in.shape[0]
    doc_row = doc_ids[0]
    sources = doc_source[0]
    row_count = doc_row.shape[0]
    head_dim = 256
    index = jnp.arange(row_count, dtype=jnp.int32)
    first_index = jnp.sum((doc_row[None, :] < doc_row[:, None]).astype(jnp.int32), axis=1)
    frequency = rope_base ** (-(2.0 * jnp.arange(head_dim // 2, dtype=f32)) / head_dim)
    angle = (index - first_index).astype(f32)[:, None] * frequency[None, :]
    cosine = jnp.cos(angle)
    sine = jnp.sin(angle)
    allowed = (doc_row[:, None] == doc_row[None, :]) & (index[None, :] <= index[:, None])
    mix_ratio = mixing.astype(f32)
    scale_of = mix_ratio * mix_ratio.shape[0] / jnp.sum(mix_ratio)
    dataset_ids = jnp.arange(mix_ratio.shape[0], dtype=jnp.int32)
    doc_weight = jnp.sum(
        jnp.where(sources[:, None] == dataset_ids[None, :], scale_of[None, :], 0.0), axis=1
    )
    doc_numbers = jnp.arange(sources.shape[0], dtype=jnp.int32)
    token_weight = jnp.sum(
        jnp.where(doc_row[:, None] == doc_numbers[None, :], doc_weight[None, :], 0.0), axis=1
    )
    stream = tokens.astype(f32)
    states = []
    for step in range(loop_count):
        current = tuple((weight[step] for weight in adapter_args))
        stream, kept = forward_loop(stream, norm_gains, weights, current, cosine, sine, allowed)
        states.append(kept)
    block_out = stream.astype(bf16)
    grad_stream = cotangent.astype(f32) * token_weight[:, None]
    gain_total = jnp.zeros_like(norm_gains)
    for step in reversed(range(loop_count)):
        current = tuple((weight[step] for weight in adapter_args))
        grad_stream, gain_term = backward_loop(
            grad_stream, norm_gains, weights, current, cosine, sine, allowed, states[step]
        )
        gain_total = gain_total + gain_term
    gain_tile = jnp.pad(gain_total.reshape(10, 128), ((0, 6), (0, 0)))
    everything, shares = summed_gradients(states, gain_tile)
    gain, *sums = unpacked(everything, shares)
    return (block_out, grad_stream, gain[:10].reshape(2, 640), *sums)


def solution(mesh):
    rows = P(("loop", "dp"), None)
    columns = P(None, "dp")
    placed = (
        *(rows,) * 4,
        P(),
        P(),
        columns,
        columns,
        P("dp", None),
        columns,
        columns,
        P("dp", None),
        *(P(),) * 6,
    )
    return jax.shard_map(
        body,
        mesh=mesh,
        in_specs=placed,
        out_specs=(
            rows,
            rows,
            P(),
            columns,
            columns,
            P("dp", None),
            columns,
            columns,
            P("dp", None),
            *(P(),) * 6,
        ),
        check_vma=False,
    )
```

```python
import jax
import jax.numpy as jnp
from jax import lax
from jax.experimental import pallas as pl
from jax.experimental.pallas import tpu as pltpu
from jax.sharding import PartitionSpec as P

eps = 1e-06
rope_base = 10000.0
masked = -1e30
MESH = pl.DeviceIdType.MESH
bf16 = jnp.bfloat16
f32 = jnp.float32

ORDERS = (("x", "y", "z"), ("y", "z", "x"), ("z", "x", "y"))

CHUNKS = {
    "ffn": (0, 0, 8),
    "gate": (0, 8, 5),
    "q": (0, 13, 3),
    "in": (1, 0, 5),
    "qkv": (1, 5, 3),
    "up": (1, 8, 5),
    "o": (1, 13, 3),
    "attn": (2, 0, 2),
    "down": (2, 2, 4),
    "back": (2, 6, 3),
    "wdown": (2, 9, 5),
    "kv": (2, 14, 2),
}
STEPS = ("attn", "qkv", "ffn", "in", "down", "back", "q", "o", "wdown", "gate", "up", "kv")
GROUPS = ((0, 0, 8), (1, 0, 8), (2, 0, 9), (0, 8, 8), (1, 8, 8), (2, 9, 7))
IN_GROUP = tuple(
    tuple(
        k
        for k, name in enumerate(STEPS)
        if CHUNKS[name][0] == part and first <= CHUNKS[name][1] < first + count
    )
    for part, first, count in GROUPS
)


def place():
    lo = lax.axis_index("loop")
    dp = lax.axis_index("dp")
    return {"x": dp // 8, "y": dp % 4, "z": (dp // 4) % 2 * 2 + lo // 2, "c": lo % 2}


def device(at):
    return ((at["z"] % 2) * 2 + at["c"], at["x"] * 8 + (at["z"] // 2) * 4 + at["y"])


def moved(me, axis, by):
    return {**me, axis: (me[axis] + by) % 4}


def other_core(me):
    return {**me, "c": 1 - me["c"]}


def other_low(me):
    return {**me, "z": me["z"] + 1 - 2 * (me["z"] % 2)}


def greet(peers):
    barrier = pltpu.get_barrier_semaphore()
    for peer in peers:
        pl.semaphore_signal(barrier, inc=1, device_id=device(peer), device_id_type=MESH)
    pl.semaphore_wait(barrier, len(peers))


def sending(src, dst, send, recv, peer):
    return pltpu.make_async_remote_copy(
        src_ref=src,
        dst_ref=dst,
        send_sem=send,
        recv_sem=recv,
        device_id=device(peer),
        device_id_type=MESH,
    )


class Gather:
    def __init__(self, me, index, order, piece, region, sems):
        self.me, self.index, self.order, self.piece, self.region = me, index, order, piece, region
        self.send, self.recv, self.core_send, self.core_recv, self.local = sems
        self.sent = []
        self.due = []

    def spot(self, stage, by):
        fixed = {axis: self.me[axis] for axis in self.order[stage:]}
        fixed[self.order[stage]] = (self.me[self.order[stage]] + by) % 4
        return fixed

    def to_core(self, source, fixed, k):
        i, me = self.index, self.me
        copy = sending(
            source,
            self.region(fixed, me["c"]),
            self.core_send.at[i, k],
            self.core_recv.at[i, k],
            other_core(me),
        )
        copy.start()
        self.sent.append(copy)
        there = self.region(fixed, 1 - me["c"])
        self.due.append(
            sending(there, there, self.core_send.at[i, k], self.core_recv.at[i, k], other_core(me))
        )

    def start(self):
        fixed = self.spot(0, 0)
        self.kept = pltpu.make_async_copy(
            self.piece, self.region(fixed, self.me["c"]), self.local.at[self.index]
        )
        self.kept.start()
        self.spread(0, self.piece)
        self.to_core(self.piece, fixed, 0)

    def spread(self, stage, source=None):
        if stage == 1:
            self.kept.wait()
        here = self.region(self.spot(stage, 0), self.me["c"])
        for by in (2, 1, 3):
            copy = sending(
                here if source is None else source,
                here,
                self.send.at[self.index, stage, by - 1],
                self.recv.at[self.index, stage, 3 - by],
                moved(self.me, self.order[stage], by),
            )
            copy.start()
            self.sent.append(copy)

    def arrive(self, stage):
        for by in (1, 3, 2):
            fixed = self.spot(stage, by)
            there = self.region(fixed, self.me["c"])
            sending(
                there,
                there,
                self.send.at[self.index, stage, by - 1],
                self.recv.at[self.index, stage, by - 1],
                moved(self.me, self.order[stage], by),
            ).wait_recv()
            self.to_core(there, fixed, 1 + 3 * stage + by - 1)

    def finish(self):
        for copy in self.due:
            copy.wait_recv()
        for copy in self.sent:
            copy.wait_send()


def gather_sems(items):
    return [
        pltpu.SemaphoreType.DMA((items, 3, 3)),
        pltpu.SemaphoreType.DMA((items, 3, 3)),
        pltpu.SemaphoreType.DMA((items, 10)),
        pltpu.SemaphoreType.DMA((items, 10)),
        pltpu.SemaphoreType.DMA((items,)),
    ]


def chip_peers(me):
    return [moved(me, axis, by) for axis in ("x", "y", "z") for by in (1, 2, 3)]


WEIGHT_ITEMS = (
    (1, 3, 0, 384),
    (2, 3, 384, 640),
    (0, 4, 0, 384),
    (2, 4, 384, 640),
    (0, 0, 0, 640),
    (1, 1, 0, 640),
    (2, 2, 0, 640),
)

NAMES = (
    ("m", 2048),
    ("gf", 640),
    ("gud", 256),
    ("ud", 256),
    ("n2", 640),
    ("ggate", 2048),
    ("gup", 2048),
    ("gu2a", 256),
    ("gu2b", 256),
    ("u2a", 256),
    ("u2b", 256),
    ("o", 1024),
    ("ga", 640),
    ("guo", 256),
    ("uo", 256),
    ("n1", 640),
    ("gqp", 1024),
    ("gkvp", 512),
    ("gu1a", 256),
    ("gu1b", 256),
    ("u1a", 256),
    ("u1b", 256),
)
ADAPTERS = ((4, 640, 256), (256, 1536), (2, 256, 2048), (1024, 256), (2048, 256), (2, 256, 640))


def product(left, right):
    return lax.dot_general(left, right, (((1,), (0,)), ((), ())), preferred_element_type=f32)


def against(left, right):
    return lax.dot_general(left, right, (((1,), (1,)), ((), ())), preferred_element_type=f32)


def crossed(left, right):
    return lax.dot_general(left, right, (((0,), (0,)), ((), ())), preferred_element_type=f32)


def block(i, width=256):
    return pl.ds(pl.multiple_of(i * width, width), width)


CURVE = 0.7978845608028654
CUBE = 0.044715


def block_kernel(*refs):
    (tokens, cotangent, doc_row, doc_source, mixing, gains) = refs[:6]
    shards = refs[6:12]
    adapters_in = refs[12:18]
    outs = refs[18:]
    block_out, token_grad, gain_tile = outs[:3]
    kept_out = dict(zip((name for name, _ in NAMES), outs[3 : 3 + len(NAMES)]))
    rest = outs[3 + len(NAMES) :]
    kept = dict(zip((name for name, _ in NAMES), rest[: len(NAMES)]))
    rest = rest[len(NAMES) :]
    whole = rest[:5]
    both_piece = rest[5]
    a_in, a_qkv, a_ffn, a_attn, a_down, a_back = rest[6:12]
    (cosine, sine, mask, stream, hidden, q_rot, k_rot, value, probs, gate, up, grad, normed, gain_sum) = rest[12:26]
    kept_sem, adapter_sem, piece_sem = rest[26:29]
    gather = rest[29:]

    me = place()
    quarter = (me["z"] % 2) * 2 + me["c"]
    w_gate, w_up, w_down, w_both, w_kv = whole

    fetch = [
        pltpu.make_async_copy(shards[0], both_piece.at[:32], piece_sem.at[0]),
        pltpu.make_async_copy(shards[2], both_piece.at[32:], piece_sem.at[1]),
    ]
    for copy in fetch:
        copy.start()
    adapters = []
    for loop in range(2):
        for i, (source, target) in enumerate(
            zip(adapters_in, (a_in, a_qkv, a_ffn, a_attn, a_down, a_back))
        ):
            copy = pltpu.make_async_copy(source.at[loop], target.at[loop], adapter_sem.at[loop, i])
            copy.start()
            adapters.append(copy)
    greet(chip_peers(me) + [other_core(me)])
    for copy in fetch:
        copy.wait()
    own = pl.ds(pl.multiple_of(quarter * 16, 16), 16)
    sources = (shards[3].at[own], shards[4].at[own], shards[5].at[own], both_piece.at[own], shards[1])
    items = []
    for i, (part, array, low, high) in enumerate(WEIGHT_ITEMS):

        def region(fixed, core, array=array, low=low, high=high):
            every = slice(None)
            zh = fixed["z"] // 2 if "z" in fixed else every
            zl = fixed["z"] % 2 if "z" in fixed else every
            return whole[array].at[
                fixed.get("x", every), zh, fixed.get("y", every), zl, core, :, pl.ds(low, high - low)
            ]

        items.append(
            Gather(me, i, ORDERS[part][::-1], sources[array].at[:, pl.ds(low, high - low)], region, gather)
        )
    for item in items:
        item.start()

    rows_of = lax.broadcasted_iota(jnp.int32, (256, 256), 0)
    columns_of = lax.broadcasted_iota(jnp.int32, (256, 256), 1)
    along = jnp.broadcast_to(doc_row[...], (256, 256))
    down = jnp.sum(jnp.where(rows_of == columns_of, along, 0), axis=1, keepdims=True)
    before = jnp.sum(jnp.where(along < down, 1, 0), axis=1, keepdims=True)
    mask[...] = jnp.where((along == down) & (columns_of <= rows_of), 1.0, 0.0)
    position = (lax.broadcasted_iota(jnp.int32, (256, 1), 0) - before).astype(f32)
    lanes = lax.broadcasted_iota(jnp.int32, (1, 128), 1).astype(f32)
    frequency = jnp.exp(lanes * (-2.0 / 256) * jnp.log(f32(rope_base)))
    angle = position * frequency
    cosine[...] = jnp.cos(angle)
    sine[...] = jnp.sin(angle)
    ratios = jnp.float32(0)
    for i in range(8):
        ratios += mixing[i].astype(f32)
    weight = jnp.zeros((256, 1), f32)
    for i in range(4):
        scale = mixing[doc_source[0, i]].astype(f32) * 8.0 / ratios
        weight = jnp.where(down == i, scale, weight)
    stream[0] = tokens[...].astype(f32)
    grad[...] = cotangent[...].astype(f32) * weight
    gain_sum[...] = jnp.zeros_like(gain_sum)
    for copy in adapters:
        copy.wait()

    for stage in range(3):
        for item in items:
            item.arrive(stage)
            if stage < 2:
                item.spread(stage + 1)
    for item in items:
        item.finish()

    def wide_rows(array, i):
        return array[i // 2, i % 2].reshape(256, 640)

    def q_rows(i):
        return w_both[i, :, :, 0].reshape(256, 640)

    def o_rows(i):
        return w_both[i, :, :, 1].reshape(256, 640)

    def kv_rows(i):
        return w_kv[2 * i : 2 * i + 2, :, :, 0, 0].reshape(256, 640)

    def q_all():
        return w_both[:, :, :, 0].reshape(1024, 640)

    def o_all():
        return w_both[:, :, :, 1].reshape(1024, 640)

    def kv_all():
        return w_kv[:, :, :, 0, 0].reshape(512, 640)

    def all_rows(array):
        return array[...].reshape(2048, 640)

    scale = 256 ** (-0.5)

    def rotated(first, second, sign):
        c = cosine[...]
        s = sine[...] * sign
        return first * c - second * s, second * c + first * s

    def to_hbm(name, loop):
        pltpu.make_async_copy(kept[name], kept_out[name].at[loop], kept_sem.at[ORDER[name]]).start()

    def drained(name, loop):
        pltpu.make_async_copy(kept[name], kept_out[name].at[loop], kept_sem.at[ORDER[name]]).wait()

    def norm(source, gain, target):
        @pl.loop(0, 4)
        def _(i):
            x = source[block(i, 64), :]
            inverse = lax.rsqrt(jnp.mean(x * x, axis=-1, keepdims=True) + eps)
            target[block(i, 64), :] = (x * inverse * gain).astype(bf16)

    def forward(loop):
        norm(stream.at[loop], gains[0:1, :], kept["n1"])
        kept["u1a"][...] = product(kept["n1"][...], a_in[loop, 0]).astype(bf16)
        kept["u1b"][...] = product(kept["n1"][...], a_in[loop, 1]).astype(bf16)

        k_pre = against(kept["n1"][...], kv_rows(0)) + product(kept["u1b"][...], a_qkv[loop, :, 1024:1280])
        first, second = rotated(k_pre[:, :128], k_pre[:, 128:], 1.0)
        k_rot[loop, :, :128] = first.astype(bf16)
        k_rot[loop, :, 128:] = second.astype(bf16)
        value[loop] = (
            against(kept["n1"][...], kv_rows(1)) + product(kept["u1b"][...], a_qkv[loop, :, 1280:1536])
        ).astype(bf16)

        @pl.loop(0, 4)
        def _(h):
            q_pre = against(kept["n1"][...], q_rows(h)) + product(kept["u1a"][...], a_qkv[loop, :, block(h)])
            first, second = rotated(q_pre[:, :128], q_pre[:, 128:], 1.0)
            q_rot[loop, h, :, :128] = first.astype(bf16)
            q_rot[loop, h, :, 128:] = second.astype(bf16)
            scores = against(q_rot[loop, h], k_rot[loop]) * scale
            scores = jnp.where(mask[...] > 0.5, scores, masked)
            expo = jnp.exp(scores - jnp.max(scores, axis=-1, keepdims=True))
            p = expo / jnp.sum(expo, axis=-1, keepdims=True)
            probs[loop, h] = p
            kept["o"][:, block(h)] = product(p.astype(bf16), value[loop]).astype(bf16)

        kept["uo"][...] = product(kept["o"][...], a_attn[loop]).astype(bf16)
        hidden[loop] = stream[loop] + (
            product(kept["o"][...], o_all()) + product(kept["uo"][...], a_back[loop, 0])
        )
        norm(hidden.at[loop], gains[1:2, :], kept["n2"])
        kept["u2a"][...] = product(kept["n2"][...], a_in[loop, 2]).astype(bf16)
        kept["u2b"][...] = product(kept["n2"][...], a_in[loop, 3]).astype(bf16)

        @pl.loop(0, 8)
        def _(i):
            g = against(kept["n2"][...], wide_rows(w_gate, i)) + product(
                kept["u2a"][...], a_ffn[loop, 0, :, block(i)]
            )
            u = against(kept["n2"][...], wide_rows(w_up, i)) + product(
                kept["u2b"][...], a_ffn[loop, 1, :, block(i)]
            )
            gate[loop, :, block(i)] = g
            up[loop, :, block(i)] = u
            bend = jnp.tanh(CURVE * (g + CUBE * g * g * g))
            kept["m"][:, block(i)] = (0.5 * g * (1.0 + bend) * u).astype(bf16)

        kept["ud"][...] = product(kept["m"][...], a_down[loop]).astype(bf16)
        stream[loop + 1] = hidden[loop] + (
            product(kept["m"][...], all_rows(w_down)) + product(kept["ud"][...], a_back[loop, 1])
        )

    forward_names = ("n1", "u1a", "u1b", "o", "uo", "n2", "u2a", "u2b", "m", "ud")
    backward_names = tuple(name for name, _ in NAMES if name not in forward_names)

    def norm_back(source, which, out=None):
        gain = gains[which : which + 1, :]

        @pl.loop(0, 4)
        def _(i):
            rows = block(i, 64)
            x = source[rows, :]
            g = normed[rows, :]
            inverse = lax.rsqrt(jnp.mean(x * x, axis=-1, keepdims=True) + eps)
            scaled = g * gain
            step = inverse * (
                scaled - x * inverse * inverse * jnp.mean(scaled * x, axis=-1, keepdims=True)
            )
            grad[rows, :] = grad[rows, :] + step
            gain_sum[which : which + 1, :] += jnp.sum(g * x * inverse, axis=0, keepdims=True)

    def backward(loop):
        kept["gf"][...] = grad[...].astype(bf16)
        kept["gud"][...] = against(kept["gf"][...], a_back[loop, 1]).astype(bf16)

        @pl.loop(0, 8)
        def _(i):
            gm = against(kept["gf"][...], wide_rows(w_down, i)) + against(
                kept["gud"][...], a_down[loop, block(i), :]
            )
            g = gate[loop, :, block(i)]
            u = up[loop, :, block(i)]
            square = g * g
            bend = jnp.tanh(CURVE * (g + CUBE * g * square))
            half = 0.5 * (1.0 + bend)
            slope = half + 0.5 * g * (1.0 - bend * bend) * (CURVE * (1.0 + 3.0 * CUBE * square))
            kept["ggate"][:, block(i)] = (gm * u * slope).astype(bf16)
            kept["gup"][:, block(i)] = (gm * (g * half)).astype(bf16)

        kept["gu2a"][...] = against(kept["ggate"][...], a_ffn[loop, 0]).astype(bf16)
        kept["gu2b"][...] = against(kept["gup"][...], a_ffn[loop, 1]).astype(bf16)
        normed[...] = (
            product(kept["ggate"][...], all_rows(w_gate))
            + product(kept["gup"][...], all_rows(w_up))
            + against(kept["gu2a"][...], a_in[loop, 2])
            + against(kept["gu2b"][...], a_in[loop, 3])
        )
        norm_back(hidden.at[loop], 1)
        kept["ga"][...] = grad[...].astype(bf16)
        kept["guo"][...] = against(kept["ga"][...], a_back[loop, 0]).astype(bf16)

        def head(h, carry):
            grad_key, grad_value = carry
            go = (
                against(kept["ga"][...], o_rows(h)) + against(kept["guo"][...], a_attn[loop, block(h), :])
            ).astype(bf16)
            p = probs[loop, h]
            gp = against(go, value[loop])
            gs = (p * (gp - jnp.sum(p * gp, axis=-1, keepdims=True))).astype(bf16)
            gq = product(gs, k_rot[loop]) * scale
            first, second = rotated(gq[:, :128], gq[:, 128:], -1.0)
            at = pl.multiple_of(h * 256, 256)
            kept["gqp"][:, pl.ds(at, 128)] = first.astype(bf16)
            kept["gqp"][:, pl.ds(at + 128, 128)] = second.astype(bf16)
            grad_key += crossed(gs, q_rot[loop, h])
            grad_value += crossed(p.astype(bf16), go)
            return grad_key, grad_value

        zero = jnp.zeros((256, 256), f32)
        grad_key, grad_value = lax.fori_loop(0, 4, head, (zero, zero))
        grad_key = grad_key * scale
        first, second = rotated(grad_key[:, :128], grad_key[:, 128:], -1.0)
        kept["gkvp"][:, :128] = first.astype(bf16)
        kept["gkvp"][:, 128:256] = second.astype(bf16)
        kept["gkvp"][:, 256:] = grad_value.astype(bf16)
        kept["gu1a"][...] = against(kept["gqp"][...], a_qkv[loop, :, :1024]).astype(bf16)
        kept["gu1b"][...] = against(kept["gkvp"][...], a_qkv[loop, :, 1024:]).astype(bf16)
        normed[...] = (
            product(kept["gqp"][...], q_all())
            + product(kept["gkvp"][...], kv_all())
            + against(kept["gu1a"][...], a_in[loop, 0])
            + against(kept["gu1b"][...], a_in[loop, 1])
        )
        norm_back(stream.at[loop], 0)

    forward(0)
    for name in forward_names:
        to_hbm(name, 0)
    for name in forward_names:
        drained(name, 0)
    forward(1)
    for name in forward_names:
        to_hbm(name, 1)
    block_out[...] = stream[2].astype(bf16)
    backward(1)
    for name in backward_names:
        to_hbm(name, 1)
    for name in backward_names:
        drained(name, 1)
    backward(0)
    for name in backward_names:
        to_hbm(name, 0)
    token_grad[...] = grad[...]
    gain_tile[...] = jnp.zeros_like(gain_tile)
    for i in range(2):
        for t in range(5):
            gain_tile[5 * i + t : 5 * i + t + 1, :] = gain_sum[i : i + 1, 128 * t : 128 * t + 128]
    for name in forward_names:
        drained(name, 1)
    for name in backward_names:
        drained(name, 0)


ORDER = {name: i for i, (name, _) in enumerate(NAMES)}


def block_pass(tokens, cotangent, doc_ids, doc_source, mixing, norm_gains, shards, adapters):
    vmem = pl.BlockSpec(memory_space=pltpu.VMEM)
    smem = pl.BlockSpec(memory_space=pltpu.SMEM)
    anywhere = pl.BlockSpec(memory_space=pl.ANY)
    dma = pltpu.SemaphoreType.DMA
    return pl.pallas_call(
        block_kernel,
        out_shape=[
            jax.ShapeDtypeStruct((256, 640), bf16),
            jax.ShapeDtypeStruct((256, 640), f32),
            jax.ShapeDtypeStruct((16, 128), f32),
        ]
        + [jax.ShapeDtypeStruct((2, 256, width), bf16) for _, width in NAMES],
        in_specs=[vmem, vmem, vmem, smem, smem, vmem] + [anywhere] * 12,
        out_specs=[vmem] * 3 + [anywhere] * len(NAMES),
        scratch_shapes=[pltpu.VMEM((256, width), bf16) for _, width in NAMES]
        + [pltpu.VMEM((4, 2, 4, 2, 2, 16, 640), bf16)] * 5
        + [pltpu.VMEM((64, 640), bf16)]
        + [pltpu.VMEM((2, *shape), bf16) for shape in ADAPTERS]
        + [
            pltpu.VMEM((256, 128), f32),
            pltpu.VMEM((256, 128), f32),
            pltpu.VMEM((256, 256), f32),
            pltpu.VMEM((3, 256, 640), f32),
            pltpu.VMEM((2, 256, 640), f32),
            pltpu.VMEM((2, 4, 256, 256), bf16),
            pltpu.VMEM((2, 256, 256), bf16),
            pltpu.VMEM((2, 256, 256), bf16),
            pltpu.VMEM((2, 4, 256, 256), f32),
            pltpu.VMEM((2, 256, 2048), f32),
            pltpu.VMEM((2, 256, 2048), f32),
            pltpu.VMEM((256, 640), f32),
            pltpu.VMEM((256, 640), f32),
            pltpu.VMEM((2, 640), f32),
            dma((len(NAMES),)),
            dma((2, 6)),
            dma((2,)),
        ]
        + gather_sems(len(WEIGHT_ITEMS)),
        compiler_params=pltpu.CompilerParams(
            collective_id=1, has_side_effects=True, vmem_limit_bytes=60 * 2**20
        ),
        name="block",
    )(tokens, cotangent, doc_ids, doc_source, mixing, norm_gains, *shards, *adapters)


NEEDS = {
    "attn": ("o", "guo"),
    "qkv": ("u1a", "gqp", "u1b", "gkvp"),
    "ffn": ("u2a", "ggate", "u2b", "gup"),
    "in": ("n1", "n2", "gu1a", "gu1b", "gu2a", "gu2b"),
    "down": ("m", "gud"),
    "back": ("uo", "ga", "ud", "gf"),
    "q": (),
    "o": (),
    "gate": (),
    "up": (),
    "wdown": (),
    "kv": (),
}
LOAD_ORDER = tuple(name for step in STEPS for name in NEEDS[step])


def chip_spot(order, x, y, z):
    at = {"x": x, "y": y, "z": z}
    return tuple(at[axis] for axis in order)


def split_spot(q):
    return (q // 16, (q // 4) % 4, q % 4)


def grads_kernel(*refs):
    count = len(NAMES)
    given = {
        (name, loop): refs[i].at[loop] for loop in range(2) for i, (name, _) in enumerate(NAMES)
    }
    gain_ref = refs[count]
    all_ref, share_ref = refs[count + 1 : count + 3]
    rest = refs[count + 3 :]
    held = {
        (name, loop): rest[i].at[loop] for loop in range(2) for i, (name, _) in enumerate(NAMES)
    }
    rest = rest[count:]
    total, from_core, to_core, got_one, got_two, got_three = rest[:6]
    (load_sem, pair_send, pair_recv, one_send, one_recv, two_send, two_recv, three_send, three_recv) = rest[6:15]
    share_send, share_recv, share_local = rest[15:18]
    spread_sems = rest[18:]

    loads = {}
    for i, name in enumerate(LOAD_ORDER):
        for loop in range(2):
            loads[name, loop] = pltpu.make_async_copy(
                given[name, loop], held[name, loop], load_sem.at[i, loop]
            )
            loads[name, loop].start()
    me = place()
    core = me["c"]
    greet(
        chip_peers(me) + [other_core(me), other_core(other_low(me))]
    )

    def put(part, spot, first, slot, tile, zero, one):
        i, j, k = spot
        own = jnp.where(core == 0, zero, one)
        away = jnp.where(core == 0, one, zero)
        total[part, i, j, k, first + tile] = own.astype(bf16)
        to_core[slot, i, j, k, tile] = away.astype(bf16)

    def shared(left, right, columns):
        return crossed(held[left, 0][:, columns], held[right, 0][...]) + crossed(
            held[left, 1][:, columns], held[right, 1][...]
        )

    def wide_rows(name, left, right, slot):
        part, first, _ = CHUNKS[name]

        @pl.loop(0, 8)
        def _(i):
            value = shared(left, right, block(i))
            for y in range(4):
                for low in range(2):
                    row = 64 * y + 32 * low
                    for t in range(5):
                        lanes = slice(128 * t, 128 * t + 128)
                        put(
                            part,
                            chip_spot(ORDERS[part], i // 2, y, (i % 2) * 2 + low),
                            first,
                            slot,
                            t,
                            value[row : row + 16, lanes],
                            value[row + 16 : row + 32, lanes],
                        )

    def narrow_rows(name, left, right, slot):
        part, first, _ = CHUNKS[name]

        @pl.loop(0, 4)
        def _(i):
            value = shared(left, right, block(i))
            for high in range(2):
                for y in range(4):
                    for low in range(2):
                        row = 128 * high + 32 * y + 16 * low
                        for t in range(3):
                            u = min(t + 3, 4)
                            put(
                                part,
                                chip_spot(ORDERS[part], i, y, high * 2 + low),
                                first,
                                slot,
                                t,
                                value[row : row + 16, 128 * t : 128 * t + 128],
                                value[row : row + 16, 128 * u : 128 * u + 128],
                            )

    def kv_rows(slot):
        part, first, _ = CHUNKS["kv"]

        @pl.loop(0, 2)
        def _(i):
            value = shared("gkvp", "n1", block(i))
            for k in range(16):
                for low, tiles in enumerate((((0, 3), (1, 3)), ((2, 4), (2, 4)))):
                    for t, (zero, one) in enumerate(tiles):
                        put(
                            part,
                            chip_spot(ORDERS[part], 2 * i + k // 8, k % 4, (k // 4) % 2 * 2 + low),
                            first,
                            slot,
                            t,
                            value[16 * k : 16 * k + 16, 128 * zero : 128 * zero + 128],
                            value[16 * k : 16 * k + 16, 128 * one : 128 * one + 128],
                        )

    def ffn_tiles(slot):
        part, first, _ = CHUNKS["ffn"]
        for loop in range(2):
            for j, (left, right) in enumerate((("u2a", "ggate"), ("u2b", "gup"))):

                @pl.loop(0, 8)
                def _(b, loop=loop, j=j, left=left, right=right):
                    value = crossed(held[left, loop][...], held[right, loop][:, block(b)])
                    for h in range(8):
                        for t in range(2):
                            put(
                                part,
                                (b // 2, (b % 2) * 2 + h // 4, h % 4),
                                first,
                                slot,
                                (loop * 2 + j) * 2 + t,
                                value[32 * h : 32 * h + 16, 128 * t : 128 * t + 128],
                                value[32 * h + 16 : 32 * h + 32, 128 * t : 128 * t + 128],
                            )

    def in_tiles(slot):
        part, first, _ = CHUNKS["in"]
        for loop in range(2):
            for j, name in enumerate(("gu1a", "gu1b", "gu2a", "gu2b")):
                value = crossed(
                    held["n1" if j < 2 else "n2", loop][...], held[name, loop][...]
                )
                for r in range(8):
                    for t in range(5):
                        row = 80 * r + 16 * t
                        put(
                            part,
                            split_spot((loop * 4 + j) * 8 + r),
                            first,
                            slot,
                            t,
                            value[row : row + 16, :128],
                            value[row : row + 16, 128:],
                        )

    def qkv_tiles(slot):
        part, first, _ = CHUNKS["qkv"]
        for loop in range(2):
            for k in range(3):
                if k < 2:
                    right = held["gqp", loop][:, 512 * k : 512 * k + 512]
                    value = crossed(held["u1a", loop][...], right)
                else:
                    value = crossed(held["u1b", loop][...], held["gkvp", loop][...])
                for t in range(4):
                    tile = 4 * k + t
                    for h in range(8):
                        put(
                            part,
                            split_spot(loop * 32 + tile // 3 * 8 + h),
                            first,
                            slot,
                            tile % 3,
                            value[32 * h : 32 * h + 16, 128 * t : 128 * t + 128],
                            value[32 * h + 16 : 32 * h + 32, 128 * t : 128 * t + 128],
                        )

    def tall_tiles(name, left, right, slot):
        part, first, _ = CHUNKS[name]
        blocks = 4 if name == "attn" else 8
        for loop in range(2):

            @pl.loop(0, blocks)
            def _(i, loop=loop):
                value = crossed(held[left, loop][:, block(i)], held[right, loop][...])
                for h in range(8):
                    for t in range(2):
                        if name == "attn":
                            spot = (loop * 2 + i // 2, (i % 2) * 2 + h // 4, h % 4)
                            tile = t
                        else:
                            spot = (i // 2, (i % 2) * 2 + h // 4, h % 4)
                            tile = loop * 2 + t
                        put(
                            part,
                            spot,
                            first,
                            slot,
                            tile,
                            value[32 * h : 32 * h + 16, 128 * t : 128 * t + 128],
                            value[32 * h + 16 : 32 * h + 32, 128 * t : 128 * t + 128],
                        )

    def back_tiles(slot):
        part, first, _ = CHUNKS["back"]
        for loop in range(2):
            for b, (left, right) in enumerate((("uo", "ga"), ("ud", "gf"))):
                value = crossed(held[left, loop][...], held[right, loop][...])
                for g in range(16):
                    rows = slice(16 * g, 16 * g + 16)
                    q = (loop * 2 + b) * 16 + g
                    for t in range(3):
                        u = min(t + 3, 4)
                        one = value[rows, 128 * u : 128 * u + 128]
                        if q == 0 and t == 2:
                            one = gain_ref[...]
                        put(
                            part,
                            split_spot(q),
                            first,
                            slot,
                            t,
                            value[rows, 128 * t : 128 * t + 128],
                            one,
                        )

    def work(name, slot):
        if name == "ffn":
            ffn_tiles(slot)
        elif name == "in":
            in_tiles(slot)
        elif name == "qkv":
            qkv_tiles(slot)
        elif name == "attn":
            tall_tiles(name, "o", "guo", slot)
        elif name == "down":
            tall_tiles(name, "m", "gud", slot)
        elif name == "back":
            back_tiles(slot)
        elif name == "gate":
            wide_rows(name, "ggate", "n2", slot)
        elif name == "up":
            wide_rows(name, "gup", "n2", slot)
        elif name == "wdown":
            wide_rows(name, "m", "gf", slot)
        elif name == "q":
            narrow_rows(name, "gqp", "n1", slot)
        elif name == "o":
            narrow_rows(name, "o", "ga", slot)
        else:
            kv_rows(slot)

    sent = []
    pair = {}

    def combine(k):
        part, first, tiles = CHUNKS[STEPS[k]]
        axis = ORDERS[part][0]
        pair[k].wait_recv()

        @pl.loop(0, 16)
        def _(i):
            for j in range(4):
                at = (part, i // 4, i % 4, j, pl.ds(first, tiles))
                total[at] = (total[at].astype(f32) + from_core[at].astype(f32)).astype(bf16)

        for by in (2, 1, 3):
            copy = sending(
                total.at[part, (me[axis] + by) % 4, :, :, pl.ds(first, tiles)],
                got_one.at[part, 3 - by, :, :, pl.ds(first, tiles)],
                one_send.at[k, by - 1],
                one_recv.at[k, 3 - by],
                moved(me, axis, by),
            )
            copy.start()
            sent.append(copy)

    for k, name in enumerate(STEPS):
        part, first, tiles = CHUNKS[name]
        slot = k % 2
        for need in NEEDS[name]:
            loads[need, 0].wait()
            loads[need, 1].wait()
        if k >= 2:
            pair[k - 2].wait_send()
        work(name, slot)
        pair[k] = sending(
            to_core.at[slot, :, :, :, pl.ds(0, tiles)],
            from_core.at[part, :, :, :, pl.ds(first, tiles)],
            pair_send.at[k],
            pair_recv.at[k],
            other_core(me),
        )
        pair[k].start()
        if k >= 1:
            combine(k - 1)
    combine(len(STEPS) - 1)
    pair[len(STEPS) - 2].wait_send()
    pair[len(STEPS) - 1].wait_send()

    def second(g):
        part, first, tiles = GROUPS[g]
        one, two, _ = ORDERS[part]
        for k in IN_GROUP[g]:
            _, start, length = CHUNKS[STEPS[k]]
            for by in (1, 3, 2):
                there = got_one.at[part, by - 1, :, :, pl.ds(start, length)]
                sending(
                    there, there, one_send.at[k, by - 1], one_recv.at[k, by - 1], moved(me, one, by)
                ).wait_recv()

        @pl.loop(0, 16)
        def _(i):
            at = (part, me[one], i // 4, i % 4, pl.ds(first, tiles))
            value = total[at].astype(f32)
            for s in range(3):
                value += got_one[part, s, i // 4, i % 4, pl.ds(first, tiles)].astype(f32)
            total[at] = value.astype(bf16)

        for by in (2, 1, 3):
            copy = sending(
                total.at[part, me[one], (me[two] + by) % 4, :, pl.ds(first, tiles)],
                got_two.at[part, 3 - by, :, pl.ds(first, tiles)],
                two_send.at[g, by - 1],
                two_recv.at[g, 3 - by],
                moved(me, two, by),
            )
            copy.start()
            sent.append(copy)

    def third(g):
        part, first, tiles = GROUPS[g]
        one, two, three = ORDERS[part]
        for by in (1, 3, 2):
            there = got_two.at[part, by - 1, :, pl.ds(first, tiles)]
            sending(
                there, there, two_send.at[g, by - 1], two_recv.at[g, by - 1], moved(me, two, by)
            ).wait_recv()

        @pl.loop(0, 4)
        def _(i):
            at = (part, me[one], me[two], i, pl.ds(first, tiles))
            value = total[at].astype(f32)
            for s in range(3):
                value += got_two[part, s, i, pl.ds(first, tiles)].astype(f32)
            total[at] = value.astype(bf16)

        for by in (2, 1, 3):
            copy = sending(
                total.at[part, me[one], me[two], (me[three] + by) % 4, pl.ds(first, tiles)],
                got_three.at[part, 3 - by, pl.ds(first, tiles)],
                three_send.at[g, by - 1],
                three_recv.at[g, 3 - by],
                moved(me, three, by),
            )
            copy.start()
            sent.append(copy)

    def last(g):
        part, first, tiles = GROUPS[g]
        one, two, three = ORDERS[part]
        for by in (1, 3, 2):
            there = got_three.at[part, by - 1, pl.ds(first, tiles)]
            sending(
                there, there, three_send.at[g, by - 1], three_recv.at[g, by - 1], moved(me, three, by)
            ).wait_recv()
        at = (part, me[one], me[two], me[three], pl.ds(first, tiles))
        value = total[at].astype(f32)
        for s in range(3):
            value += got_three[part, s, pl.ds(first, tiles)].astype(f32)
        total[at] = value.astype(bf16)
        return total.at[at]

    gathers = []

    def start_gather(g):
        part, first, tiles = GROUPS[g]
        order = ORDERS[part]

        def region(fixed, core):
            spot = tuple(fixed.get(axis, slice(None)) for axis in order)
            return all_ref.at[(core, part, *spot, pl.ds(first, tiles))]

        gathers.append(Gather(me, part, order[::-1], last(g), region, spread_sems))
        gathers[-1].start()

    shares = []

    def share(g):
        part, first, tiles = GROUPS[g]
        mine = last(g)
        low = me["z"] % 2

        def spot(low, core):
            return share_ref.at[low * 2 + core, part, pl.ds(0, tiles)]

        local = pltpu.make_async_copy(mine, spot(low, core), share_local.at[part])
        local.start()
        shares.append(local.wait)
        for k, peer in enumerate(
            (other_low(me), other_core(me), other_core(other_low(me)))
        ):
            copy = sending(
                mine, spot(low, core), share_send.at[part, k], share_recv.at[part, k], peer
            )
            copy.start()
            sent.append(copy)
            there = spot(peer["z"] % 2, peer["c"])
            shares.append(
                sending(there, there, share_send.at[part, k], share_recv.at[part, k], peer).wait_recv
            )

    for g in range(3):
        second(g)
    for g in range(3):
        third(g)
    for g in range(3):
        start_gather(g)
    for g in range(3, 6):
        second(g)
    for item in gathers:
        item.arrive(0)
        item.spread(1)
    for g in range(3, 6):
        third(g)
    for item in gathers:
        item.arrive(1)
        item.spread(2)
    for g in range(3, 6):
        share(g)
    for item in gathers:
        item.arrive(2)
    for item in gathers:
        item.finish()
    for wait in shares:
        wait()
    for copy in sent:
        copy.wait_send()


def summed_gradients(kept, gain_tile):
    anywhere = pl.BlockSpec(memory_space=pl.ANY)
    dma = pltpu.SemaphoreType.DMA
    return pl.pallas_call(
        grads_kernel,
        out_shape=[
            jax.ShapeDtypeStruct((2, 3, 4, 4, 4, 9, 16, 128), bf16),
            jax.ShapeDtypeStruct((4, 3, 8, 16, 128), bf16),
        ],
        in_specs=[anywhere] * len(NAMES) + [pl.BlockSpec(memory_space=pltpu.VMEM)],
        out_specs=[anywhere] * 2,
        scratch_shapes=[
            pltpu.VMEM((2, 256, width), bf16) for _, width in NAMES
        ]
        + [
            pltpu.VMEM((3, 4, 4, 4, 16, 16, 128), bf16),
            pltpu.VMEM((3, 4, 4, 4, 16, 16, 128), bf16),
            pltpu.VMEM((2, 4, 4, 4, 8, 16, 128), bf16),
            pltpu.VMEM((3, 3, 4, 4, 16, 16, 128), bf16),
            pltpu.VMEM((3, 3, 4, 16, 16, 128), bf16),
            pltpu.VMEM((3, 3, 16, 16, 128), bf16),
            dma((len(NAMES), 2)),
            dma((len(STEPS),)),
            dma((len(STEPS),)),
            dma((len(STEPS), 3)),
            dma((len(STEPS), 3)),
            dma((6, 3)),
            dma((6, 3)),
            dma((6, 3)),
            dma((6, 3)),
            dma((3, 3)),
            dma((3, 3)),
            dma((3,)),
        ]
        + gather_sems(3),
        compiler_params=pltpu.CompilerParams(
            collective_id=2, has_side_effects=True, vmem_limit_bytes=60 * 2**20
        ),
        name="grads",
    )(*kept, gain_tile)


def unpack_kernel(all_ref, share_ref, *outs):
    (gain, wq, wkv, wo, wgate, wup, wdown, w_in, w_qkv, w_ffn, w_attn, w_down, w_back) = outs

    def tile(core, part, q, t):
        return all_ref[core, part, q, t].astype(f32)

    for q in range(8):
        for core in range(2):
            for t in range(5):
                w_in[0, 0, 80 * q + 16 * t : 80 * q + 16 * t + 16, 128 * core : 128 * core + 128] = tile(core, 1, q, t)
            for t in range(3):
                w_qkv[0, 32 * q + 16 * core : 32 * q + 16 * core + 16, 128 * t : 128 * t + 128] = tile(core, 1, q, 5 + t)
            row = slice(32 * q + 16 * core, 32 * q + 16 * core + 16)
            for k in range(4):
                for t in range(2):
                    w_ffn[k // 2, k % 2, row, 128 * t : 128 * t + 128] = tile(core, 0, q, 2 * k + t)
            for t in range(2):
                lanes = slice(128 * t, 128 * t + 128)
                w_attn[0, row, lanes] = tile(core, 2, q, t)
                for loop in range(2):
                    w_down[loop, row, lanes] = tile(core, 2, q, 2 + loop * 2 + t)
            for t in range(3 - core):
                u = 3 * core + t
                w_back[0, 0, 16 * q : 16 * q + 16, 128 * u : 128 * u + 128] = tile(core, 2, q, 6 + t)

    @pl.when(pl.program_id(0) == 0)
    def _():
        gain[...] = tile(1, 2, 0, 8)

        def mine(low, core, part, t):
            return share_ref[low * 2 + core, part, t].astype(f32)

        def wide(part, first):
            rows = []
            for low in range(2):
                for core in range(2):
                    rows.append(jnp.concatenate([mine(low, core, part, first + t) for t in range(5)], axis=1))
            return jnp.concatenate(rows, axis=0)

        def narrow(part, first):
            rows = []
            for low in range(2):
                tiles = [mine(low, 0, part, first + t) for t in range(3)]
                tiles += [mine(low, 1, part, first + t) for t in range(2)]
                rows.append(jnp.concatenate(tiles, axis=1))
            return jnp.concatenate(rows, axis=0)

        wgate[...] = wide(0, 0)
        wup[...] = wide(1, 0)
        wdown[...] = wide(2, 0)
        wq[...] = narrow(0, 5)
        wo[...] = narrow(1, 5)
        kv = [mine(0, 0, 2, 5), mine(0, 0, 2, 6), mine(1, 0, 2, 5), mine(0, 1, 2, 5), mine(1, 1, 2, 5)]
        wkv[...] = jnp.concatenate(kv, axis=1)


def unpacked(everything, shares):
    def whole(*shape):
        return jax.ShapeDtypeStruct(shape, f32), pl.BlockSpec(shape, lambda i: (0,) * len(shape))

    def cut(shape, block, index):
        return jax.ShapeDtypeStruct(shape, f32), pl.BlockSpec(block, index)

    outs = [
        whole(16, 128),
        whole(32, 640),
        whole(16, 640),
        whole(32, 640),
        whole(64, 640),
        whole(64, 640),
        whole(64, 640),
        cut((2, 4, 640, 256), (1, 1, 640, 256), lambda i: (i // 4, i % 4, 0, 0)),
        cut((2, 256, 1536), (1, 256, 384), lambda i: (i // 4, 0, i % 4)),
        cut((2, 2, 256, 2048), (2, 2, 256, 256), lambda i: (0, 0, 0, i)),
        cut((2, 1024, 256), (1, 256, 256), lambda i: (i // 4, i % 4, 0)),
        cut((2, 2048, 256), (2, 256, 256), lambda i: (0, i, 0)),
        cut((2, 2, 256, 640), (1, 1, 128, 640), lambda i: (i // 4, (i // 2) % 2, i % 2, 0)),
    ]
    return pl.pallas_call(
        unpack_kernel,
        grid=(8,),
        out_shape=[shape for shape, _ in outs],
        in_specs=[
            pl.BlockSpec((2, 3, 8, 9, 16, 128), lambda i: (0, 0, i, 0, 0, 0)),
            pl.BlockSpec((4, 3, 8, 16, 128), lambda i: (0, 0, 0, 0, 0)),
        ],
        out_specs=[spec for _, spec in outs],
        compiler_params=pltpu.CompilerParams(vmem_limit_bytes=40 * 2**20),
        name="unpack",
    )(everything.reshape(2, 3, 64, 9, 16, 128), shares)


def body(
    tokens,
    cotangent,
    doc_ids,
    doc_source,
    mixing,
    norm_gains,
    wq,
    wkv,
    wo,
    wgate,
    wup,
    wdown,
    *adapters,
):
    shards = (wq.T, wkv.T, wo, wgate.T, wup.T, wdown)
    block_out, token_grad, gain_tile, *kept = block_pass(
        tokens, cotangent, doc_ids, doc_source, mixing, norm_gains, shards, adapters
    )
    everything, shares = summed_gradients(kept, gain_tile)
    gain, wq_sum, wkv_sum, wo_sum, wgate_sum, wup_sum, wdown_sum, *sums = unpacked(everything, shares)
    return (
        block_out,
        token_grad,
        gain[:10].reshape(2, 640),
        wq_sum.T,
        wkv_sum.T,
        wo_sum,
        wgate_sum.T,
        wup_sum.T,
        wdown_sum,
        *sums,
    )


def solution(mesh):
    rows = P(("loop", "dp"), None)
    columns = P(None, "dp")
    placed = (
        *(rows,) * 4,
        P(),
        P(),
        columns,
        columns,
        P("dp", None),
        columns,
        columns,
        P("dp", None),
        *(P(),) * 6,
    )
    return jax.shard_map(
        body,
        mesh=mesh,
        in_specs=placed,
        out_specs=(
            rows,
            rows,
            P(),
            columns,
            columns,
            P("dp", None),
            columns,
            columns,
            P("dp", None),
            *(P(),) * 6,
        ),
        check_vma=False,
    )
```

```python
import jax
import jax.numpy as jnp
from jax import lax
from jax.experimental import pallas as pl
from jax.experimental.pallas import tpu as pltpu
from jax.sharding import PartitionSpec as P

eps = 1e-06
rope_base = 10000.0
masked = -1e30
MESH = pl.DeviceIdType.MESH
bf16 = jnp.bfloat16
f32 = jnp.float32

ORDERS = (("x", "y", "z"), ("y", "z", "x"), ("z", "x", "y"))

CHUNKS = {
    "ffn": (0, 0, 8),
    "gate": (0, 8, 5),
    "q": (0, 13, 3),
    "in": (1, 0, 5),
    "qkv": (1, 5, 3),
    "up": (1, 8, 5),
    "o": (1, 13, 3),
    "attn": (2, 0, 2),
    "down": (2, 2, 4),
    "back": (2, 6, 3),
    "wdown": (2, 9, 5),
    "kv": (2, 14, 2),
}
STEPS = ("attn", "qkv", "ffn", "in", "down", "back", "q", "o", "wdown", "gate", "up", "kv")
GROUPS = ((0, 0, 8), (1, 0, 8), (2, 0, 9), (0, 8, 8), (1, 8, 8), (2, 9, 7))
IN_GROUP = tuple(
    tuple(
        k
        for k, name in enumerate(STEPS)
        if CHUNKS[name][0] == part and first <= CHUNKS[name][1] < first + count
    )
    for part, first, count in GROUPS
)


HALVES = (slice(0, 2), slice(2, 4))


def place():
    lo = lax.axis_index("loop")
    dp = lax.axis_index("dp")
    return {"x": dp // 8, "y": dp % 4, "z": (dp // 4) % 2 * 2 + lo // 2, "c": lo % 2}


def device(at):
    return ((at["z"] % 2) * 2 + at["c"], at["x"] * 8 + (at["z"] // 2) * 4 + at["y"])


def moved(me, axis, by):
    return {**me, axis: (me[axis] + by) % 4}


def other_core(me):
    return {**me, "c": 1 - me["c"]}


def other_low(me):
    return {**me, "z": me["z"] + 1 - 2 * (me["z"] % 2)}


def greet(peers):
    barrier = pltpu.get_barrier_semaphore()
    for peer in peers:
        pl.semaphore_signal(barrier, inc=1, device_id=device(peer), device_id_type=MESH)
    pl.semaphore_wait(barrier, len(peers))


def sending(src, dst, send, recv, peer):
    return pltpu.make_async_remote_copy(
        src_ref=src,
        dst_ref=dst,
        send_sem=send,
        recv_sem=recv,
        device_id=device(peer),
        device_id_type=MESH,
    )


class Gather:
    def __init__(self, me, index, order, piece, region, sems):
        self.me, self.index, self.order, self.piece, self.region = me, index, order, piece, region
        self.send, self.recv, self.core_send, self.core_recv, self.local = sems
        self.sent = []
        self.due = []

    def spot(self, stage, by):
        fixed = {axis: self.me[axis] for axis in self.order[stage:]}
        fixed[self.order[stage]] = (self.me[self.order[stage]] + by) % 4
        return fixed

    def to_core(self, source, fixed, k):
        i, me = self.index, self.me
        copy = sending(
            source,
            self.region(fixed, me["c"]),
            self.core_send.at[i, k],
            self.core_recv.at[i, k],
            other_core(me),
        )
        copy.start()
        self.sent.append(copy)
        there = self.region(fixed, 1 - me["c"])
        self.due.append(
            sending(there, there, self.core_send.at[i, k], self.core_recv.at[i, k], other_core(me))
        )

    def half(self, by, which):
        return {**self.spot(2, by), self.order[0]: HALVES[which]}

    def pass_on(self, by, which, step, slot):
        here = self.region(self.half(by, which), self.me["c"])
        copy = sending(
            here,
            here,
            self.send.at[self.index, 2, slot],
            self.recv.at[self.index, 2, slot],
            moved(self.me, self.order[2], step),
        )
        copy.start()
        self.sent.append(copy)

    def take(self, by, which, slot):
        fixed = self.half(by, which)
        there = self.region(fixed, self.me["c"])
        sending(
            there,
            there,
            self.send.at[self.index, 2, slot],
            self.recv.at[self.index, 2, slot],
            moved(self.me, self.order[2], by),
        ).wait_recv()
        return there, fixed

    def begin_ring(self):
        self.pass_on(0, 0, 1, 0)
        self.pass_on(0, 1, 3, 3)
        self.pass_on(0, 1, 1, 1)
        self.pass_on(0, 0, 3, 2)

    def turn_ring(self):
        left = self.take(3, 0, 0)
        self.pass_on(3, 0, 1, 4)
        right = self.take(1, 1, 3)
        self.pass_on(1, 1, 3, 5)
        self.to_core(*left, 7)
        self.to_core(*right, 8)

    def end_ring(self):
        self.to_core(*self.take(3, 1, 1), 9)
        self.to_core(*self.take(1, 0, 2), 10)
        self.to_core(*self.take(2, 0, 4), 11)
        self.to_core(*self.take(2, 1, 5), 12)

    def start(self):
        fixed = self.spot(0, 0)
        self.kept = pltpu.make_async_copy(
            self.piece, self.region(fixed, self.me["c"]), self.local.at[self.index]
        )
        self.kept.start()
        self.spread(0, self.piece)
        self.to_core(self.piece, fixed, 0)

    def spread(self, stage, source=None):
        if stage == 1:
            self.kept.wait()
        here = self.region(self.spot(stage, 0), self.me["c"])
        for by in (2, 1, 3):
            copy = sending(
                here if source is None else source,
                here,
                self.send.at[self.index, stage, by - 1],
                self.recv.at[self.index, stage, 3 - by],
                moved(self.me, self.order[stage], by),
            )
            copy.start()
            self.sent.append(copy)

    def arrive(self, stage):
        for by in (1, 3, 2):
            fixed = self.spot(stage, by)
            there = self.region(fixed, self.me["c"])
            sending(
                there,
                there,
                self.send.at[self.index, stage, by - 1],
                self.recv.at[self.index, stage, by - 1],
                moved(self.me, self.order[stage], by),
            ).wait_recv()
            self.to_core(there, fixed, 1 + 3 * stage + by - 1)

    def finish(self):
        for copy in self.due:
            copy.wait_recv()
        for copy in self.sent:
            copy.wait_send()


def gather_sems(items):
    return [
        pltpu.SemaphoreType.DMA((items, 3, 6)),
        pltpu.SemaphoreType.DMA((items, 3, 6)),
        pltpu.SemaphoreType.DMA((items, 13)),
        pltpu.SemaphoreType.DMA((items, 13)),
        pltpu.SemaphoreType.DMA((items,)),
    ]


def chip_peers(me):
    return [moved(me, axis, by) for axis in ("x", "y", "z") for by in (1, 2, 3)]


WEIGHT_ITEMS = (
    (1, 3, 0, 384),
    (2, 3, 384, 640),
    (0, 4, 0, 384),
    (2, 4, 384, 640),
    (0, 0, 0, 640),
    (1, 1, 0, 640),
    (2, 2, 0, 640),
)

NAMES = (
    ("m", 2048),
    ("gf", 640),
    ("gud", 256),
    ("ud", 256),
    ("n2", 640),
    ("ggate", 2048),
    ("gup", 2048),
    ("gu2a", 256),
    ("gu2b", 256),
    ("u2a", 256),
    ("u2b", 256),
    ("o", 1024),
    ("ga", 640),
    ("guo", 256),
    ("uo", 256),
    ("n1", 640),
    ("gqp", 1024),
    ("gkvp", 512),
    ("gu1a", 256),
    ("gu1b", 256),
    ("u1a", 256),
    ("u1b", 256),
)
ADAPTERS = ((4, 640, 256), (256, 1536), (2, 256, 2048), (1024, 256), (2048, 256), (2, 256, 640))


def product(left, right):
    return lax.dot_general(left, right, (((1,), (0,)), ((), ())), preferred_element_type=f32)


def against(left, right):
    return lax.dot_general(left, right, (((1,), (1,)), ((), ())), preferred_element_type=f32)


def crossed(left, right):
    return lax.dot_general(left, right, (((0,), (0,)), ((), ())), preferred_element_type=f32)


def block(i, width=256):
    return pl.ds(pl.multiple_of(i * width, width), width)


CURVE = 0.7978845608028654
CUBE = 0.044715


def block_kernel(*refs):
    (tokens, cotangent, doc_row, doc_source, mixing, gains) = refs[:6]
    shards = refs[6:12]
    adapters_in = refs[12:18]
    outs = refs[18:]
    block_out, token_grad, gain_tile = outs[:3]
    kept_out = dict(zip((name for name, _ in NAMES), outs[3 : 3 + len(NAMES)]))
    rest = outs[3 + len(NAMES) :]
    kept = dict(zip((name for name, _ in NAMES), rest[: len(NAMES)]))
    rest = rest[len(NAMES) :]
    whole = rest[:5]
    both_piece = rest[5]
    a_in, a_qkv, a_ffn, a_attn, a_down, a_back = rest[6:12]
    (cosine, sine, mask, stream, hidden, q_rot, k_rot, value, probs, gate, up, grad, normed, gain_sum) = rest[12:26]
    kept_sem, adapter_sem, piece_sem = rest[26:29]
    gather = rest[29:]

    me = place()
    quarter = (me["z"] % 2) * 2 + me["c"]
    w_gate, w_up, w_down, w_both, w_kv = whole

    fetch = [
        pltpu.make_async_copy(shards[0], both_piece.at[:32], piece_sem.at[0]),
        pltpu.make_async_copy(shards[2], both_piece.at[32:], piece_sem.at[1]),
    ]
    for copy in fetch:
        copy.start()
    adapters = []
    for loop in range(2):
        for i, (source, target) in enumerate(
            zip(adapters_in, (a_in, a_qkv, a_ffn, a_attn, a_down, a_back))
        ):
            copy = pltpu.make_async_copy(source.at[loop], target.at[loop], adapter_sem.at[loop, i])
            copy.start()
            adapters.append(copy)
    greet(chip_peers(me) + [other_core(me)])
    for copy in fetch:
        copy.wait()
    own = pl.ds(pl.multiple_of(quarter * 16, 16), 16)
    sources = (shards[3].at[own], shards[4].at[own], shards[5].at[own], both_piece.at[own], shards[1])
    items = []
    for i, (part, array, low, high) in enumerate(WEIGHT_ITEMS):

        def region(fixed, core, array=array, low=low, high=high):
            every = slice(None)
            zh, zl = every, every
            if isinstance(fixed.get("z"), slice):
                zh = fixed["z"].start // 2
            elif "z" in fixed:
                zh, zl = fixed["z"] // 2, fixed["z"] % 2
            return whole[array].at[
                fixed.get("x", every), zh, fixed.get("y", every), zl, core, :, pl.ds(low, high - low)
            ]

        items.append(
            Gather(me, i, ORDERS[part][::-1], sources[array].at[:, pl.ds(low, high - low)], region, gather)
        )
    for item in items:
        item.start()

    rows_of = lax.broadcasted_iota(jnp.int32, (256, 256), 0)
    columns_of = lax.broadcasted_iota(jnp.int32, (256, 256), 1)
    along = jnp.broadcast_to(doc_row[...], (256, 256))
    down = jnp.sum(jnp.where(rows_of == columns_of, along, 0), axis=1, keepdims=True)
    before = jnp.sum(jnp.where(along < down, 1, 0), axis=1, keepdims=True)
    mask[...] = jnp.where((along == down) & (columns_of <= rows_of), 1.0, 0.0)
    position = (lax.broadcasted_iota(jnp.int32, (256, 1), 0) - before).astype(f32)
    lanes = lax.broadcasted_iota(jnp.int32, (1, 128), 1).astype(f32)
    frequency = jnp.exp(lanes * (-2.0 / 256) * jnp.log(f32(rope_base)))
    angle = position * frequency
    cosine[...] = jnp.cos(angle)
    sine[...] = jnp.sin(angle)
    ratios = jnp.float32(0)
    for i in range(8):
        ratios += mixing[i].astype(f32)
    weight = jnp.zeros((256, 1), f32)
    for i in range(4):
        scale = mixing[doc_source[0, i]].astype(f32) * 8.0 / ratios
        weight = jnp.where(down == i, scale, weight)
    stream[0] = tokens[...].astype(f32)
    grad[...] = cotangent[...].astype(f32) * weight
    gain_sum[...] = jnp.zeros_like(gain_sum)
    for copy in adapters:
        copy.wait()

    for item in items:
        item.arrive(0)
        item.spread(1)
    for item in items:
        item.arrive(1)
        item.begin_ring()
    for item in items:
        item.turn_ring()
    for item in items:
        item.end_ring()
    for item in items:
        item.finish()

    def wide_rows(array, i):
        return array[i].reshape(512, 640)

    def q_rows(i):
        return w_both[i, :, :, 0].reshape(256, 640)

    def o_rows(i):
        return w_both[i, :, :, 1].reshape(256, 640)

    def kv_rows(i):
        return w_kv[2 * i : 2 * i + 2, :, :, 0, 0].reshape(256, 640)

    def q_all():
        return w_both[:, :, :, 0].reshape(1024, 640)

    def o_all():
        return w_both[:, :, :, 1].reshape(1024, 640)

    def kv_all():
        return w_kv[:, :, :, 0, 0].reshape(512, 640)

    def all_rows(array):
        return array[...].reshape(2048, 640)

    scale = 256 ** (-0.5)

    def rotated(first, second, sign):
        c = cosine[...]
        s = sine[...] * sign
        return first * c - second * s, second * c + first * s

    def to_hbm(name, loop):
        pltpu.make_async_copy(kept[name], kept_out[name].at[loop], kept_sem.at[ORDER[name]]).start()

    def drained(name, loop):
        pltpu.make_async_copy(kept[name], kept_out[name].at[loop], kept_sem.at[ORDER[name]]).wait()

    def norm(source, gain, target):
        for i in range(4):
            rows = slice(64 * i, 64 * i + 64)
            x = source[rows, :]
            inverse = lax.rsqrt(jnp.mean(x * x, axis=-1, keepdims=True) + eps)
            target[rows, :] = (x * inverse * gain).astype(bf16)

    def forward(loop):
        norm(stream.at[loop], gains[0:1, :], kept["n1"])
        kept["u1a"][...] = product(kept["n1"][...], a_in[loop, 0]).astype(bf16)
        kept["u1b"][...] = product(kept["n1"][...], a_in[loop, 1]).astype(bf16)

        k_pre = against(kept["n1"][...], kv_rows(0)) + product(kept["u1b"][...], a_qkv[loop, :, 1024:1280])
        first, second = rotated(k_pre[:, :128], k_pre[:, 128:], 1.0)
        k_rot[loop, :, :128] = first.astype(bf16)
        k_rot[loop, :, 128:] = second.astype(bf16)
        value[loop] = (
            against(kept["n1"][...], kv_rows(1)) + product(kept["u1b"][...], a_qkv[loop, :, 1280:1536])
        ).astype(bf16)

        for h in range(4):
            at = slice(256 * h, 256 * h + 256)
            q_pre = against(kept["n1"][...], q_rows(h)) + product(kept["u1a"][...], a_qkv[loop, :, at])
            first, second = rotated(q_pre[:, :128], q_pre[:, 128:], 1.0)
            q_rot[loop, h, :, :128] = first.astype(bf16)
            q_rot[loop, h, :, 128:] = second.astype(bf16)
            scores = against(q_rot[loop, h], k_rot[loop]) * scale
            scores = jnp.where(mask[...] > 0.5, scores, masked)
            expo = jnp.exp(scores - jnp.max(scores, axis=-1, keepdims=True))
            p = expo / jnp.sum(expo, axis=-1, keepdims=True)
            probs[loop, h] = p
            kept["o"][:, at] = product(p.astype(bf16), value[loop]).astype(bf16)

        kept["uo"][...] = product(kept["o"][...], a_attn[loop]).astype(bf16)
        hidden[loop] = stream[loop] + (
            product(kept["o"][...], o_all()) + product(kept["uo"][...], a_back[loop, 0])
        )
        norm(hidden.at[loop], gains[1:2, :], kept["n2"])
        kept["u2a"][...] = product(kept["n2"][...], a_in[loop, 2]).astype(bf16)
        kept["u2b"][...] = product(kept["n2"][...], a_in[loop, 3]).astype(bf16)

        for i in range(4):
            at = slice(512 * i, 512 * i + 512)
            g = against(kept["n2"][...], wide_rows(w_gate, i)) + product(
                kept["u2a"][...], a_ffn[loop, 0, :, at]
            )
            u = against(kept["n2"][...], wide_rows(w_up, i)) + product(
                kept["u2b"][...], a_ffn[loop, 1, :, at]
            )
            gate[loop, :, at] = g
            up[loop, :, at] = u
            bend = jnp.tanh(CURVE * (g + CUBE * g * g * g))
            kept["m"][:, at] = (0.5 * g * (1.0 + bend) * u).astype(bf16)

        kept["ud"][...] = product(kept["m"][...], a_down[loop]).astype(bf16)
        stream[loop + 1] = hidden[loop] + (
            product(kept["m"][...], all_rows(w_down)) + product(kept["ud"][...], a_back[loop, 1])
        )

    forward_names = ("n1", "u1a", "u1b", "o", "uo", "n2", "u2a", "u2b", "m", "ud")
    backward_names = tuple(name for name, _ in NAMES if name not in forward_names)

    def norm_back(source, which, out=None):
        gain = gains[which : which + 1, :]

        for i in range(4):
            rows = slice(64 * i, 64 * i + 64)
            x = source[rows, :]
            g = normed[rows, :]
            inverse = lax.rsqrt(jnp.mean(x * x, axis=-1, keepdims=True) + eps)
            scaled = g * gain
            step = inverse * (
                scaled - x * inverse * inverse * jnp.mean(scaled * x, axis=-1, keepdims=True)
            )
            grad[rows, :] = grad[rows, :] + step
            gain_sum[which : which + 1, :] += jnp.sum(g * x * inverse, axis=0, keepdims=True)

    def backward(loop):
        kept["gf"][...] = grad[...].astype(bf16)
        kept["gud"][...] = against(kept["gf"][...], a_back[loop, 1]).astype(bf16)

        for i in range(4):
            at = slice(512 * i, 512 * i + 512)
            gm = against(kept["gf"][...], wide_rows(w_down, i)) + against(
                kept["gud"][...], a_down[loop, at, :]
            )
            g = gate[loop, :, at]
            u = up[loop, :, at]
            square = g * g
            bend = jnp.tanh(CURVE * (g + CUBE * g * square))
            half = 0.5 * (1.0 + bend)
            slope = half + 0.5 * g * (1.0 - bend * bend) * (CURVE * (1.0 + 3.0 * CUBE * square))
            kept["ggate"][:, at] = (gm * u * slope).astype(bf16)
            kept["gup"][:, at] = (gm * (g * half)).astype(bf16)

        kept["gu2a"][...] = against(kept["ggate"][...], a_ffn[loop, 0]).astype(bf16)
        kept["gu2b"][...] = against(kept["gup"][...], a_ffn[loop, 1]).astype(bf16)
        normed[...] = (
            product(kept["ggate"][...], all_rows(w_gate))
            + product(kept["gup"][...], all_rows(w_up))
            + against(kept["gu2a"][...], a_in[loop, 2])
            + against(kept["gu2b"][...], a_in[loop, 3])
        )
        norm_back(hidden.at[loop], 1)
        kept["ga"][...] = grad[...].astype(bf16)
        kept["guo"][...] = against(kept["ga"][...], a_back[loop, 0]).astype(bf16)

        def head(h, carry):
            grad_key, grad_value = carry
            at = slice(256 * h, 256 * h + 256)
            go = (
                against(kept["ga"][...], o_rows(h)) + against(kept["guo"][...], a_attn[loop, at, :])
            ).astype(bf16)
            p = probs[loop, h]
            gp = against(go, value[loop])
            gs = (p * (gp - jnp.sum(p * gp, axis=-1, keepdims=True))).astype(bf16)
            gq = product(gs, k_rot[loop]) * scale
            first, second = rotated(gq[:, :128], gq[:, 128:], -1.0)
            kept["gqp"][:, 256 * h : 256 * h + 128] = first.astype(bf16)
            kept["gqp"][:, 256 * h + 128 : 256 * h + 256] = second.astype(bf16)
            grad_key += crossed(gs, q_rot[loop, h])
            grad_value += crossed(p.astype(bf16), go)
            return grad_key, grad_value

        sums = (jnp.zeros((256, 256), f32), jnp.zeros((256, 256), f32))
        for h in range(4):
            sums = head(h, sums)
        grad_key, grad_value = sums
        grad_key = grad_key * scale
        first, second = rotated(grad_key[:, :128], grad_key[:, 128:], -1.0)
        kept["gkvp"][:, :128] = first.astype(bf16)
        kept["gkvp"][:, 128:256] = second.astype(bf16)
        kept["gkvp"][:, 256:] = grad_value.astype(bf16)
        kept["gu1a"][...] = against(kept["gqp"][...], a_qkv[loop, :, :1024]).astype(bf16)
        kept["gu1b"][...] = against(kept["gkvp"][...], a_qkv[loop, :, 1024:]).astype(bf16)
        normed[...] = (
            product(kept["gqp"][...], q_all())
            + product(kept["gkvp"][...], kv_all())
            + against(kept["gu1a"][...], a_in[loop, 0])
            + against(kept["gu1b"][...], a_in[loop, 1])
        )
        norm_back(stream.at[loop], 0)

    forward(0)
    for name in forward_names:
        to_hbm(name, 0)
    for name in forward_names:
        drained(name, 0)
    forward(1)
    for name in forward_names:
        to_hbm(name, 1)
    block_out[...] = stream[2].astype(bf16)
    backward(1)
    for name in backward_names:
        to_hbm(name, 1)
    for name in backward_names:
        drained(name, 1)
    backward(0)
    for name in backward_names:
        to_hbm(name, 0)
    token_grad[...] = grad[...]
    gain_tile[...] = jnp.zeros_like(gain_tile)
    for i in range(2):
        for t in range(5):
            gain_tile[5 * i + t : 5 * i + t + 1, :] = gain_sum[i : i + 1, 128 * t : 128 * t + 128]
    for name in forward_names:
        drained(name, 1)
    for name in backward_names:
        drained(name, 0)


ORDER = {name: i for i, (name, _) in enumerate(NAMES)}


def block_pass(tokens, cotangent, doc_ids, doc_source, mixing, norm_gains, shards, adapters):
    vmem = pl.BlockSpec(memory_space=pltpu.VMEM)
    smem = pl.BlockSpec(memory_space=pltpu.SMEM)
    anywhere = pl.BlockSpec(memory_space=pl.ANY)
    dma = pltpu.SemaphoreType.DMA
    return pl.pallas_call(
        block_kernel,
        out_shape=[
            jax.ShapeDtypeStruct((256, 640), bf16),
            jax.ShapeDtypeStruct((256, 640), f32),
            jax.ShapeDtypeStruct((16, 128), f32),
        ]
        + [jax.ShapeDtypeStruct((2, 256, width), bf16) for _, width in NAMES],
        in_specs=[vmem, vmem, vmem, smem, smem, vmem] + [anywhere] * 12,
        out_specs=[vmem] * 3 + [anywhere] * len(NAMES),
        scratch_shapes=[pltpu.VMEM((256, width), bf16) for _, width in NAMES]
        + [pltpu.VMEM((4, 2, 4, 2, 2, 16, 640), bf16)] * 5
        + [pltpu.VMEM((64, 640), bf16)]
        + [pltpu.VMEM((2, *shape), bf16) for shape in ADAPTERS]
        + [
            pltpu.VMEM((256, 128), f32),
            pltpu.VMEM((256, 128), f32),
            pltpu.VMEM((256, 256), f32),
            pltpu.VMEM((3, 256, 640), f32),
            pltpu.VMEM((2, 256, 640), f32),
            pltpu.VMEM((2, 4, 256, 256), bf16),
            pltpu.VMEM((2, 256, 256), bf16),
            pltpu.VMEM((2, 256, 256), bf16),
            pltpu.VMEM((2, 4, 256, 256), f32),
            pltpu.VMEM((2, 256, 2048), f32),
            pltpu.VMEM((2, 256, 2048), f32),
            pltpu.VMEM((256, 640), f32),
            pltpu.VMEM((256, 640), f32),
            pltpu.VMEM((2, 640), f32),
            dma((len(NAMES),)),
            dma((2, 6)),
            dma((2,)),
        ]
        + gather_sems(len(WEIGHT_ITEMS)),
        compiler_params=pltpu.CompilerParams(
            collective_id=1, has_side_effects=True, vmem_limit_bytes=60 * 2**20
        ),
        name="block",
    )(tokens, cotangent, doc_ids, doc_source, mixing, norm_gains, *shards, *adapters)


NEEDS = {
    "attn": ("o", "guo"),
    "qkv": ("u1a", "gqp", "u1b", "gkvp"),
    "ffn": ("u2a", "ggate", "u2b", "gup"),
    "in": ("n1", "n2", "gu1a", "gu1b", "gu2a", "gu2b"),
    "down": ("m", "gud"),
    "back": ("uo", "ga", "ud", "gf"),
    "q": (),
    "o": (),
    "gate": (),
    "up": (),
    "wdown": (),
    "kv": (),
}
LOAD_ORDER = tuple(name for step in STEPS for name in NEEDS[step])


def chip_spot(order, x, y, z):
    at = {"x": x, "y": y, "z": z}
    return tuple(at[axis] for axis in order)


def split_spot(q):
    return (q // 16, (q // 4) % 4, q % 4)


def grads_kernel(*refs):
    count = len(NAMES)
    given = {
        (name, loop): refs[i].at[loop] for loop in range(2) for i, (name, _) in enumerate(NAMES)
    }
    gain_ref = refs[count]
    all_ref, share_ref = refs[count + 1 : count + 3]
    rest = refs[count + 3 :]
    refs_of = {name: rest[i] for i, (name, _) in enumerate(NAMES)}
    held = {
        (name, loop): rest[i].at[loop] for loop in range(2) for i, (name, _) in enumerate(NAMES)
    }
    rest = rest[count:]
    total, from_core, to_core, got_one, got_two, got_three = rest[:6]
    (load_sem, pair_send, pair_recv, one_send, one_recv, two_send, two_recv, three_send, three_recv) = rest[6:15]
    share_send, share_recv, share_local = rest[15:18]
    spread_sems = rest[18:]

    loads = {}
    for i, name in enumerate(LOAD_ORDER):
        for loop in range(2):
            loads[name, loop] = pltpu.make_async_copy(
                given[name, loop], held[name, loop], load_sem.at[i, loop]
            )
            loads[name, loop].start()
    me = place()
    core = me["c"]
    greet(
        chip_peers(me) + [other_core(me), other_core(other_low(me))]
    )

    def put(part, spot, first, slot, tile, zero, one):
        i, j, k = spot
        own = jnp.where(core == 0, zero, one)
        away = jnp.where(core == 0, one, zero)
        total[part, i, j, k, first + tile] = own.astype(bf16)
        to_core[slot, i, j, k, tile] = away.astype(bf16)

    def shared(left, right, columns):
        width = columns.stop - columns.start if isinstance(columns, slice) else columns.size
        return crossed(
            refs_of[left][:, :, columns].reshape(512, width), refs_of[right][...].reshape(512, 640)
        )

    def wide_rows(name, left, right, slot):
        part, first, _ = CHUNKS[name]

        @pl.loop(0, 2)
        def _(i):
            value = shared(left, right, block(i, 1024))
            for x in range(2):
                for high in range(2):
                    for y in range(4):
                        for low in range(2):
                            row = 512 * x + 256 * high + 64 * y + 32 * low
                            for t in range(5):
                                lanes = slice(128 * t, 128 * t + 128)
                                put(
                                    part,
                                    chip_spot(ORDERS[part], 2 * i + x, y, high * 2 + low),
                                    first,
                                    slot,
                                    t,
                                    value[row : row + 16, lanes],
                                    value[row + 16 : row + 32, lanes],
                                )

    def narrow_rows(name, left, right, slot):
        part, first, _ = CHUNKS[name]
        value = shared(left, right, slice(0, 1024))
        for x in range(4):
            for high in range(2):
                for y in range(4):
                    for low in range(2):
                        row = 256 * x + 128 * high + 32 * y + 16 * low
                        for t in range(3):
                            u = min(t + 3, 4)
                            put(
                                part,
                                chip_spot(ORDERS[part], x, y, high * 2 + low),
                                first,
                                slot,
                                t,
                                value[row : row + 16, 128 * t : 128 * t + 128],
                                value[row : row + 16, 128 * u : 128 * u + 128],
                            )

    def kv_rows(slot):
        part, first, _ = CHUNKS["kv"]
        value = shared("gkvp", "n1", slice(0, 512))
        for k in range(32):
            for low, tiles in enumerate((((0, 3), (1, 3)), ((2, 4), (2, 4)))):
                for t, (zero, one) in enumerate(tiles):
                    put(
                        part,
                        chip_spot(ORDERS[part], k // 8, k % 4, (k // 4) % 2 * 2 + low),
                        first,
                        slot,
                        t,
                        value[16 * k : 16 * k + 16, 128 * zero : 128 * zero + 128],
                        value[16 * k : 16 * k + 16, 128 * one : 128 * one + 128],
                    )

    def ffn_tiles(slot):
        part, first, _ = CHUNKS["ffn"]
        for loop in range(2):
            for j, (left, right) in enumerate((("u2a", "ggate"), ("u2b", "gup"))):

                @pl.loop(0, 2)
                def _(i, loop=loop, j=j, left=left, right=right):
                    value = crossed(held[left, loop][...], held[right, loop][:, block(i, 1024)])
                    for b in range(4):
                        for h in range(8):
                            for t in range(2):
                                lanes = slice(256 * b + 128 * t, 256 * b + 128 * t + 128)
                                put(
                                    part,
                                    (2 * i + b // 2, (b % 2) * 2 + h // 4, h % 4),
                                    first,
                                    slot,
                                    (loop * 2 + j) * 2 + t,
                                    value[32 * h : 32 * h + 16, lanes],
                                    value[32 * h + 16 : 32 * h + 32, lanes],
                                )

    def in_tiles(slot):
        part, first, _ = CHUNKS["in"]
        for loop in range(2):
            for j, name in enumerate(("gu1a", "gu1b", "gu2a", "gu2b")):
                value = crossed(
                    held["n1" if j < 2 else "n2", loop][...], held[name, loop][...]
                )
                for r in range(8):
                    for t in range(5):
                        row = 80 * r + 16 * t
                        put(
                            part,
                            split_spot((loop * 4 + j) * 8 + r),
                            first,
                            slot,
                            t,
                            value[row : row + 16, :128],
                            value[row : row + 16, 128:],
                        )

    def qkv_tiles(slot):
        part, first, _ = CHUNKS["qkv"]
        for loop in range(2):
            for k in range(3):
                if k < 2:
                    right = held["gqp", loop][:, 512 * k : 512 * k + 512]
                    value = crossed(held["u1a", loop][...], right)
                else:
                    value = crossed(held["u1b", loop][...], held["gkvp", loop][...])
                for t in range(4):
                    tile = 4 * k + t
                    for h in range(8):
                        put(
                            part,
                            split_spot(loop * 32 + tile // 3 * 8 + h),
                            first,
                            slot,
                            tile % 3,
                            value[32 * h : 32 * h + 16, 128 * t : 128 * t + 128],
                            value[32 * h + 16 : 32 * h + 32, 128 * t : 128 * t + 128],
                        )

    def tall_tiles(name, left, right, slot):
        part, first, _ = CHUNKS[name]
        for loop in range(2):

            @pl.loop(0, 1 if name == "attn" else 2)
            def _(i, loop=loop):
                value = crossed(held[left, loop][:, block(i, 1024)], held[right, loop][...])
                for b in range(4):
                    for h in range(8):
                        for t in range(2):
                            if name == "attn":
                                spot = (loop * 2 + b // 2, (b % 2) * 2 + h // 4, h % 4)
                                tile = t
                            else:
                                spot = (2 * i + b // 2, (b % 2) * 2 + h // 4, h % 4)
                                tile = loop * 2 + t
                            row = 256 * b + 32 * h
                            put(
                                part,
                                spot,
                                first,
                                slot,
                                tile,
                                value[row : row + 16, 128 * t : 128 * t + 128],
                                value[row + 16 : row + 32, 128 * t : 128 * t + 128],
                            )

    def back_tiles(slot):
        part, first, _ = CHUNKS["back"]
        for loop in range(2):
            for b, (left, right) in enumerate((("uo", "ga"), ("ud", "gf"))):
                value = crossed(held[left, loop][...], held[right, loop][...])
                for g in range(16):
                    rows = slice(16 * g, 16 * g + 16)
                    q = (loop * 2 + b) * 16 + g
                    for t in range(3):
                        u = min(t + 3, 4)
                        one = value[rows, 128 * u : 128 * u + 128]
                        if q == 0 and t == 2:
                            one = gain_ref[...]
                        put(
                            part,
                            split_spot(q),
                            first,
                            slot,
                            t,
                            value[rows, 128 * t : 128 * t + 128],
                            one,
                        )

    def work(name, slot):
        if name == "ffn":
            ffn_tiles(slot)
        elif name == "in":
            in_tiles(slot)
        elif name == "qkv":
            qkv_tiles(slot)
        elif name == "attn":
            tall_tiles(name, "o", "guo", slot)
        elif name == "down":
            tall_tiles(name, "m", "gud", slot)
        elif name == "back":
            back_tiles(slot)
        elif name == "gate":
            wide_rows(name, "ggate", "n2", slot)
        elif name == "up":
            wide_rows(name, "gup", "n2", slot)
        elif name == "wdown":
            wide_rows(name, "m", "gf", slot)
        elif name == "q":
            narrow_rows(name, "gqp", "n1", slot)
        elif name == "o":
            narrow_rows(name, "o", "ga", slot)
        else:
            kv_rows(slot)

    sent = []
    pair = {}

    def combine(k):
        part, first, tiles = CHUNKS[STEPS[k]]
        axis = ORDERS[part][0]
        pair[k].wait_recv()

        @pl.loop(0, 16)
        def _(i):
            for j in range(4):
                at = (part, i // 4, i % 4, j, pl.ds(first, tiles))
                total[at] = (total[at].astype(f32) + from_core[at].astype(f32)).astype(bf16)

        first_hop(k, 2, 0, 1, 1, 0)
        first_hop(k, 2, 1, 3, 1, 1)
        first_hop(k, 1, 1, 1, 2, 3)
        first_hop(k, 3, 0, 3, 0, 4)

    def half_slab(ref, k, slot, which):
        part, first, tiles = CHUNKS[STEPS[k]]
        return ref.at[part, slot, HALVES[which], :, pl.ds(first, tiles)]

    def first_hop(k, by, which, step, slot, sem):
        part, _, _ = CHUNKS[STEPS[k]]
        axis = ORDERS[part][0]
        copy = sending(
            half_slab(total, k, (me[axis] + by) % 4, which),
            half_slab(got_one, k, slot, which),
            one_send.at[k, sem],
            one_recv.at[k, sem],
            moved(me, axis, step),
        )
        copy.start()
        sent.append(copy)

    def first_got(k, which, slot, sem):
        part, _, _ = CHUNKS[STEPS[k]]
        there = half_slab(got_one, k, slot, which)
        sending(
            there, there, one_send.at[k, sem], one_recv.at[k, sem], moved(me, ORDERS[part][0], 1)
        ).wait_recv()

    def relay(k):
        part, first, tiles = CHUNKS[STEPS[k]]
        axis = ORDERS[part][0]
        for which, step, slot, sem in ((0, 1, 2, 2), (1, 3, 0, 5)):
            first_got(k, which, 1, which)
            to = (me[axis] + step) % 4

            @pl.loop(0, 2)
            def _(i, which=which, to=to):
                for j in range(4):
                    at = (part, to, 2 * which + i, j, pl.ds(first, tiles))
                    more = got_one[part, 1, 2 * which + i, j, pl.ds(first, tiles)].astype(f32)
                    total[at] = (total[at].astype(f32) + more).astype(bf16)

            first_hop(k, step, which, step, slot, sem)

    def second(g):
        part, first, tiles = GROUPS[g]
        one, two, _ = ORDERS[part]
        for k in IN_GROUP[g]:
            first_got(k, 0, 2, 2)
            first_got(k, 1, 2, 3)
            first_got(k, 0, 0, 4)
            first_got(k, 1, 0, 5)

        @pl.loop(0, 16)
        def _(i):
            at = (part, me[one], i // 4, i % 4, pl.ds(first, tiles))
            value = total[at].astype(f32)
            for s in (0, 2):
                value += got_one[part, s, i // 4, i % 4, pl.ds(first, tiles)].astype(f32)
            total[at] = value.astype(bf16)

        for by in (2, 1, 3):
            copy = sending(
                total.at[part, me[one], (me[two] + by) % 4, :, pl.ds(first, tiles)],
                got_two.at[part, 3 - by, :, pl.ds(first, tiles)],
                two_send.at[g, by - 1],
                two_recv.at[g, 3 - by],
                moved(me, two, by),
            )
            copy.start()
            sent.append(copy)

    def third(g):
        part, first, tiles = GROUPS[g]
        one, two, three = ORDERS[part]
        for by in (1, 3, 2):
            there = got_two.at[part, by - 1, :, pl.ds(first, tiles)]
            sending(
                there, there, two_send.at[g, by - 1], two_recv.at[g, by - 1], moved(me, two, by)
            ).wait_recv()

        @pl.loop(0, 4)
        def _(i):
            at = (part, me[one], me[two], i, pl.ds(first, tiles))
            value = total[at].astype(f32)
            for s in range(3):
                value += got_two[part, s, i, pl.ds(first, tiles)].astype(f32)
            total[at] = value.astype(bf16)

        for by in (2, 1, 3):
            copy = sending(
                total.at[part, me[one], me[two], (me[three] + by) % 4, pl.ds(first, tiles)],
                got_three.at[part, 3 - by, pl.ds(first, tiles)],
                three_send.at[g, by - 1],
                three_recv.at[g, 3 - by],
                moved(me, three, by),
            )
            copy.start()
            sent.append(copy)

    def last(g):
        part, first, tiles = GROUPS[g]
        one, two, three = ORDERS[part]
        for by in (1, 3, 2):
            there = got_three.at[part, by - 1, pl.ds(first, tiles)]
            sending(
                there, there, three_send.at[g, by - 1], three_recv.at[g, by - 1], moved(me, three, by)
            ).wait_recv()
        at = (part, me[one], me[two], me[three], pl.ds(first, tiles))
        value = total[at].astype(f32)
        for s in range(3):
            value += got_three[part, s, pl.ds(first, tiles)].astype(f32)
        total[at] = value.astype(bf16)
        return total.at[at]

    gathers = []

    def start_gather(g):
        part, first, tiles = GROUPS[g]
        order = ORDERS[part]

        def region(fixed, core):
            spot = tuple(fixed.get(axis, slice(None)) for axis in order)
            return all_ref.at[(core, part, *spot, pl.ds(first, tiles))]

        gathers.append(Gather(me, part, order[::-1], last(g), region, spread_sems))
        gathers[-1].start()

    shares = []

    def share(g):
        part, first, tiles = GROUPS[g]
        mine = last(g)
        low = me["z"] % 2

        def spot(low, core):
            return share_ref.at[low * 2 + core, part, pl.ds(0, tiles)]

        local = pltpu.make_async_copy(mine, spot(low, core), share_local.at[part])
        local.start()
        shares.append(local.wait)
        for k, peer in enumerate(
            (other_low(me), other_core(me), other_core(other_low(me)))
        ):
            copy = sending(
                mine, spot(low, core), share_send.at[part, k], share_recv.at[part, k], peer
            )
            copy.start()
            sent.append(copy)
            there = spot(peer["z"] % 2, peer["c"])
            shares.append(
                sending(there, there, share_send.at[part, k], share_recv.at[part, k], peer).wait_recv
            )

    def gather_near():
        for item in gathers:
            item.arrive(0)
            item.spread(1)

    def gather_ring():
        for item in gathers:
            item.arrive(1)
            item.begin_ring()

    def every(task, groups):
        for g in groups:
            task(g)

    meanwhile = {
        "wdown": lambda: every(second, (0, 1)),
        "gate": lambda: every(second, (2,)),
        "up": lambda: every(third, (0, 1, 2)),
        "kv": lambda: every(start_gather, (0, 1, 2)),
    }
    for k, name in enumerate(STEPS):
        part, first, tiles = CHUNKS[name]
        slot = k % 2
        for need in NEEDS[name]:
            loads[need, 0].wait()
            loads[need, 1].wait()
        if k >= 2:
            pair[k - 2].wait_send()
        work(name, slot)
        pair[k] = sending(
            to_core.at[slot, :, :, :, pl.ds(0, tiles)],
            from_core.at[part, :, :, :, pl.ds(first, tiles)],
            pair_send.at[k],
            pair_recv.at[k],
            other_core(me),
        )
        pair[k].start()
        if k >= 1:
            combine(k - 1)
        if k >= 2:
            relay(k - 2)
        if name in meanwhile:
            meanwhile[name]()
    final = len(STEPS) - 1
    combine(final)
    relay(final - 1)
    gather_near()
    relay(final)
    gather_ring()
    every(second, (3, 4, 5))
    for item in gathers:
        item.turn_ring()
    every(third, (3, 4, 5))
    every(share, (3, 4, 5))
    for item in gathers:
        item.end_ring()
    for item in gathers:
        item.finish()
    pair[final - 1].wait_send()
    pair[final].wait_send()
    for wait in shares:
        wait()
    for copy in sent:
        copy.wait_send()


def summed_gradients(kept, gain_tile):
    anywhere = pl.BlockSpec(memory_space=pl.ANY)
    dma = pltpu.SemaphoreType.DMA
    return pl.pallas_call(
        grads_kernel,
        out_shape=[
            jax.ShapeDtypeStruct((2, 3, 4, 4, 4, 9, 16, 128), bf16),
            jax.ShapeDtypeStruct((4, 3, 8, 16, 128), bf16),
        ],
        in_specs=[anywhere] * len(NAMES) + [pl.BlockSpec(memory_space=pltpu.VMEM)],
        out_specs=[anywhere] * 2,
        scratch_shapes=[
            pltpu.VMEM((2, 256, width), bf16) for _, width in NAMES
        ]
        + [
            pltpu.VMEM((3, 4, 4, 4, 16, 16, 128), bf16),
            pltpu.VMEM((3, 4, 4, 4, 16, 16, 128), bf16),
            pltpu.VMEM((2, 4, 4, 4, 8, 16, 128), bf16),
            pltpu.VMEM((3, 3, 4, 4, 16, 16, 128), bf16),
            pltpu.VMEM((3, 3, 4, 16, 16, 128), bf16),
            pltpu.VMEM((3, 3, 16, 16, 128), bf16),
            dma((len(NAMES), 2)),
            dma((len(STEPS),)),
            dma((len(STEPS),)),
            dma((len(STEPS), 6)),
            dma((len(STEPS), 6)),
            dma((6, 3)),
            dma((6, 3)),
            dma((6, 3)),
            dma((6, 3)),
            dma((3, 3)),
            dma((3, 3)),
            dma((3,)),
        ]
        + gather_sems(3),
        compiler_params=pltpu.CompilerParams(
            collective_id=2, has_side_effects=True, vmem_limit_bytes=60 * 2**20
        ),
        name="grads",
    )(*kept, gain_tile)


def unpack_kernel(all_ref, share_ref, *outs):
    (gain, wq, wkv, wo, wgate, wup, wdown, w_in, w_qkv, w_ffn, w_attn, w_down, w_back) = outs

    def tile(core, part, q, t):
        return all_ref[core, part, q, t].astype(f32)

    for q in range(8):
        for core in range(2):
            for t in range(5):
                w_in[0, 0, 80 * q + 16 * t : 80 * q + 16 * t + 16, 128 * core : 128 * core + 128] = tile(core, 1, q, t)
            for t in range(3):
                w_qkv[0, 32 * q + 16 * core : 32 * q + 16 * core + 16, 128 * t : 128 * t + 128] = tile(core, 1, q, 5 + t)
            row = slice(32 * q + 16 * core, 32 * q + 16 * core + 16)
            for k in range(4):
                for t in range(2):
                    w_ffn[k // 2, k % 2, row, 128 * t : 128 * t + 128] = tile(core, 0, q, 2 * k + t)
            for t in range(2):
                lanes = slice(128 * t, 128 * t + 128)
                w_attn[0, row, lanes] = tile(core, 2, q, t)
                for loop in range(2):
                    w_down[loop, row, lanes] = tile(core, 2, q, 2 + loop * 2 + t)
            for t in range(3 - core):
                u = 3 * core + t
                w_back[0, 0, 16 * q : 16 * q + 16, 128 * u : 128 * u + 128] = tile(core, 2, q, 6 + t)

    @pl.when(pl.program_id(0) == 0)
    def _():
        gain[...] = tile(1, 2, 0, 8)

        def mine(low, core, part, t):
            return share_ref[low * 2 + core, part, t].astype(f32)

        def wide(part, first):
            rows = []
            for low in range(2):
                for core in range(2):
                    rows.append(jnp.concatenate([mine(low, core, part, first + t) for t in range(5)], axis=1))
            return jnp.concatenate(rows, axis=0)

        def narrow(part, first):
            rows = []
            for low in range(2):
                tiles = [mine(low, 0, part, first + t) for t in range(3)]
                tiles += [mine(low, 1, part, first + t) for t in range(2)]
                rows.append(jnp.concatenate(tiles, axis=1))
            return jnp.concatenate(rows, axis=0)

        wgate[...] = wide(0, 0)
        wup[...] = wide(1, 0)
        wdown[...] = wide(2, 0)
        wq[...] = narrow(0, 5)
        wo[...] = narrow(1, 5)
        kv = [mine(0, 0, 2, 5), mine(0, 0, 2, 6), mine(1, 0, 2, 5), mine(0, 1, 2, 5), mine(1, 1, 2, 5)]
        wkv[...] = jnp.concatenate(kv, axis=1)


def unpacked(everything, shares):
    def whole(*shape):
        return jax.ShapeDtypeStruct(shape, f32), pl.BlockSpec(shape, lambda i: (0,) * len(shape))

    def cut(shape, block, index):
        return jax.ShapeDtypeStruct(shape, f32), pl.BlockSpec(block, index)

    outs = [
        whole(16, 128),
        whole(32, 640),
        whole(16, 640),
        whole(32, 640),
        whole(64, 640),
        whole(64, 640),
        whole(64, 640),
        cut((2, 4, 640, 256), (1, 1, 640, 256), lambda i: (i // 4, i % 4, 0, 0)),
        cut((2, 256, 1536), (1, 256, 384), lambda i: (i // 4, 0, i % 4)),
        cut((2, 2, 256, 2048), (2, 2, 256, 256), lambda i: (0, 0, 0, i)),
        cut((2, 1024, 256), (1, 256, 256), lambda i: (i // 4, i % 4, 0)),
        cut((2, 2048, 256), (2, 256, 256), lambda i: (0, i, 0)),
        cut((2, 2, 256, 640), (1, 1, 128, 640), lambda i: (i // 4, (i // 2) % 2, i % 2, 0)),
    ]
    return pl.pallas_call(
        unpack_kernel,
        grid=(8,),
        out_shape=[shape for shape, _ in outs],
        in_specs=[
            pl.BlockSpec((2, 3, 8, 9, 16, 128), lambda i: (0, 0, i, 0, 0, 0)),
            pl.BlockSpec((4, 3, 8, 16, 128), lambda i: (0, 0, 0, 0, 0)),
        ],
        out_specs=[spec for _, spec in outs],
        compiler_params=pltpu.CompilerParams(vmem_limit_bytes=60 * 2**20),
        name="unpack",
    )(everything.reshape(2, 3, 64, 9, 16, 128), shares)


def body(
    tokens,
    cotangent,
    doc_ids,
    doc_source,
    mixing,
    norm_gains,
    wq,
    wkv,
    wo,
    wgate,
    wup,
    wdown,
    *adapters,
):
    shards = (wq.T, wkv.T, wo, wgate.T, wup.T, wdown)
    block_out, token_grad, gain_tile, *kept = block_pass(
        tokens, cotangent, doc_ids, doc_source, mixing, norm_gains, shards, adapters
    )
    everything, shares = summed_gradients(kept, gain_tile)
    gain, wq_sum, wkv_sum, wo_sum, wgate_sum, wup_sum, wdown_sum, *sums = unpacked(everything, shares)
    return (
        block_out,
        token_grad,
        gain[:10].reshape(2, 640),
        wq_sum.T,
        wkv_sum.T,
        wo_sum,
        wgate_sum.T,
        wup_sum.T,
        wdown_sum,
        *sums,
    )


def solution(mesh):
    rows = P(("loop", "dp"), None)
    columns = P(None, "dp")
    placed = (
        *(rows,) * 4,
        P(),
        P(),
        columns,
        columns,
        P("dp", None),
        columns,
        columns,
        P("dp", None),
        *(P(),) * 6,
    )
    return jax.shard_map(
        body,
        mesh=mesh,
        in_specs=placed,
        out_specs=(
            rows,
            rows,
            P(),
            columns,
            columns,
            P("dp", None),
            columns,
            columns,
            P("dp", None),
            *(P(),) * 6,
        ),
        check_vma=False,
    )
```

```python
import jax
import jax.numpy as jnp
from jax import lax
from jax.experimental import pallas as pl
from jax.experimental.pallas import tpu as pltpu
from jax.sharding import PartitionSpec as P

eps = 1e-06
rope_base = 10000.0
masked = -1e30
MESH = pl.DeviceIdType.MESH
bf16 = jnp.bfloat16
f32 = jnp.float32

ORDERS = (("x", "y", "z"), ("y", "z", "x"), ("z", "x", "y"))

ADAPTER_CHUNKS = {
    "ffn": (0, 0, 4),
    "mix": (1, 0, 4),
    "attn": (2, 0, 1),
    "down": (2, 1, 2),
    "back": (2, 3, 2),
}
SHARED_CHUNKS = {
    "gate": (0, 4, 5),
    "q": (0, 9, 3),
    "up": (1, 4, 5),
    "o": (1, 9, 3),
    "wdown": (2, 5, 5),
    "kv": (2, 10, 2),
}
CHUNKS = {**ADAPTER_CHUNKS, **SHARED_CHUNKS}
ADAPTER_GROUPS = ((0, 0, 4), (1, 0, 4), (2, 0, 5))
GROUPS = ADAPTER_GROUPS + ((0, 4, 8), (1, 4, 8), (2, 5, 7))
LATE_STEPS = ("ffn", "down", "attn", "mix", "back")
STEPS = ("attn", "mix", "ffn", "down", "back", "q", "o", "kv", "wdown", "gate", "up")

HALVES = (slice(0, 2), slice(2, 4))


def place():
    lo = lax.axis_index("loop")
    dp = lax.axis_index("dp")
    return {"x": dp // 8, "y": dp % 4, "z": (dp // 4) % 2 * 2 + lo // 2, "c": lo % 2}


def device(at):
    return ((at["z"] % 2) * 2 + at["c"], at["x"] * 8 + (at["z"] // 2) * 4 + at["y"])


def moved(me, axis, by):
    return {**me, axis: (me[axis] + by) % 4}


def other_core(me):
    return {**me, "c": 1 - me["c"]}


def other_low(me):
    return {**me, "z": me["z"] + 1 - 2 * (me["z"] % 2)}


def greet(peers):
    barrier = pltpu.get_barrier_semaphore()
    for peer in peers:
        pl.semaphore_signal(barrier, inc=1, device_id=device(peer), device_id_type=MESH)
    pl.semaphore_wait(barrier, len(peers))


def sending(src, dst, send, recv, peer):
    return pltpu.make_async_remote_copy(
        src_ref=src,
        dst_ref=dst,
        send_sem=send,
        recv_sem=recv,
        device_id=device(peer),
        device_id_type=MESH,
    )


class Gather:
    def __init__(self, me, index, order, piece, region, sems):
        self.me, self.index, self.order, self.piece, self.region = me, index, order, piece, region
        self.send, self.recv, self.core_send, self.core_recv, self.local = sems
        self.sent = []

    def spot(self, stage, by):
        fixed = {axis: self.me[axis] for axis in self.order[stage:]}
        fixed[self.order[stage]] = (self.me[self.order[stage]] + by) % 4
        return fixed

    def to_core(self, source, fixed):
        i, me = self.index, self.me
        sending(
            source,
            self.region(fixed, me["c"]),
            self.core_send.at[i],
            self.core_recv.at[i],
            other_core(me),
        ).start()

    def half(self, by, which):
        return {**self.spot(2, by), self.order[0]: HALVES[which]}

    def pass_on(self, by, which, step, slot):
        here = self.region(self.half(by, which), self.me["c"])
        copy = sending(
            here,
            here,
            self.send.at[self.index, 6 + slot],
            self.recv.at[self.index, 6 + slot],
            moved(self.me, self.order[2], step),
        )
        copy.start()
        self.sent.append(copy)

    def take(self, by, which, slot):
        fixed = self.half(by, which)
        there = self.region(fixed, self.me["c"])
        sending(
            there,
            there,
            self.send.at[self.index, 6 + slot],
            self.recv.at[self.index, 6 + slot],
            moved(self.me, self.order[2], by),
        ).wait_recv()
        return there, fixed

    def begin_ring(self):
        self.pass_on(0, 0, 1, 0)
        self.pass_on(0, 1, 3, 3)
        self.pass_on(0, 1, 1, 1)
        self.pass_on(0, 0, 3, 2)

    def turn_ring(self):
        left = self.take(3, 0, 0)
        self.pass_on(3, 0, 1, 4)
        right = self.take(1, 1, 3)
        self.pass_on(1, 1, 3, 5)
        self.to_core(*left)
        self.to_core(*right)

    def end_ring(self):
        self.to_core(*self.take(3, 1, 1))
        self.to_core(*self.take(1, 0, 2))
        self.to_core(*self.take(2, 0, 4))
        self.to_core(*self.take(2, 1, 5))

    def start(self):
        fixed = self.spot(0, 0)
        self.kept = pltpu.make_async_copy(
            self.piece, self.region(fixed, self.me["c"]), self.local.at[self.index]
        )
        self.kept.start()
        self.spread(0, self.piece)
        self.to_core(self.piece, fixed)

    def spread(self, stage, source=None):
        if stage == 1:
            self.kept.wait()
        here = self.region(self.spot(stage, 0), self.me["c"])
        for by in (2, 1, 3):
            copy = sending(
                here if source is None else source,
                here,
                self.send.at[self.index, 3 * stage + by - 1],
                self.recv.at[self.index, 3 * stage + 3 - by],
                moved(self.me, self.order[stage], by),
            )
            copy.start()
            self.sent.append(copy)

    def arrive(self, stage):
        for by in (1, 3, 2):
            fixed = self.spot(stage, by)
            there = self.region(fixed, self.me["c"])
            sending(
                there,
                there,
                self.send.at[self.index, 3 * stage + by - 1],
                self.recv.at[self.index, 3 * stage + by - 1],
                moved(self.me, self.order[stage], by),
            ).wait_recv()
            self.to_core(there, fixed)

    def finish(self):
        i, me = self.index, self.me
        theirs = self.region({}, 1 - me["c"])
        sending(theirs, theirs, self.core_send.at[i], self.core_recv.at[i], other_core(me)).wait_recv()

    def close(self):
        i, me = self.index, self.me
        mine = self.region({}, me["c"])
        sending(mine, mine, self.core_send.at[i], self.core_recv.at[i], other_core(me)).wait_send()
        for copy in self.sent:
            copy.wait_send()


def gather_sems(items):
    return [
        pltpu.SemaphoreType.DMA((items, 12)),
        pltpu.SemaphoreType.DMA((items, 12)),
        pltpu.SemaphoreType.DMA((items,)),
        pltpu.SemaphoreType.DMA((items,)),
        pltpu.SemaphoreType.DMA((items,)),
    ]


def chip_peers(me):
    return [moved(me, axis, by) for axis in ("x", "y", "z") for by in (1, 2, 3)]


def chip_spot(order, x, y, z):
    at = {"x": x, "y": y, "z": z}
    return tuple(at[axis] for axis in order)


def split_spot(q):
    return (q // 16, (q // 4) % 4, q % 4)


class Sums:
    def __init__(self, me, steps, groups, buffers, sems):
        self.me, self.steps, self.groups = me, steps, groups
        self.total, self.from_core, self.to_core, self.got_one = buffers[:4]
        self.pair_send, self.pair_recv, self.one_send, self.one_recv = sems[:4]
        if len(sems) > 4:
            self.got_two, self.got_three = buffers[4:]
            self.two_send, self.two_recv, self.three_send, self.three_recv = sems[4:]
        self.pair = []
        self.sent = []

    def slot(self, name):
        k = self.steps.index(name)
        if k >= 2:
            self.pair[k - 2].wait_send()
        return k % 2

    def put(self, name, spot, slot, tile, zero, one):
        part, first, _ = CHUNKS[name]
        i, j, k = spot
        core = self.me["c"]
        self.total[part, i, j, k, first + tile] = jnp.where(core == 0, zero, one).astype(bf16)
        self.to_core[slot, i, j, k, tile] = jnp.where(core == 0, one, zero).astype(bf16)

    def send_pair(self, k):
        part, first, tiles = CHUNKS[self.steps[k]]
        self.pair.append(sending(
            self.to_core.at[k % 2, :, :, :, pl.ds(0, tiles)],
            self.from_core.at[part, :, :, :, pl.ds(first, tiles)],
            self.pair_send.at[k],
            self.pair_recv.at[k],
            other_core(self.me),
        ))
        self.pair[k].start()

    def combine(self, k):
        part, first, tiles = CHUNKS[self.steps[k]]
        self.pair[k].wait_recv()

        @pl.loop(0, 16)
        def _(i):
            for j in range(4):
                at = (part, i // 4, i % 4, j, pl.ds(first, tiles))
                self.total[at] = (self.total[at].astype(f32) + self.from_core[at].astype(f32)).astype(bf16)

        self.first_hop(k, 2, 0, 1, 1, 0)
        self.first_hop(k, 2, 1, 3, 1, 1)
        self.first_hop(k, 1, 1, 1, 2, 3)
        self.first_hop(k, 3, 0, 3, 0, 4)

    def half_slab(self, ref, k, slot, which):
        part, first, tiles = CHUNKS[self.steps[k]]
        return ref.at[part, slot, HALVES[which], :, pl.ds(first, tiles)]

    def axis(self, k):
        return ORDERS[CHUNKS[self.steps[k]][0]][0]

    def first_hop(self, k, by, which, step, slot, sem):
        axis = self.axis(k)
        copy = sending(
            self.half_slab(self.total, k, (self.me[axis] + by) % 4, which),
            self.half_slab(self.got_one, k, slot, which),
            self.one_send.at[k, sem],
            self.one_recv.at[k, sem],
            moved(self.me, axis, step),
        )
        copy.start()
        self.sent.append(copy)

    def first_got(self, k, which, slot, sem):
        there = self.half_slab(self.got_one, k, slot, which)
        sending(
            there,
            there,
            self.one_send.at[k, sem],
            self.one_recv.at[k, sem],
            moved(self.me, self.axis(k), 1),
        ).wait_recv()

    def relay(self, k):
        part, first, tiles = CHUNKS[self.steps[k]]
        for which, step, slot, sem in ((0, 1, 2, 2), (1, 3, 0, 5)):
            self.first_got(k, which, 1, which)
            to = (self.me[self.axis(k)] + step) % 4

            @pl.loop(0, 2)
            def _(i, which=which, to=to):
                for j in range(4):
                    at = (part, to, 2 * which + i, j, pl.ds(first, tiles))
                    more = self.got_one[part, 1, 2 * which + i, j, pl.ds(first, tiles)].astype(f32)
                    self.total[at] = (self.total[at].astype(f32) + more).astype(bf16)

            self.first_hop(k, step, which, step, slot, sem)

    def slab(self, part):
        return self.total.at[part, self.me[ORDERS[part][0]]]

    def first_sum(self, g):
        part, first, tiles = self.groups[g]
        slab, got = self.slab(part), self.got_one
        for k, name in enumerate(self.steps):
            if CHUNKS[name][0] == part and first <= CHUNKS[name][1] < first + tiles:
                self.first_got(k, 0, 2, 2)
                self.first_got(k, 1, 2, 3)
                self.first_got(k, 0, 0, 4)
                self.first_got(k, 1, 0, 5)

        @pl.loop(0, 16)
        def _(i):
            at = (i // 4, i % 4, pl.ds(first, tiles))
            value = slab[at].astype(f32)
            for s in (0, 2):
                value += got[part, s, i // 4, i % 4, pl.ds(first, tiles)].astype(f32)
            slab[at] = value.astype(bf16)

    def second(self, g):
        self.first_sum(g)
        self.send_second(g)

    def send_second(self, g):
        part, first, tiles = self.groups[g]
        two = ORDERS[part][1]
        for by in (2, 1, 3):
            copy = sending(
                self.slab(part).at[(self.me[two] + by) % 4, :, pl.ds(first, tiles)],
                self.got_two.at[part, 3 - by, :, pl.ds(first, tiles)],
                self.two_send.at[g, by - 1],
                self.two_recv.at[g, 3 - by],
                moved(self.me, two, by),
            )
            copy.start()
            self.sent.append(copy)

    def third(self, g):
        part, first, tiles = self.groups[g]
        _, two, three = ORDERS[part]
        me, got = self.me, self.got_two
        slab = self.slab(part).at[me[two]]
        for by in (1, 3, 2):
            there = got.at[part, by - 1, :, pl.ds(first, tiles)]
            sending(
                there, there, self.two_send.at[g, by - 1], self.two_recv.at[g, by - 1], moved(me, two, by)
            ).wait_recv()

        @pl.loop(0, 4)
        def _(i):
            at = (i, pl.ds(first, tiles))
            value = slab[at].astype(f32)
            for s in range(3):
                value += got[part, s, i, pl.ds(first, tiles)].astype(f32)
            slab[at] = value.astype(bf16)

        for by in (2, 1, 3):
            copy = sending(
                slab.at[(me[three] + by) % 4, pl.ds(first, tiles)],
                self.got_three.at[part, 3 - by, pl.ds(first, tiles)],
                self.three_send.at[g, by - 1],
                self.three_recv.at[g, 3 - by],
                moved(me, three, by),
            )
            copy.start()
            self.sent.append(copy)

    def last(self, g):
        part, first, tiles = self.groups[g]
        _, two, three = ORDERS[part]
        me, got = self.me, self.got_three
        for by in (1, 3, 2):
            there = got.at[part, by - 1, pl.ds(first, tiles)]
            sending(
                there, there, self.three_send.at[g, by - 1], self.three_recv.at[g, by - 1], moved(me, three, by)
            ).wait_recv()
        mine = self.slab(part).at[me[two], me[three], pl.ds(first, tiles)]
        value = mine[...].astype(f32)
        for s in range(3):
            value += got[part, s, pl.ds(first, tiles)].astype(f32)
        mine[...] = value.astype(bf16)
        return mine

    def finish(self):
        for copy in self.pair[-2:]:
            copy.wait_send()
        for copy in self.sent:
            copy.wait_send()


class LateSums(Sums):
    def __init__(self, me, groups, slab, buffers, sems):
        self.me, self.groups, self.kept = me, groups, slab
        self.got_two, self.got_three = buffers
        self.two_send, self.two_recv, self.three_send, self.three_recv = sems
        self.pair = []
        self.sent = []

    def slab(self, part):
        return self.kept.at[part]


def sums_scratch(tiles, widest, steps, groups, later=True):
    dma = pltpu.SemaphoreType.DMA
    buffers = [
        pltpu.VMEM((3, 4, 4, 4, tiles, 16, 128), bf16),
        pltpu.VMEM((3, 4, 4, 4, tiles, 16, 128), bf16),
        pltpu.VMEM((2, 4, 4, 4, widest, 16, 128), bf16),
        pltpu.VMEM((3, 3, 4, 4, tiles, 16, 128), bf16),
    ]
    sems = [dma((steps,)), dma((steps,)), dma((steps, 6)), dma((steps, 6))]
    if not later:
        return buffers + sems
    more, more_sems = late_scratch(tiles, groups)
    return buffers + more + sems + more_sems


def late_scratch(tiles, groups):
    return [
        pltpu.VMEM((3, 3, 4, tiles, 16, 128), bf16),
        pltpu.VMEM((3, 3, tiles, 16, 128), bf16),
    ], [pltpu.SemaphoreType.DMA((groups, 3))] * 4


def product(left, right):
    return lax.dot_general(left, right, (((1,), (0,)), ((), ())), preferred_element_type=f32)


def against(left, right):
    return lax.dot_general(left, right, (((1,), (1,)), ((), ())), preferred_element_type=f32)


def crossed(left, right):
    return lax.dot_general(left, right, (((0,), (0,)), ((), ())), preferred_element_type=f32)


def block(i, width=256):
    return pl.ds(pl.multiple_of(i * width, width), width)


def adapter_products(sums, held, name, gain=None):
    slot = sums.slot(name)

    def put(spot, tile, zero, one):
        sums.put(name, spot, slot, tile, zero, one)

    if name == "ffn":
        for j, (left, right) in enumerate((("u2a", "ggate"), ("u2b", "gup"))):

            @pl.loop(0, 2)
            def _(i, j=j, left=left, right=right):
                value = crossed(held[left][...], held[right][:, block(i, 1024)])
                for b in range(4):
                    for h in range(8):
                        for t in range(2):
                            lanes = slice(256 * b + 128 * t, 256 * b + 128 * t + 128)
                            put(
                                (2 * i + b // 2, (b % 2) * 2 + h // 4, h % 4),
                                j * 2 + t,
                                value[32 * h : 32 * h + 16, lanes],
                                value[32 * h + 16 : 32 * h + 32, lanes],
                            )

    elif name == "mix":
        for j, right in enumerate(("gu1a", "gu1b", "gu2a", "gu2b")):
            value = crossed(held["n1" if j < 2 else "n2"][...], held[right][...])
            for r in range(40):
                rows = slice(16 * r, 16 * r + 16)
                put(split_spot(10 * j + r // 4), r % 4, value[rows, :128], value[rows, 128:])
        for k in range(3):
            if k < 2:
                value = crossed(held["u1a"][...], held["gqp"][:, 512 * k : 512 * k + 512])
            else:
                value = crossed(held["u1b"][...], held["gkvp"][...])
            for t in range(4):
                lanes = slice(128 * t, 128 * t + 128)
                for h in range(8):
                    put(
                        split_spot(40 + 2 * (4 * k + t) + h // 4),
                        h % 4,
                        value[32 * h : 32 * h + 16, lanes],
                        value[32 * h + 16 : 32 * h + 32, lanes],
                    )
    elif name == "attn":
        value = crossed(held["o"][...], held["guo"][...])
        for q in range(64):
            rows = slice(16 * q, 16 * q + 16)
            put(split_spot(q), 0, value[rows, :128], value[rows, 128:])
    elif name == "down":

        @pl.loop(0, 2)
        def _(i):
            value = crossed(held["m"][:, block(i, 1024)], held["gud"][...])
            for b in range(4):
                for h in range(8):
                    row = 256 * b + 32 * h
                    for t in range(2):
                        lanes = slice(128 * t, 128 * t + 128)
                        put(
                            (2 * i + b // 2, (b % 2) * 2 + h // 4, h % 4),
                            t,
                            value[row : row + 16, lanes],
                            value[row + 16 : row + 32, lanes],
                        )

    else:
        for b, (left, right) in enumerate((("uo", "ga"), ("ud", "gf"))):
            value = crossed(held[left][...], held[right][...])
            for g in range(16):
                tiles = [value[16 * g : 16 * g + 16, 128 * t : 128 * t + 128] for t in range(5)]
                q = 2 * (16 * b + g)
                put(split_spot(q), 0, tiles[0], tiles[2])
                put(split_spot(q), 1, tiles[1], tiles[3])
                more = tiles[4] if gain is None or q else gain
                put(split_spot(q + 1), 0, tiles[4], more)
                put(split_spot(q + 1), 1, tiles[4], tiles[4])


WEIGHT_ITEMS = (
    (1, 3, 0, 256),
    (2, 3, 256, 640),
    (0, 4, 0, 128),
    (0, 5, 0, 128),
    (0, 0, 0, 640),
    (1, 1, 0, 640),
    (2, 2, 0, 640),
)

NAMES = (
    ("m", 2048),
    ("gf", 640),
    ("gud", 256),
    ("ud", 256),
    ("n2", 640),
    ("ggate", 2048),
    ("gup", 2048),
    ("gu2a", 256),
    ("gu2b", 256),
    ("u2a", 256),
    ("u2b", 256),
    ("o", 1024),
    ("ga", 640),
    ("guo", 256),
    ("uo", 256),
    ("n1", 640),
    ("gqp", 1024),
    ("gkvp", 512),
    ("gu1a", 256),
    ("gu1b", 256),
    ("u1a", 256),
    ("u1b", 256),
)
BOTH = ("m", "gf", "n2", "ggate", "gup", "o", "ga", "n1", "gqp", "gkvp")
ORDER = {name: i for i, (name, _) in enumerate(NAMES)}
ADAPTERS = ((4, 640, 256), (256, 1536), (2, 256, 2048), (1024, 256), (2048, 256), (2, 256, 640))


CURVE = 0.7978845608028654
CUBE = 0.044715


def block_kernel(*refs):
    (tokens, cotangent, doc_row, doc_source, mixing, gains) = refs[:6]
    shards = refs[6:12]
    adapters_in = refs[12:18]
    outs = refs[18:]
    block_out, token_grad, gain_tile, slab_out = outs[:4]
    kept_out = dict(zip((name for name, _ in NAMES), outs[4 : 4 + len(NAMES)]))
    rest = outs[4 + len(NAMES) :]
    kept = dict(zip((name for name, _ in NAMES), rest[: len(NAMES)]))
    rest = rest[len(NAMES) :]
    whole = rest[:6]
    both_piece = rest[6]
    a_in, a_qkv, a_ffn, a_attn, a_down, a_back = rest[7:13]
    (cosine, sine, mask, stream, hidden, q_rot, k_rot, value, probs, gate, up, grad, normed, gain_sum) = rest[13:27]
    kept_sem, adapter_sem, piece_sem = rest[27:30]
    gather = rest[30:35]
    slab_sem = rest[35]
    late = rest[36:]

    me = place()
    quarter = (me["z"] % 2) * 2 + me["c"]
    w_gate, w_up, w_down, w_both, w_kv, w_kv_last = whole

    fetch = [
        pltpu.make_async_copy(shards[0], both_piece.at[:32], piece_sem.at[0]),
        pltpu.make_async_copy(shards[2], both_piece.at[32:], piece_sem.at[1]),
    ]
    for copy in fetch:
        copy.start()
    adapter_names = ("in", "qkv", "ffn", "attn", "down", "back")
    waiting = {}

    def load(name, loop):
        i = adapter_names.index(name)
        target = (a_in, a_qkv, a_ffn, a_attn, a_down, a_back)[i]
        waiting[name] = pltpu.make_async_copy(adapters_in[i].at[loop], target, adapter_sem.at[i])
        waiting[name].start()

    def need(name):
        if name in waiting:
            waiting.pop(name).wait()

    for name in adapter_names:
        load(name, 0)
    greet(chip_peers(me) + [other_core(me)])
    for copy in fetch:
        copy.wait()
    own = pl.ds(pl.multiple_of(quarter * 16, 16), 16)
    sources = (shards[3].at[own], shards[4].at[own], shards[5].at[own], both_piece.at[own])
    lanes_of_kv = pl.ds(pl.multiple_of(quarter * 128, 128), 128)
    sources += (shards[1].at[:, lanes_of_kv], shards[1].at[:, pl.ds(512, 128)])
    items = []
    for i, (part, array, low, high) in enumerate(WEIGHT_ITEMS):

        def region(fixed, core, array=array, low=low, high=high):
            every = slice(None)
            zh, zl = every, every
            if isinstance(fixed.get("z"), slice):
                zh = fixed["z"].start // 2
            elif "z" in fixed:
                zh, zl = fixed["z"] // 2, fixed["z"] % 2
            return whole[array].at[
                fixed.get("x", every), zh, fixed.get("y", every), zl, core, :, pl.ds(low, high - low)
            ]

        items.append(
            Gather(me, i, ORDERS[part][::-1], sources[array].at[:, pl.ds(low, high - low)], region, gather)
        )
    for item in items:
        item.start()

    rows_of = lax.broadcasted_iota(jnp.int32, (256, 256), 0)
    columns_of = lax.broadcasted_iota(jnp.int32, (256, 256), 1)
    along = jnp.broadcast_to(doc_row[...], (256, 256))
    down = jnp.sum(jnp.where(rows_of == columns_of, along, 0), axis=1, keepdims=True)
    before = jnp.sum(jnp.where(along < down, 1, 0), axis=1, keepdims=True)
    mask[...] = jnp.where((along == down) & (columns_of <= rows_of), 1.0, 0.0)
    position = (lax.broadcasted_iota(jnp.int32, (256, 1), 0) - before).astype(f32)
    lanes = lax.broadcasted_iota(jnp.int32, (1, 128), 1).astype(f32)
    frequency = jnp.exp(lanes * (-2.0 / 256) * jnp.log(f32(rope_base)))
    angle = position * frequency
    cosine[...] = jnp.cos(angle)
    sine[...] = jnp.sin(angle)
    ratios = jnp.float32(0)
    for i in range(8):
        ratios += mixing[i].astype(f32)
    weight = jnp.zeros((256, 1), f32)
    for i in range(4):
        scale = mixing[doc_source[0, i]].astype(f32) * 8.0 / ratios
        weight = jnp.where(down == i, scale, weight)
    stream[0] = tokens[...].astype(f32)
    grad[...] = cotangent[...].astype(f32) * weight
    gain_sum[...] = jnp.zeros_like(gain_sum)
    soon, later = items[:4], items[4:]
    for item in items:
        item.arrive(0)
        item.spread(1)
    for item in soon:
        item.arrive(1)
        item.begin_ring()
    for item in later:
        item.arrive(1)
    for item in soon:
        item.turn_ring()
    for item in later:
        item.begin_ring()
    for item in soon:
        item.end_ring()
    for item in soon:
        item.finish()

    def turn_weights():
        for item in later:
            item.turn_ring()

    def rest_of_weights():
        for item in later:
            item.end_ring()
        for item in later:
            item.finish()

    def wide_rows(array, i):
        return array[i].reshape(512, 640)

    def q_rows(i):
        return w_both[i, :, :, 0].reshape(256, 640)

    def o_rows(i):
        return w_both[i, :, :, 1].reshape(256, 640)

    def kv_rows(i):
        return kv_of(slice(2 * i, 2 * i + 2), 256)

    def kv_of(x, rows):
        tiles = [w_kv[x, :, :, low, core].reshape(rows, 128) for low in range(2) for core in range(2)]
        return jnp.concatenate([*tiles, w_kv_last[x, :, :, 0, 0].reshape(rows, 128)], axis=1)

    def q_all():
        return w_both[:, :, :, 0].reshape(1024, 640)

    def o_all():
        return w_both[:, :, :, 1].reshape(1024, 640)

    def kv_all():
        return kv_of(slice(0, 4), 512)

    def all_rows(array):
        return array[...].reshape(2048, 640)

    scale = 256 ** (-0.5)

    def rotated(first, second, sign):
        c = cosine[...]
        s = sine[...] * sign
        return first * c - second * s, second * c + first * s

    def out_of(name, loop):
        target = kept_out[name].at[loop] if name in BOTH else kept_out[name]
        return pltpu.make_async_copy(kept[name], target, kept_sem.at[ORDER[name]])

    leaving = set()

    def to_hbm(names, loop):
        for name in names:
            if loop == 0 or name in BOTH:
                out_of(name, loop).start()
                leaving.add((name, loop))

    def drained(names, loop):
        for name in names:
            if (name, loop) in leaving:
                leaving.discard((name, loop))
                out_of(name, loop).wait()

    def norm(source, gain, target):
        for i in range(4):
            rows = slice(64 * i, 64 * i + 64)
            x = source[rows, :]
            inverse = lax.rsqrt(jnp.mean(x * x, axis=-1, keepdims=True) + eps)
            target[rows, :] = (x * inverse * gain).astype(bf16)

    first_names = ("n1", "u1a", "u1b", "o", "uo")
    second_names = ("n2", "u2a", "u2b", "m", "ud")

    def forward(loop):
        drained(first_names, 0)
        need("in")
        norm(stream.at[loop], gains[0:1, :], kept["n1"])
        kept["u1a"][...] = product(kept["n1"][...], a_in[0]).astype(bf16)
        kept["u1b"][...] = product(kept["n1"][...], a_in[1]).astype(bf16)

        need("qkv")
        k_pre = against(kept["n1"][...], kv_rows(0)) + product(kept["u1b"][...], a_qkv[:, 1024:1280])
        first, second = rotated(k_pre[:, :128], k_pre[:, 128:], 1.0)
        k_rot[loop, :, :128] = first.astype(bf16)
        k_rot[loop, :, 128:] = second.astype(bf16)
        value[loop] = (
            against(kept["n1"][...], kv_rows(1)) + product(kept["u1b"][...], a_qkv[:, 1280:1536])
        ).astype(bf16)

        if loop == 0:
            turn_weights()
        for h in range(4):
            at = slice(256 * h, 256 * h + 256)
            q_pre = against(kept["n1"][...], q_rows(h)) + product(kept["u1a"][...], a_qkv[:, at])
            first, second = rotated(q_pre[:, :128], q_pre[:, 128:], 1.0)
            q_rot[loop, h, :, :128] = first.astype(bf16)
            q_rot[loop, h, :, 128:] = second.astype(bf16)
            scores = against(q_rot[loop, h], k_rot[loop]) * scale
            scores = jnp.where(mask[...] > 0.5, scores, masked)
            expo = jnp.exp(scores - jnp.max(scores, axis=-1, keepdims=True))
            p = expo * (1.0 / jnp.sum(expo, axis=-1, keepdims=True))
            probs[loop, h] = p
            kept["o"][:, at] = product(p.astype(bf16), value[loop]).astype(bf16)

        if loop == 0:
            load("qkv", 1)
        need("attn")
        need("back")
        kept["uo"][...] = product(kept["o"][...], a_attn[...]).astype(bf16)
        hidden[loop] = stream[loop] + (
            product(kept["o"][...], o_all()) + product(kept["uo"][...], a_back[0])
        )
        to_hbm(first_names, loop)
        if loop == 0:
            load("attn", 1)
        drained(second_names, 0)
        if loop == 0:
            rest_of_weights()
        norm(hidden.at[loop], gains[1:2, :], kept["n2"])
        kept["u2a"][...] = product(kept["n2"][...], a_in[2]).astype(bf16)
        kept["u2b"][...] = product(kept["n2"][...], a_in[3]).astype(bf16)
        if loop == 0:
            load("in", 1)
        need("ffn")

        for i in range(4):
            at = slice(512 * i, 512 * i + 512)
            g = against(kept["n2"][...], wide_rows(w_gate, i)) + product(
                kept["u2a"][...], a_ffn[0, :, at]
            )
            u = against(kept["n2"][...], wide_rows(w_up, i)) + product(
                kept["u2b"][...], a_ffn[1, :, at]
            )
            gate[loop, :, at] = g
            up[loop, :, at] = u
            bend = jnp.tanh(CURVE * (g + CUBE * g * g * g))
            kept["m"][:, at] = (0.5 * g * (1.0 + bend) * u).astype(bf16)

        if loop == 0:
            load("ffn", 1)
        need("down")
        kept["ud"][...] = product(kept["m"][...], a_down[...]).astype(bf16)
        stream[loop + 1] = hidden[loop] + (
            product(kept["m"][...], all_rows(w_down)) + product(kept["ud"][...], a_back[1])
        )
        to_hbm(second_names, loop)
        if loop == 0:
            load("down", 1)
            load("back", 1)

    def norm_back(source, which):
        gain = gains[which : which + 1, :]

        for i in range(4):
            rows = slice(64 * i, 64 * i + 64)
            x = source[rows, :]
            g = normed[rows, :]
            inverse = lax.rsqrt(jnp.mean(x * x, axis=-1, keepdims=True) + eps)
            scaled = g * gain
            step = inverse * (
                scaled - x * inverse * inverse * jnp.mean(scaled * x, axis=-1, keepdims=True)
            )
            grad[rows, :] = grad[rows, :] + step
            gain_sum[which : which + 1, :] += jnp.sum(g * x * inverse, axis=0, keepdims=True)

    ffn_names = ("gf", "gud", "ggate", "gup", "gu2a", "gu2b")
    attention_names = ("ga", "guo", "gqp", "gkvp", "gu1a", "gu1b")

    def backward_ffn(loop):
        drained(ffn_names, 1)
        need("back")
        need("down")
        kept["gf"][...] = grad[...].astype(bf16)
        kept["gud"][...] = against(kept["gf"][...], a_back[1]).astype(bf16)

        for i in range(4):
            at = slice(512 * i, 512 * i + 512)
            gm = against(kept["gf"][...], wide_rows(w_down, i)) + against(
                kept["gud"][...], a_down[at, :]
            )
            g = gate[loop, :, at]
            u = up[loop, :, at]
            square = g * g
            bend = jnp.tanh(CURVE * (g + CUBE * g * square))
            half = 0.5 * (1.0 + bend)
            slope = half + 0.5 * g * (1.0 - bend * bend) * (CURVE * (1.0 + 3.0 * CUBE * square))
            kept["ggate"][:, at] = (gm * u * slope).astype(bf16)
            kept["gup"][:, at] = (gm * (g * half)).astype(bf16)

        need("ffn")
        kept["gu2a"][...] = against(kept["ggate"][...], a_ffn[0]).astype(bf16)
        kept["gu2b"][...] = against(kept["gup"][...], a_ffn[1]).astype(bf16)
        to_hbm(ffn_names, loop)

    def backward_hidden(loop):
        need("in")
        normed[...] = (
            product(kept["ggate"][...], all_rows(w_gate))
            + product(kept["gup"][...], all_rows(w_up))
            + against(kept["gu2a"][...], a_in[2])
            + against(kept["gu2b"][...], a_in[3])
        )
        norm_back(hidden.at[loop], 1)

    def backward_attention(loop, between=()):
        drained(attention_names, 1)
        need("attn")
        kept["ga"][...] = grad[...].astype(bf16)
        kept["guo"][...] = against(kept["ga"][...], a_back[0]).astype(bf16)

        def head(h, carry):
            grad_key, grad_value = carry
            at = slice(256 * h, 256 * h + 256)
            go = (
                against(kept["ga"][...], o_rows(h)) + against(kept["guo"][...], a_attn[at, :])
            ).astype(bf16)
            p = probs[loop, h]
            gp = against(go, value[loop])
            gs = (p * (gp - jnp.sum(p * gp, axis=-1, keepdims=True))).astype(bf16)
            gq = product(gs, k_rot[loop]) * scale
            first, second = rotated(gq[:, :128], gq[:, 128:], -1.0)
            kept["gqp"][:, 256 * h : 256 * h + 128] = first.astype(bf16)
            kept["gqp"][:, 256 * h + 128 : 256 * h + 256] = second.astype(bf16)
            grad_key += crossed(gs, q_rot[loop, h])
            grad_value += crossed(p.astype(bf16), go)
            return grad_key, grad_value

        sums_of_heads = (jnp.zeros((256, 256), f32), jnp.zeros((256, 256), f32))
        for h in range(4):
            sums_of_heads = head(h, sums_of_heads)
            if h == 2:
                for task in between:
                    task()
        grad_key, grad_value = sums_of_heads
        grad_key = grad_key * scale
        first, second = rotated(grad_key[:, :128], grad_key[:, 128:], -1.0)
        kept["gkvp"][:, :128] = first.astype(bf16)
        kept["gkvp"][:, 128:256] = second.astype(bf16)
        kept["gkvp"][:, 256:] = grad_value.astype(bf16)
        need("qkv")
        kept["gu1a"][...] = against(kept["gqp"][...], a_qkv[:, :1024]).astype(bf16)
        kept["gu1b"][...] = against(kept["gkvp"][...], a_qkv[:, 1024:]).astype(bf16)
        to_hbm(attention_names, loop)

    def backward_stream(loop):
        normed[...] = (
            product(kept["gqp"][...], q_all())
            + product(kept["gkvp"][...], kv_all())
            + against(kept["gu1a"][...], a_in[0])
            + against(kept["gu1b"][...], a_in[1])
        )
        norm_back(stream.at[loop], 0)

    sums = Sums(me, LATE_STEPS, ADAPTER_GROUPS, late[:4], late[4:])

    def summing(name):
        adapter_products(sums, kept, name)
        sums.send_pair(LATE_STEPS.index(name))

    forward(0)
    forward(1)
    block_out[...] = stream[2].astype(bf16)
    backward_ffn(1)
    summing("ffn")
    summing("down")
    backward_hidden(1)
    sums.combine(0)
    backward_attention(1)
    sums.combine(1)
    sums.relay(0)
    summing("attn")
    backward_stream(1)
    for name in ("back", "down", "ffn", "in", "attn", "qkv"):
        load(name, 0)
    summing("mix")
    sums.combine(2)
    sums.relay(1)
    summing("back")
    backward_ffn(0)
    sums.combine(3)
    sums.combine(4)
    sums.relay(2)
    backward_hidden(0)
    backward_attention(0, (lambda: sums.relay(3), lambda: sums.relay(4)))
    backward_stream(0)
    token_grad[...] = grad[...]
    gain_tile[...] = jnp.zeros_like(gain_tile)
    for i in range(2):
        for t in range(5):
            gain_tile[5 * i + t : 5 * i + t + 1, :] = gain_sum[i : i + 1, 128 * t : 128 * t + 128]
    for g in range(3):
        sums.first_sum(g)
    slab_copies = []
    for part in range(3):
        slab_copies.append(pltpu.make_async_copy(sums.slab(part), slab_out.at[part], slab_sem.at[part]))
        slab_copies[-1].start()
    sums.finish()
    for item in items:
        item.close()
    for copy in slab_copies:
        copy.wait()
    for names in (first_names, second_names, ffn_names, attention_names):
        for loop in range(2):
            drained(names, loop)


def block_pass(tokens, cotangent, doc_ids, doc_source, mixing, norm_gains, shards, adapters):
    vmem = pl.BlockSpec(memory_space=pltpu.VMEM)
    smem = pl.BlockSpec(memory_space=pltpu.SMEM)
    anywhere = pl.BlockSpec(memory_space=pl.ANY)
    dma = pltpu.SemaphoreType.DMA
    return pl.pallas_call(
        block_kernel,
        out_shape=[
            jax.ShapeDtypeStruct((256, 640), bf16),
            jax.ShapeDtypeStruct((256, 640), f32),
            jax.ShapeDtypeStruct((16, 128), f32),
            jax.ShapeDtypeStruct((3, 4, 4, 5, 16, 128), bf16),
        ]
        + [
            jax.ShapeDtypeStruct((2, 256, width) if name in BOTH else (256, width), bf16)
            for name, width in NAMES
        ],
        in_specs=[vmem, vmem, vmem, smem, smem, vmem] + [anywhere] * 12,
        out_specs=[vmem] * 3 + [anywhere] * (1 + len(NAMES)),
        scratch_shapes=[pltpu.VMEM((256, width), bf16) for _, width in NAMES]
        + [pltpu.VMEM((4, 2, 4, 2, 2, 16, 640), bf16)] * 4
        + [pltpu.VMEM((4, 2, 4, 2, 2, 16, 128), bf16)] * 2
        + [pltpu.VMEM((64, 640), bf16)]
        + [pltpu.VMEM(shape, bf16) for shape in ADAPTERS]
        + [
            pltpu.VMEM((256, 128), f32),
            pltpu.VMEM((256, 128), f32),
            pltpu.VMEM((256, 256), f32),
            pltpu.VMEM((3, 256, 640), f32),
            pltpu.VMEM((2, 256, 640), f32),
            pltpu.VMEM((2, 4, 256, 256), bf16),
            pltpu.VMEM((2, 256, 256), bf16),
            pltpu.VMEM((2, 256, 256), bf16),
            pltpu.VMEM((2, 4, 256, 256), f32),
            pltpu.VMEM((2, 256, 2048), f32),
            pltpu.VMEM((2, 256, 2048), f32),
            pltpu.VMEM((256, 640), f32),
            pltpu.VMEM((256, 640), f32),
            pltpu.VMEM((2, 640), f32),
            dma((len(NAMES),)),
            dma((6,)),
            dma((2,)),
        ]
        + gather_sems(len(WEIGHT_ITEMS))
        + [dma((3,))]
        + sums_scratch(5, 4, len(LATE_STEPS), len(ADAPTER_GROUPS), later=False),
        compiler_params=pltpu.CompilerParams(
            collective_id=1, has_side_effects=True, vmem_limit_bytes=60 * 2**20
        ),
        name="block",
    )(tokens, cotangent, doc_ids, doc_source, mixing, norm_gains, *shards, *adapters)


NEEDS = {
    "attn": ("o", "guo"),
    "mix": ("n1", "n2", "gu1a", "gu1b", "gu2a", "gu2b", "u1a", "gqp", "u1b", "gkvp"),
    "ffn": ("u2a", "ggate", "u2b", "gup"),
    "down": ("m", "gud"),
    "back": ("uo", "ga", "ud", "gf"),
}
LOAD_ORDER = tuple(name for step in STEPS[:5] for name in NEEDS[step])
SHARED_OPERANDS = {
    "gate": ("ggate", "n2"),
    "up": ("gup", "n2"),
    "wdown": ("m", "gf"),
    "q": ("gqp", "n1"),
    "o": ("o", "ga"),
    "kv": ("gkvp", "n1"),
}


def shared_products(sums, held, name):
    slot = sums.slot(name)
    order = ORDERS[CHUNKS[name][0]]
    left, right = (held[operand] for operand in SHARED_OPERANDS[name])
    right = right[...].reshape(512, 640)

    if name in ("gate", "up", "wdown"):

        @pl.loop(0, 2)
        def _(i):
            value = crossed(left[:, :, block(i, 1024)].reshape(512, 1024), right)
            for x in range(2):
                for high in range(2):
                    for y in range(4):
                        for low in range(2):
                            row = 512 * x + 256 * high + 64 * y + 32 * low
                            for t in range(5):
                                lanes = slice(128 * t, 128 * t + 128)
                                sums.put(
                                    name,
                                    chip_spot(order, 2 * i + x, y, high * 2 + low),
                                    slot,
                                    t,
                                    value[row : row + 16, lanes],
                                    value[row + 16 : row + 32, lanes],
                                )

    elif name in ("q", "o"):
        value = crossed(left[...].reshape(512, 1024), right)
        for x in range(4):
            for high in range(2):
                for y in range(4):
                    for low in range(2):
                        row = 256 * x + 128 * high + 32 * y + 16 * low
                        tiles = [value[row : row + 16, 128 * t : 128 * t + 128] for t in range(5)]
                        for t in range(3):
                            sums.put(
                                name,
                                chip_spot(order, x, y, high * 2 + low),
                                slot,
                                t,
                                tiles[t],
                                tiles[min(t + 3, 4)],
                            )
    else:
        value = crossed(left[...].reshape(512, 512), right)
        for k in range(32):
            tiles = [value[16 * k : 16 * k + 16, 128 * t : 128 * t + 128] for t in range(5)]
            for low, ends in enumerate((((0, 3), (1, 3)), ((2, 4), (2, 4)))):
                for t, (zero, one) in enumerate(ends):
                    sums.put(
                        name,
                        chip_spot(order, k // 8, k % 4, (k // 4) % 2 * 2 + low),
                        slot,
                        t,
                        tiles[zero],
                        tiles[one],
                    )


def grads_kernel(*refs):
    count = len(NAMES)
    given = dict(zip((name for name, _ in NAMES), refs[:count]))
    gain_ref, slab_ref = refs[count : count + 2]
    all_ref, share_ref = refs[count + 2 : count + 4]
    rest = refs[count + 4 :]
    held = dict(zip((name for name, _ in NAMES), rest[:count]))
    load_sem, share_send, share_recv, share_local = rest[count : count + 4]
    gather = rest[count + 4 : count + 9]
    me = place()
    slab, slab_sem = rest[count + 9 : count + 11]
    after = rest[count + 11 :]
    late_sums = LateSums(me, ADAPTER_GROUPS, slab, after[:2], after[2:6])
    sums = Sums(me, STEPS, GROUPS, after[6:12], after[12:])

    slab_copy = pltpu.make_async_copy(slab_ref, slab, slab_sem)
    slab_copy.start()

    loads = {}
    for i, name in enumerate(LOAD_ORDER):
        loads[name] = pltpu.make_async_copy(given[name], held[name], load_sem.at[i])
        loads[name].start()
    greet(chip_peers(me) + [other_core(me), other_core(other_low(me))])

    def spreading(loop, g, piece):
        part, first, tiles = GROUPS[g]
        order = ORDERS[part]

        def region(fixed, core):
            spot = tuple(fixed.get(axis, slice(None)) for axis in order)
            return all_ref.at[(loop, core, part, *spot, pl.ds(first, tiles))]

        item = Gather(me, loop * 3 + part, order[::-1], piece, region, gather)
        item.start()
        return item

    def near(items):
        for item in items:
            item.arrive(0)
            item.spread(1)

    def ring(items):
        for item in items:
            item.arrive(1)
            item.begin_ring()

    def turn(items):
        for item in items:
            item.turn_ring()

    def end(items):
        for item in items:
            item.end_ring()

    shares = []

    def share(g):
        part, first, tiles = GROUPS[g]
        mine = sums.last(g)
        low = me["z"] % 2

        def spot(low, core):
            return share_ref.at[low * 2 + core, part, pl.ds(0, tiles)]

        local = pltpu.make_async_copy(mine, spot(low, me["c"]), share_local.at[part])
        local.start()
        shares.append(local.wait)
        for k, peer in enumerate(
            (other_low(me), other_core(me), other_core(other_low(me)))
        ):
            copy = sending(
                mine, spot(low, me["c"]), share_send.at[part, k], share_recv.at[part, k], peer
            )
            copy.start()
            sums.sent.append(copy)
            there = spot(peer["z"] % 2, peer["c"])
            shares.append(
                sending(there, there, share_send.at[part, k], share_recv.at[part, k], peer).wait_recv
            )

    def summing(k):
        name = STEPS[k]
        if name in NEEDS:
            for operand in NEEDS[name]:
                loads[operand].wait()
            first_loop = {n: held[n].at[0] if n in BOTH else held[n] for n in held}
            adapter_products(sums, first_loop, name, gain_ref[...])
        else:
            shared_products(sums, held, name)
        sums.send_pair(k)

    def each(task, groups):
        for g in groups:
            task(g)

    slab_copy.wait()
    each(late_sums.send_second, range(3))
    late, early = [], []
    adapter_groups, shared_groups = range(3), range(3, 6)
    summing(0)
    summing(1)
    summing(2)
    summing(3)
    sums.combine(0)
    summing(4)
    each(late_sums.third, adapter_groups)
    sums.combine(2)
    sums.combine(1)
    sums.combine(3)
    sums.combine(4)
    late.extend(spreading(1, g, late_sums.last(g)) for g in adapter_groups)
    summing(5)
    summing(6)
    sums.relay(0)
    summing(7)
    sums.relay(2)
    sums.relay(4)
    sums.relay(3)
    sums.relay(1)
    summing(8)
    near(late)
    sums.combine(6)
    each(sums.second, adapter_groups)
    sums.combine(7)
    ring(late)
    sums.combine(5)
    summing(9)
    summing(10)
    each(sums.third, adapter_groups)
    sums.combine(8)
    sums.combine(9)
    sums.combine(10)
    early.extend(spreading(0, g, sums.last(g)) for g in adapter_groups)
    sums.relay(8)
    sums.relay(9)
    sums.relay(7)
    sums.relay(10)
    sums.relay(6)
    sums.relay(5)
    turn(late)
    near(early)
    each(sums.second, shared_groups)
    ring(early)
    each(sums.third, shared_groups)
    turn(early)
    end(late)
    each(share, shared_groups)
    end(early)
    for item in late + early:
        item.finish()
    for item in late + early:
        item.close()
    sums.finish()
    late_sums.finish()
    for wait in shares:
        wait()


def summed_gradients(kept, gain_tile, slab):
    anywhere = pl.BlockSpec(memory_space=pl.ANY)
    vmem = pl.BlockSpec(memory_space=pltpu.VMEM)
    dma = pltpu.SemaphoreType.DMA
    more, more_sems = late_scratch(5, len(ADAPTER_GROUPS))
    return pl.pallas_call(
        grads_kernel,
        out_shape=[
            jax.ShapeDtypeStruct((2, 2, 3, 4, 4, 4, 5, 16, 128), bf16),
            jax.ShapeDtypeStruct((4, 3, 8, 16, 128), bf16),
        ],
        in_specs=[anywhere] * len(NAMES) + [vmem, anywhere],
        out_specs=[anywhere] * 2,
        scratch_shapes=[
            pltpu.VMEM((2, 256, width) if name in BOTH else (256, width), bf16)
            for name, width in NAMES
        ]
        + [
            dma((len(NAMES),)),
            dma((3, 3)),
            dma((3, 3)),
            dma((3,)),
        ]
        + gather_sems(6)
        + [pltpu.VMEM((3, 4, 4, 5, 16, 128), bf16), dma]
        + more
        + more_sems
        + sums_scratch(12, 5, len(STEPS), len(GROUPS)),
        compiler_params=pltpu.CompilerParams(
            collective_id=2, has_side_effects=True, vmem_limit_bytes=60 * 2**20
        ),
        name="grads",
    )(*kept, gain_tile, slab)


def unpack_kernel(zero_ref, one_ref, two_ref, share_ref, *outs):
    (gain, wq, wkv, wo, wgate, wup, wdown, w_in, w_qkv, w_ffn, w_attn, w_down, w_back) = outs
    loop, step = pl.program_id(0), pl.program_id(1)

    for q in range(16):
        for core in range(2):
            row = slice(32 * (q % 8) + 16 * core, 32 * (q % 8) + 16 * core + 16)
            for j in range(2):
                for t in range(2):
                    lanes = slice(256 * (q // 8) + 128 * t, 256 * (q // 8) + 128 * t + 128)
                    w_ffn[0, j, row, lanes] = zero_ref[0, core, 0, q, 2 * j + t].astype(f32)
            rows = slice(16 * q, 16 * q + 16)
            w_attn[0, rows, 128 * core : 128 * core + 128] = two_ref[0, core, 0, q, 0].astype(f32)
            for t in range(2):
                w_down[0, 32 * q + 16 * core : 32 * q + 16 * core + 16, 128 * t : 128 * t + 128] = two_ref[
                    0, core, 0, q, 1 + t
                ].astype(f32)
    for g in range(8):
        rows = slice(16 * g, 16 * g + 16)
        for t, (more, core, tile) in enumerate(((0, 0, 3), (0, 0, 4), (0, 1, 3), (0, 1, 4), (1, 0, 3))):
            w_back[0, 0, rows, 128 * t : 128 * t + 128] = two_ref[0, core, 0, 2 * g + more, tile].astype(f32)
    for core in range(2):
        for r in range(40):
            w_in[0, 0, 16 * r : 16 * r + 16, 128 * core : 128 * core + 128] = one_ref[
                0, core, 0, 10 * step + r // 4, r % 4
            ].astype(f32)
        for t in range(3):
            for h in range(8):
                w_qkv[0, 32 * h + 16 * core : 32 * h + 16 * core + 16, 128 * t : 128 * t + 128] = one_ref[
                    0, core, 0, 40 + 6 * step + 2 * t + h // 4, h % 4
                ].astype(f32)

    @pl.when((loop == 0) & (step == 0))
    def _():
        tile = two_ref[0, 1, 0, 1, 3].astype(f32)
        for i in range(2):
            for t in range(5):
                gain[i : i + 1, 128 * t : 128 * t + 128] = tile[5 * i + t : 5 * i + t + 1, :]

        def mine(low, core, part, t):
            return share_ref[low * 2 + core, part, t].astype(f32)

        def wide(part, first):
            rows = []
            for low in range(2):
                for core in range(2):
                    rows.append(jnp.concatenate([mine(low, core, part, first + t) for t in range(5)], axis=1))
            return jnp.concatenate(rows, axis=0)

        def narrow(part, first):
            rows = []
            for low in range(2):
                tiles = [mine(low, 0, part, first + t) for t in range(3)]
                tiles += [mine(low, 1, part, first + t) for t in range(2)]
                rows.append(jnp.concatenate(tiles, axis=1))
            return jnp.concatenate(rows, axis=0)

        wgate[...] = wide(0, 0)
        wup[...] = wide(1, 0)
        wdown[...] = wide(2, 0)
        wq[...] = narrow(0, 5)
        wo[...] = narrow(1, 5)
        kv = [mine(0, 0, 2, 5), mine(0, 0, 2, 6), mine(1, 0, 2, 5), mine(0, 1, 2, 5), mine(1, 1, 2, 5)]
        wkv[...] = jnp.concatenate(kv, axis=1)


def unpacked(everything, shares):
    def whole(*shape):
        return jax.ShapeDtypeStruct(shape, f32), pl.BlockSpec(shape, lambda l, s: (0,) * len(shape))

    def cut(shape, size, index):
        return jax.ShapeDtypeStruct(shape, f32), pl.BlockSpec(size, index)

    outs = [
        whole(2, 640),
        whole(32, 640),
        whole(16, 640),
        whole(32, 640),
        whole(64, 640),
        whole(64, 640),
        whole(64, 640),
        cut((2, 4, 640, 256), (1, 1, 640, 256), lambda l, s: (l, s, 0, 0)),
        cut((2, 256, 1536), (1, 256, 384), lambda l, s: (l, 0, s)),
        cut((2, 2, 256, 2048), (1, 2, 256, 512), lambda l, s: (l, 0, 0, s)),
        cut((2, 1024, 256), (1, 256, 256), lambda l, s: (l, s, 0)),
        cut((2, 2048, 256), (1, 512, 256), lambda l, s: (l, s, 0)),
        cut((2, 2, 256, 640), (1, 1, 128, 640), lambda l, s: (l, s // 2, s % 2, 0)),
    ]
    everything = everything.reshape(2, 2, 3, 64, 5, 16, 128)
    return pl.pallas_call(
        unpack_kernel,
        grid=(2, 4),
        out_shape=[shape for shape, _ in outs],
        in_specs=[
            pl.BlockSpec((1, 2, 1, 16, 5, 16, 128), lambda l, s: (l, 0, 0, s, 0, 0, 0)),
            pl.BlockSpec((1, 2, 1, 64, 5, 16, 128), lambda l, s: (l, 0, 1, 0, 0, 0, 0)),
            pl.BlockSpec((1, 2, 1, 16, 5, 16, 128), lambda l, s: (l, 0, 2, s, 0, 0, 0)),
            pl.BlockSpec((4, 3, 8, 16, 128), lambda l, s: (0, 0, 0, 0, 0)),
        ],
        out_specs=[spec for _, spec in outs],
        compiler_params=pltpu.CompilerParams(vmem_limit_bytes=60 * 2**20),
        name="unpack",
    )(everything, everything, everything, shares)


def body(
    tokens,
    cotangent,
    doc_ids,
    doc_source,
    mixing,
    norm_gains,
    wq,
    wkv,
    wo,
    wgate,
    wup,
    wdown,
    *adapters,
):
    shards = (wq.T, wkv.T, wo, wgate.T, wup.T, wdown)
    block_out, token_grad, gain_tile, slab, *kept = block_pass(
        tokens, cotangent, doc_ids, doc_source, mixing, norm_gains, shards, adapters
    )
    everything, shares = summed_gradients(kept, gain_tile, slab)
    gain, wq_sum, wkv_sum, wo_sum, wgate_sum, wup_sum, wdown_sum, *sums = unpacked(everything, shares)
    return (
        block_out,
        token_grad,
        gain,
        wq_sum.T,
        wkv_sum.T,
        wo_sum,
        wgate_sum.T,
        wup_sum.T,
        wdown_sum,
        *sums,
    )


def solution(mesh):
    rows = P(("loop", "dp"), None)
    columns = P(None, "dp")
    placed = (
        *(rows,) * 4,
        P(),
        P(),
        columns,
        columns,
        P("dp", None),
        columns,
        columns,
        P("dp", None),
        *(P(),) * 6,
    )
    return jax.shard_map(
        body,
        mesh=mesh,
        in_specs=placed,
        out_specs=(
            rows,
            rows,
            P(),
            columns,
            columns,
            P("dp", None),
            columns,
            columns,
            P("dp", None),
            *(P(),) * 6,
        ),
        check_vma=False,
    )
```

```python
import jax
import jax.numpy as jnp
from jax import lax
from jax.experimental import pallas as pl
from jax.experimental.pallas import tpu as pltpu
from jax.sharding import PartitionSpec as P

eps = 1e-06
rope_base = 10000.0
masked = -1e30
MESH = pl.DeviceIdType.MESH
bf16 = jnp.bfloat16
f32 = jnp.float32

ORDERS = (("x", "y", "z"), ("y", "z", "x"), ("z", "x", "y"))

ADAPTER_CHUNKS = {
    "ffn": (0, 0, 4),
    "mix": (1, 0, 4),
    "attn": (2, 0, 1),
    "down": (2, 1, 2),
    "back": (2, 3, 2),
}
SHARED_CHUNKS = {
    "gate": (0, 4, 5),
    "q": (0, 9, 3),
    "up": (1, 4, 5),
    "o": (1, 9, 3),
    "wdown": (2, 5, 5),
    "kv": (2, 10, 2),
}
CHUNKS = {**ADAPTER_CHUNKS, **SHARED_CHUNKS}
ADAPTER_GROUPS = ((0, 0, 4), (1, 0, 4), (2, 0, 5))
GROUPS = ADAPTER_GROUPS + ((0, 4, 8), (1, 4, 8), (2, 5, 7))
LATE_STEPS = ("ffn", "down", "mix", "attn", "back")
STEPS = ("attn", "mix", "ffn", "down", "back", "q", "o", "kv", "wdown", "gate", "up")

HALVES = (slice(0, 2), slice(2, 4))


def place():
    lo = lax.axis_index("loop")
    dp = lax.axis_index("dp")
    return {"x": dp // 8, "y": dp % 4, "z": (dp // 4) % 2 * 2 + lo // 2, "c": lo % 2}


def device(at):
    return ((at["z"] % 2) * 2 + at["c"], at["x"] * 8 + (at["z"] // 2) * 4 + at["y"])


def moved(me, axis, by):
    return {**me, axis: (me[axis] + by) % 4}


def other_core(me):
    return {**me, "c": 1 - me["c"]}


def other_low(me):
    return {**me, "z": me["z"] + 1 - 2 * (me["z"] % 2)}


def greet(peers):
    barrier = pltpu.get_barrier_semaphore()
    for peer in peers:
        pl.semaphore_signal(barrier, inc=1, device_id=device(peer), device_id_type=MESH)
    pl.semaphore_wait(barrier, len(peers))


def sending(src, dst, send, recv, peer):
    return pltpu.make_async_remote_copy(
        src_ref=src,
        dst_ref=dst,
        send_sem=send,
        recv_sem=recv,
        device_id=device(peer),
        device_id_type=MESH,
    )


class Gather:
    def __init__(self, me, index, order, piece, region, sems):
        self.me, self.index, self.order, self.piece, self.region = me, index, order, piece, region
        self.send, self.recv, self.core_send, self.core_recv, self.local = sems
        self.sent = []

    def spot(self, stage, by):
        fixed = {axis: self.me[axis] for axis in self.order[stage:]}
        fixed[self.order[stage]] = (self.me[self.order[stage]] + by) % 4
        return fixed

    def to_core(self, source, fixed):
        i, me = self.index, self.me
        sending(
            source,
            self.region(fixed, me["c"]),
            self.core_send.at[i],
            self.core_recv.at[i],
            other_core(me),
        ).start()

    def half(self, by, which):
        return {**self.spot(2, by), self.order[0]: HALVES[which]}

    def pass_on(self, by, which, step, slot):
        here = self.region(self.half(by, which), self.me["c"])
        copy = sending(
            here,
            here,
            self.send.at[self.index, 6 + slot],
            self.recv.at[self.index, 6 + slot],
            moved(self.me, self.order[2], step),
        )
        copy.start()
        self.sent.append(copy)

    def take(self, by, which, slot):
        fixed = self.half(by, which)
        there = self.region(fixed, self.me["c"])
        sending(
            there,
            there,
            self.send.at[self.index, 6 + slot],
            self.recv.at[self.index, 6 + slot],
            moved(self.me, self.order[2], by),
        ).wait_recv()
        return there, fixed

    def begin_ring(self):
        self.pass_on(0, 0, 1, 0)
        self.pass_on(0, 1, 3, 3)
        self.pass_on(0, 1, 1, 1)
        self.pass_on(0, 0, 3, 2)

    def turn_ring(self):
        left = self.take(3, 0, 0)
        self.pass_on(3, 0, 1, 4)
        right = self.take(1, 1, 3)
        self.pass_on(1, 1, 3, 5)
        self.to_core(*left)
        self.to_core(*right)

    def end_ring(self):
        self.to_core(*self.take(3, 1, 1))
        self.to_core(*self.take(1, 0, 2))
        self.to_core(*self.take(2, 0, 4))
        self.to_core(*self.take(2, 1, 5))

    def start(self):
        fixed = self.spot(0, 0)
        self.kept = pltpu.make_async_copy(
            self.piece, self.region(fixed, self.me["c"]), self.local.at[self.index]
        )
        self.kept.start()
        self.spread(0, self.piece)
        self.to_core(self.piece, fixed)

    def spread(self, stage, source=None):
        if stage == 1:
            self.kept.wait()
        here = self.region(self.spot(stage, 0), self.me["c"])
        for by in (2, 1, 3):
            copy = sending(
                here if source is None else source,
                here,
                self.send.at[self.index, 3 * stage + by - 1],
                self.recv.at[self.index, 3 * stage + 3 - by],
                moved(self.me, self.order[stage], by),
            )
            copy.start()
            self.sent.append(copy)

    def arrive(self, stage):
        for by in (1, 3, 2):
            fixed = self.spot(stage, by)
            there = self.region(fixed, self.me["c"])
            sending(
                there,
                there,
                self.send.at[self.index, 3 * stage + by - 1],
                self.recv.at[self.index, 3 * stage + by - 1],
                moved(self.me, self.order[stage], by),
            ).wait_recv()
            self.to_core(there, fixed)

    def finish(self):
        i, me = self.index, self.me
        theirs = self.region({}, 1 - me["c"])
        sending(theirs, theirs, self.core_send.at[i], self.core_recv.at[i], other_core(me)).wait_recv()

    def close(self):
        i, me = self.index, self.me
        mine = self.region({}, me["c"])
        sending(mine, mine, self.core_send.at[i], self.core_recv.at[i], other_core(me)).wait_send()
        for copy in self.sent:
            copy.wait_send()


def gather_sems(items):
    return [
        pltpu.SemaphoreType.DMA((items, 12)),
        pltpu.SemaphoreType.DMA((items, 12)),
        pltpu.SemaphoreType.DMA((items,)),
        pltpu.SemaphoreType.DMA((items,)),
        pltpu.SemaphoreType.DMA((items,)),
    ]


def chip_peers(me):
    return [moved(me, axis, by) for axis in ("x", "y", "z") for by in (1, 2, 3)]


def chip_spot(order, x, y, z):
    at = {"x": x, "y": y, "z": z}
    return tuple(at[axis] for axis in order)


def split_spot(q):
    return (q // 16, (q // 4) % 4, q % 4)


class Sums:
    def __init__(self, me, steps, groups, buffers, sems):
        self.me, self.steps, self.groups = me, steps, groups
        self.total, self.from_core, self.to_core, self.got_one = buffers[:4]
        self.pair_send, self.pair_recv, self.one_send, self.one_recv = sems[:4]
        if len(sems) > 4:
            self.got_two, self.got_three = buffers[4:]
            self.two_send, self.two_recv, self.three_send, self.three_recv = sems[4:]
        self.pair = []
        self.sent = []

    def slot(self, name):
        k = self.steps.index(name)
        if k >= 2:
            self.pair[k - 2].wait_send()
        return k % 2

    def put(self, name, spot, slot, tile, zero, one):
        part, first, _ = CHUNKS[name]
        i, j, k = spot
        core = self.me["c"]
        self.total[part, i, j, k, first + tile] = jnp.where(core == 0, zero, one).astype(bf16)
        self.to_core[slot, i, j, k, tile] = jnp.where(core == 0, one, zero).astype(bf16)

    def send_pair(self, k):
        part, first, tiles = CHUNKS[self.steps[k]]
        self.pair.append(sending(
            self.to_core.at[k % 2, :, :, :, pl.ds(0, tiles)],
            self.from_core.at[part, :, :, :, pl.ds(first, tiles)],
            self.pair_send.at[k],
            self.pair_recv.at[k],
            other_core(self.me),
        ))
        self.pair[k].start()

    def combine(self, k):
        part, first, tiles = CHUNKS[self.steps[k]]
        self.pair[k].wait_recv()

        @pl.loop(0, 16)
        def _(i):
            for j in range(4):
                at = (part, i // 4, i % 4, j, pl.ds(first, tiles))
                self.total[at] = (self.total[at].astype(f32) + self.from_core[at].astype(f32)).astype(bf16)

        self.first_hop(k, 2, 0, 1, 1, 0)
        self.first_hop(k, 2, 1, 3, 1, 1)
        self.first_hop(k, 1, 1, 1, 2, 3)
        self.first_hop(k, 3, 0, 3, 0, 4)

    def half_slab(self, ref, k, slot, which):
        part, first, tiles = CHUNKS[self.steps[k]]
        return ref.at[part, slot, HALVES[which], :, pl.ds(first, tiles)]

    def axis(self, k):
        return ORDERS[CHUNKS[self.steps[k]][0]][0]

    def first_hop(self, k, by, which, step, slot, sem):
        axis = self.axis(k)
        copy = sending(
            self.half_slab(self.total, k, (self.me[axis] + by) % 4, which),
            self.half_slab(self.got_one, k, slot, which),
            self.one_send.at[k, sem],
            self.one_recv.at[k, sem],
            moved(self.me, axis, step),
        )
        copy.start()
        self.sent.append(copy)

    def first_got(self, k, which, slot, sem):
        there = self.half_slab(self.got_one, k, slot, which)
        sending(
            there,
            there,
            self.one_send.at[k, sem],
            self.one_recv.at[k, sem],
            moved(self.me, self.axis(k), 1),
        ).wait_recv()

    def relay(self, k):
        part, first, tiles = CHUNKS[self.steps[k]]
        for which, step, slot, sem in ((0, 1, 2, 2), (1, 3, 0, 5)):
            self.first_got(k, which, 1, which)
            to = (self.me[self.axis(k)] + step) % 4

            @pl.loop(0, 2)
            def _(i, which=which, to=to):
                for j in range(4):
                    at = (part, to, 2 * which + i, j, pl.ds(first, tiles))
                    more = self.got_one[part, 1, 2 * which + i, j, pl.ds(first, tiles)].astype(f32)
                    self.total[at] = (self.total[at].astype(f32) + more).astype(bf16)

            self.first_hop(k, step, which, step, slot, sem)

    def slab(self, part):
        return self.total.at[part, self.me[ORDERS[part][0]]]

    def first_sum(self, g):
        part, first, tiles = self.groups[g]
        slab, got = self.slab(part), self.got_one
        for k, name in enumerate(self.steps):
            if CHUNKS[name][0] == part and first <= CHUNKS[name][1] < first + tiles:
                self.first_got(k, 0, 2, 2)
                self.first_got(k, 1, 2, 3)
                self.first_got(k, 0, 0, 4)
                self.first_got(k, 1, 0, 5)

        @pl.loop(0, 16)
        def _(i):
            at = (i // 4, i % 4, pl.ds(first, tiles))
            value = slab[at].astype(f32)
            for s in (0, 2):
                value += got[part, s, i // 4, i % 4, pl.ds(first, tiles)].astype(f32)
            slab[at] = value.astype(bf16)

    def second(self, g):
        self.first_sum(g)
        self.send_second(g)

    def send_second(self, g):
        part, first, tiles = self.groups[g]
        two = ORDERS[part][1]
        for by in (2, 1, 3):
            copy = sending(
                self.slab(part).at[(self.me[two] + by) % 4, :, pl.ds(first, tiles)],
                self.got_two.at[part, 3 - by, :, pl.ds(first, tiles)],
                self.two_send.at[g, by - 1],
                self.two_recv.at[g, 3 - by],
                moved(self.me, two, by),
            )
            copy.start()
            self.sent.append(copy)

    def third(self, g):
        part, first, tiles = self.groups[g]
        _, two, three = ORDERS[part]
        me, got = self.me, self.got_two
        slab = self.slab(part).at[me[two]]
        for by in (1, 3, 2):
            there = got.at[part, by - 1, :, pl.ds(first, tiles)]
            sending(
                there, there, self.two_send.at[g, by - 1], self.two_recv.at[g, by - 1], moved(me, two, by)
            ).wait_recv()

        @pl.loop(0, 4)
        def _(i):
            at = (i, pl.ds(first, tiles))
            value = slab[at].astype(f32)
            for s in range(3):
                value += got[part, s, i, pl.ds(first, tiles)].astype(f32)
            slab[at] = value.astype(bf16)

        for by in (2, 1, 3):
            copy = sending(
                slab.at[(me[three] + by) % 4, pl.ds(first, tiles)],
                self.got_three.at[part, 3 - by, pl.ds(first, tiles)],
                self.three_send.at[g, by - 1],
                self.three_recv.at[g, 3 - by],
                moved(me, three, by),
            )
            copy.start()
            self.sent.append(copy)

    def last(self, g):
        part, first, tiles = self.groups[g]
        _, two, three = ORDERS[part]
        me, got = self.me, self.got_three
        for by in (1, 3, 2):
            there = got.at[part, by - 1, pl.ds(first, tiles)]
            sending(
                there, there, self.three_send.at[g, by - 1], self.three_recv.at[g, by - 1], moved(me, three, by)
            ).wait_recv()
        mine = self.slab(part).at[me[two], me[three], pl.ds(first, tiles)]
        value = mine[...].astype(f32)
        for s in range(3):
            value += got[part, s, pl.ds(first, tiles)].astype(f32)
        mine[...] = value.astype(bf16)
        return mine

    def finish(self):
        for copy in self.pair[-2:]:
            copy.wait_send()
        for copy in self.sent:
            copy.wait_send()


class LateSums(Sums):
    def __init__(self, me, groups, slab, buffers, sems):
        self.me, self.groups, self.kept = me, groups, slab
        self.got_two, self.got_three = buffers
        self.two_send, self.two_recv, self.three_send, self.three_recv = sems
        self.pair = []
        self.sent = []

    def slab(self, part):
        return self.kept.at[part]


def sums_scratch(tiles, widest, steps, groups, later=True):
    dma = pltpu.SemaphoreType.DMA
    buffers = [
        pltpu.VMEM((3, 4, 4, 4, tiles, 16, 128), bf16),
        pltpu.VMEM((3, 4, 4, 4, tiles, 16, 128), bf16),
        pltpu.VMEM((2, 4, 4, 4, widest, 16, 128), bf16),
        pltpu.VMEM((3, 3, 4, 4, tiles, 16, 128), bf16),
    ]
    sems = [dma((steps,)), dma((steps,)), dma((steps, 6)), dma((steps, 6))]
    if not later:
        return buffers + sems
    more, more_sems = late_scratch(tiles, groups)
    return buffers + more + sems + more_sems


def late_scratch(tiles, groups):
    return [
        pltpu.VMEM((3, 3, 4, tiles, 16, 128), bf16),
        pltpu.VMEM((3, 3, tiles, 16, 128), bf16),
    ], [pltpu.SemaphoreType.DMA((groups, 3))] * 4


def product(left, right):
    return lax.dot_general(left, right, (((1,), (0,)), ((), ())), preferred_element_type=f32)


def against(left, right):
    return lax.dot_general(left, right, (((1,), (1,)), ((), ())), preferred_element_type=f32)


def crossed(left, right):
    return lax.dot_general(left, right, (((0,), (0,)), ((), ())), preferred_element_type=f32)


def block(i, width=256):
    return pl.ds(pl.multiple_of(i * width, width), width)


def adapter_products(sums, held, name, gain=None):
    slot = sums.slot(name)

    def put(spot, tile, zero, one):
        sums.put(name, spot, slot, tile, zero, one)

    if name == "ffn":
        for j, (left, right) in enumerate((("u2a", "ggate"), ("u2b", "gup"))):

            @pl.loop(0, 2)
            def _(i, j=j, left=left, right=right):
                value = crossed(held[left][...], held[right][:, block(i, 1024)])
                for b in range(4):
                    for h in range(8):
                        for t in range(2):
                            lanes = slice(256 * b + 128 * t, 256 * b + 128 * t + 128)
                            put(
                                (2 * i + b // 2, (b % 2) * 2 + h // 4, h % 4),
                                j * 2 + t,
                                value[32 * h : 32 * h + 16, lanes],
                                value[32 * h + 16 : 32 * h + 32, lanes],
                            )

    elif name == "mix":
        for j, right in enumerate(("gu1a", "gu1b", "gu2a", "gu2b")):
            value = crossed(held["n1" if j < 2 else "n2"][...], held[right][...])
            for r in range(40):
                rows = slice(16 * r, 16 * r + 16)
                put(split_spot(16 * j + r // 4), r % 4, value[rows, :128], value[rows, 128:])
        for k in range(3):
            if k < 2:
                value = crossed(held["u1a"][...], held["gqp"][:, 512 * k : 512 * k + 512])
            else:
                value = crossed(held["u1b"][...], held["gkvp"][...])
            for t in range(4):
                lanes = slice(128 * t, 128 * t + 128)
                for h in range(8):
                    put(
                        split_spot((4 * k + t) // 3 * 16 + 10 + (4 * k + t) % 3 * 2 + h // 4),
                        h % 4,
                        value[32 * h : 32 * h + 16, lanes],
                        value[32 * h + 16 : 32 * h + 32, lanes],
                    )
    elif name == "attn":
        value = crossed(held["o"][...], held["guo"][...])
        for q in range(64):
            rows = slice(16 * q, 16 * q + 16)
            put(split_spot(q), 0, value[rows, :128], value[rows, 128:])
    elif name == "down":

        @pl.loop(0, 2)
        def _(i):
            value = crossed(held["m"][:, block(i, 1024)], held["gud"][...])
            for b in range(4):
                for h in range(8):
                    row = 256 * b + 32 * h
                    for t in range(2):
                        lanes = slice(128 * t, 128 * t + 128)
                        put(
                            (2 * i + b // 2, (b % 2) * 2 + h // 4, h % 4),
                            t,
                            value[row : row + 16, lanes],
                            value[row + 16 : row + 32, lanes],
                        )

    else:
        for b, (left, right) in enumerate((("uo", "ga"), ("ud", "gf"))):
            value = crossed(held[left][...], held[right][...])
            for g in range(16):
                tiles = [value[16 * g : 16 * g + 16, 128 * t : 128 * t + 128] for t in range(5)]
                q = 2 * (16 * b + g)
                put(split_spot(q), 0, tiles[0], tiles[2])
                put(split_spot(q), 1, tiles[1], tiles[3])
                more = tiles[4] if gain is None or q else gain
                put(split_spot(q + 1), 0, tiles[4], more)
                put(split_spot(q + 1), 1, tiles[4], tiles[4])


WEIGHT_ITEMS = (
    (1, 3, 0, 256),
    (2, 3, 256, 640),
    (0, 4, 0, 128),
    (0, 5, 0, 128),
    (0, 0, 0, 640),
    (1, 1, 0, 640),
    (2, 2, 0, 640),
)

NAMES = (
    ("m", 2048),
    ("gf", 640),
    ("gud", 256),
    ("ud", 256),
    ("n2", 640),
    ("ggate", 2048),
    ("gup", 2048),
    ("gu2a", 256),
    ("gu2b", 256),
    ("u2a", 256),
    ("u2b", 256),
    ("o", 1024),
    ("ga", 640),
    ("guo", 256),
    ("uo", 256),
    ("n1", 640),
    ("gqp", 1024),
    ("gkvp", 512),
    ("gu1a", 256),
    ("gu1b", 256),
    ("u1a", 256),
    ("u1b", 256),
)
BOTH = ("m", "gf", "n2", "ggate", "gup", "o", "ga", "n1", "gqp", "gkvp")
ORDER = {name: i for i, (name, _) in enumerate(NAMES)}
ADAPTERS = ((4, 640, 256), (256, 1536), (2, 256, 2048), (1024, 256), (2048, 256), (2, 256, 640))


CURVE = 0.7978845608028654
CUBE = 0.044715


def block_kernel(*refs):
    (tokens, cotangent, doc_row, doc_source, mixing, gains) = refs[:6]
    shards = refs[6:12]
    adapters_in = refs[12:18]
    outs = refs[18:]
    block_out, token_grad, gain_tile, slab_out = outs[:4]
    kept_out = dict(zip((name for name, _ in NAMES), outs[4 : 4 + len(NAMES)]))
    rest = outs[4 + len(NAMES) :]
    kept = dict(zip((name for name, _ in NAMES), rest[: len(NAMES)]))
    rest = rest[len(NAMES) :]
    whole = rest[:6]
    both_piece = rest[6]
    a_in, a_qkv, a_ffn, a_attn, a_down, a_back = rest[7:13]
    (cosine, sine, mask, stream, hidden, q_rot, k_rot, value, probs, gate, up, grad, normed, gain_sum) = rest[13:27]
    kept_sem, adapter_sem, piece_sem = rest[27:30]
    gather = rest[30:35]
    slab_sem = rest[35]
    late = rest[36:]

    me = place()
    quarter = (me["z"] % 2) * 2 + me["c"]
    w_gate, w_up, w_down, w_both, w_kv, w_kv_last = whole

    fetch = [
        pltpu.make_async_copy(shards[0], both_piece.at[:32], piece_sem.at[0]),
        pltpu.make_async_copy(shards[2], both_piece.at[32:], piece_sem.at[1]),
    ]
    for copy in fetch:
        copy.start()
    adapter_names = ("in", "qkv", "ffn", "attn", "down", "back")
    waiting = {}

    def load(name, loop):
        i = adapter_names.index(name)
        target = (a_in, a_qkv, a_ffn, a_attn, a_down, a_back)[i]
        waiting[name] = pltpu.make_async_copy(adapters_in[i].at[loop], target, adapter_sem.at[i])
        waiting[name].start()

    def need(name):
        if name in waiting:
            waiting.pop(name).wait()

    for name in adapter_names:
        load(name, 0)
    greet(chip_peers(me) + [other_core(me)])
    for copy in fetch:
        copy.wait()
    own = pl.ds(pl.multiple_of(quarter * 16, 16), 16)
    sources = (shards[3].at[own], shards[4].at[own], shards[5].at[own], both_piece.at[own])
    lanes_of_kv = pl.ds(pl.multiple_of(quarter * 128, 128), 128)
    sources += (shards[1].at[:, lanes_of_kv], shards[1].at[:, pl.ds(512, 128)])
    items = []
    for i, (part, array, low, high) in enumerate(WEIGHT_ITEMS):

        def region(fixed, core, array=array, low=low, high=high):
            every = slice(None)
            zh, zl = every, every
            if isinstance(fixed.get("z"), slice):
                zh = fixed["z"].start // 2
            elif "z" in fixed:
                zh, zl = fixed["z"] // 2, fixed["z"] % 2
            return whole[array].at[
                fixed.get("x", every), zh, fixed.get("y", every), zl, core, :, pl.ds(low, high - low)
            ]

        items.append(
            Gather(me, i, ORDERS[part][::-1], sources[array].at[:, pl.ds(low, high - low)], region, gather)
        )
    for item in items:
        item.start()

    rows_of = lax.broadcasted_iota(jnp.int32, (256, 256), 0)
    columns_of = lax.broadcasted_iota(jnp.int32, (256, 256), 1)
    along = jnp.broadcast_to(doc_row[...], (256, 256))
    down = jnp.sum(jnp.where(rows_of == columns_of, along, 0), axis=1, keepdims=True)
    before = jnp.sum(jnp.where(along < down, 1, 0), axis=1, keepdims=True)
    mask[...] = jnp.where((along == down) & (columns_of <= rows_of), 1.0, 0.0)
    position = (lax.broadcasted_iota(jnp.int32, (256, 1), 0) - before).astype(f32)
    lanes = lax.broadcasted_iota(jnp.int32, (1, 128), 1).astype(f32)
    frequency = jnp.exp(lanes * (-2.0 / 256) * jnp.log(f32(rope_base)))
    angle = position * frequency
    cosine[...] = jnp.cos(angle)
    sine[...] = jnp.sin(angle)
    ratios = jnp.float32(0)
    for i in range(8):
        ratios += mixing[i].astype(f32)
    weight = jnp.zeros((256, 1), f32)
    for i in range(4):
        scale = mixing[doc_source[0, i]].astype(f32) * 8.0 / ratios
        weight = jnp.where(down == i, scale, weight)
    stream[0] = tokens[...].astype(f32)
    grad[...] = cotangent[...].astype(f32) * weight
    gain_sum[...] = jnp.zeros_like(gain_sum)
    soon, later = items[:4], items[4:]
    for item in items:
        item.arrive(0)
        item.spread(1)
    for item in soon:
        item.arrive(1)
        item.begin_ring()
    for item in later:
        item.arrive(1)
    for item in soon:
        item.turn_ring()
    for item in later:
        item.begin_ring()
    for item in soon:
        item.end_ring()

    def first_weights():
        for item in soon:
            item.finish()

    def turn_weights():
        for item in later:
            item.turn_ring()

    def rest_of_weights():
        for item in later:
            item.end_ring()
        for item in later:
            item.finish()

    def wide_rows(array, i):
        return array[i].reshape(512, 640)

    def q_rows(i):
        return w_both[i, :, :, 0].reshape(256, 640)

    def o_rows(i):
        return w_both[i, :, :, 1].reshape(256, 640)

    def kv_rows(i):
        return kv_of(slice(2 * i, 2 * i + 2), 256)

    def kv_of(x, rows):
        tiles = [w_kv[x, :, :, low, core].reshape(rows, 128) for low in range(2) for core in range(2)]
        return jnp.concatenate([*tiles, w_kv_last[x, :, :, 0, 0].reshape(rows, 128)], axis=1)

    def q_all():
        return w_both[:, :, :, 0].reshape(1024, 640)

    def o_all():
        return w_both[:, :, :, 1].reshape(1024, 640)

    def kv_all():
        return kv_of(slice(0, 4), 512)

    def all_rows(array):
        return array[...].reshape(2048, 640)

    scale = 256 ** (-0.5)

    def rotated(first, second, sign):
        c = cosine[...]
        s = sine[...] * sign
        return first * c - second * s, second * c + first * s

    def out_of(name, loop):
        target = kept_out[name].at[loop] if name in BOTH else kept_out[name]
        return pltpu.make_async_copy(kept[name], target, kept_sem.at[ORDER[name]])

    leaving = set()

    def to_hbm(names, loop):
        for name in names:
            if loop == 0 or name in BOTH:
                out_of(name, loop).start()
                leaving.add((name, loop))

    def drained(names, loop):
        for name in names:
            if (name, loop) in leaving:
                leaving.discard((name, loop))
                out_of(name, loop).wait()

    def norm(source, gain, target):
        for i in range(4):
            rows = slice(64 * i, 64 * i + 64)
            x = source[rows, :]
            inverse = lax.rsqrt(jnp.mean(x * x, axis=-1, keepdims=True) + eps)
            target[rows, :] = (x * inverse * gain).astype(bf16)

    first_names = ("n1", "u1a", "u1b", "o", "uo")
    second_names = ("n2", "u2a", "u2b", "m", "ud")

    def forward(loop):
        drained(first_names, 0)
        need("in")
        norm(stream.at[loop], gains[0:1, :], kept["n1"])
        kept["u1a"][...] = product(kept["n1"][...], a_in[0]).astype(bf16)
        kept["u1b"][...] = product(kept["n1"][...], a_in[1]).astype(bf16)

        need("qkv")
        if loop == 0:
            first_weights()
        k_pre = against(kept["n1"][...], kv_rows(0)) + product(kept["u1b"][...], a_qkv[:, 1024:1280])
        first, second = rotated(k_pre[:, :128], k_pre[:, 128:], 1.0)
        k_rot[loop, :, :128] = first.astype(bf16)
        k_rot[loop, :, 128:] = second.astype(bf16)
        value[loop] = (
            against(kept["n1"][...], kv_rows(1)) + product(kept["u1b"][...], a_qkv[:, 1280:1536])
        ).astype(bf16)

        if loop == 0:
            turn_weights()
        for h in range(4):
            at = slice(256 * h, 256 * h + 256)
            q_pre = against(kept["n1"][...], q_rows(h)) + product(kept["u1a"][...], a_qkv[:, at])
            first, second = rotated(q_pre[:, :128], q_pre[:, 128:], 1.0)
            q_rot[loop, h, :, :128] = first.astype(bf16)
            q_rot[loop, h, :, 128:] = second.astype(bf16)
            scores = against(q_rot[loop, h], k_rot[loop]) * scale
            scores = jnp.where(mask[...] > 0.5, scores, masked)
            expo = jnp.exp(scores - jnp.max(scores, axis=-1, keepdims=True))
            p = expo * (1.0 / jnp.sum(expo, axis=-1, keepdims=True))
            probs[loop, h] = p
            kept["o"][:, at] = product(p.astype(bf16), value[loop]).astype(bf16)

        if loop == 0:
            load("qkv", 1)
        need("attn")
        need("back")
        kept["uo"][...] = product(kept["o"][...], a_attn[...]).astype(bf16)
        hidden[loop] = stream[loop] + (
            product(kept["o"][...], o_all()) + product(kept["uo"][...], a_back[0])
        )
        to_hbm(first_names, loop)
        if loop == 0:
            load("attn", 1)
        drained(second_names, 0)
        if loop == 0:
            rest_of_weights()
        norm(hidden.at[loop], gains[1:2, :], kept["n2"])
        kept["u2a"][...] = product(kept["n2"][...], a_in[2]).astype(bf16)
        kept["u2b"][...] = product(kept["n2"][...], a_in[3]).astype(bf16)
        if loop == 0:
            load("in", 1)
        need("ffn")

        for i in range(4):
            at = slice(512 * i, 512 * i + 512)
            g = against(kept["n2"][...], wide_rows(w_gate, i)) + product(
                kept["u2a"][...], a_ffn[0, :, at]
            )
            u = against(kept["n2"][...], wide_rows(w_up, i)) + product(
                kept["u2b"][...], a_ffn[1, :, at]
            )
            gate[loop, :, at] = g
            up[loop, :, at] = u
            bend = jnp.tanh(CURVE * (g + CUBE * g * g * g))
            kept["m"][:, at] = (0.5 * g * (1.0 + bend) * u).astype(bf16)

        if loop == 0:
            load("ffn", 1)
        need("down")
        kept["ud"][...] = product(kept["m"][...], a_down[...]).astype(bf16)
        stream[loop + 1] = hidden[loop] + (
            product(kept["m"][...], all_rows(w_down)) + product(kept["ud"][...], a_back[1])
        )
        to_hbm(second_names, loop)
        if loop == 0:
            load("down", 1)
            load("back", 1)

    def norm_back(source, which):
        gain = gains[which : which + 1, :]

        for i in range(4):
            rows = slice(64 * i, 64 * i + 64)
            x = source[rows, :]
            g = normed[rows, :]
            inverse = lax.rsqrt(jnp.mean(x * x, axis=-1, keepdims=True) + eps)
            scaled = g * gain
            step = inverse * (
                scaled - x * inverse * inverse * jnp.mean(scaled * x, axis=-1, keepdims=True)
            )
            grad[rows, :] = grad[rows, :] + step
            gain_sum[which : which + 1, :] += jnp.sum(g * x * inverse, axis=0, keepdims=True)

    ffn_names = ("gf", "gud", "ggate", "gup", "gu2a", "gu2b")
    attention_names = ("ga", "guo", "gqp", "gkvp", "gu1a", "gu1b")

    def backward_ffn(loop):
        drained(ffn_names, 1)
        need("back")
        need("down")
        kept["gf"][...] = grad[...].astype(bf16)
        kept["gud"][...] = against(kept["gf"][...], a_back[1]).astype(bf16)

        for i in range(4):
            at = slice(512 * i, 512 * i + 512)
            gm = against(kept["gf"][...], wide_rows(w_down, i)) + against(
                kept["gud"][...], a_down[at, :]
            )
            g = gate[loop, :, at]
            u = up[loop, :, at]
            square = g * g
            bend = jnp.tanh(CURVE * (g + CUBE * g * square))
            half = 0.5 * (1.0 + bend)
            slope = half + 0.5 * g * (1.0 - bend * bend) * (CURVE * (1.0 + 3.0 * CUBE * square))
            kept["ggate"][:, at] = (gm * u * slope).astype(bf16)
            kept["gup"][:, at] = (gm * (g * half)).astype(bf16)

        need("ffn")
        kept["gu2a"][...] = against(kept["ggate"][...], a_ffn[0]).astype(bf16)
        kept["gu2b"][...] = against(kept["gup"][...], a_ffn[1]).astype(bf16)
        to_hbm(ffn_names, loop)

    def backward_hidden(loop):
        need("in")
        normed[...] = (
            product(kept["ggate"][...], all_rows(w_gate))
            + product(kept["gup"][...], all_rows(w_up))
            + against(kept["gu2a"][...], a_in[2])
            + against(kept["gu2b"][...], a_in[3])
        )
        norm_back(hidden.at[loop], 1)

    def backward_attention(loop):
        drained(attention_names, 1)
        need("attn")
        kept["ga"][...] = grad[...].astype(bf16)
        kept["guo"][...] = against(kept["ga"][...], a_back[0]).astype(bf16)

        def head(h, carry):
            grad_key, grad_value = carry
            at = slice(256 * h, 256 * h + 256)
            go = (
                against(kept["ga"][...], o_rows(h)) + against(kept["guo"][...], a_attn[at, :])
            ).astype(bf16)
            p = probs[loop, h]
            gp = against(go, value[loop])
            gs = (p * (gp - jnp.sum(p * gp, axis=-1, keepdims=True))).astype(bf16)
            gq = product(gs, k_rot[loop]) * scale
            first, second = rotated(gq[:, :128], gq[:, 128:], -1.0)
            kept["gqp"][:, 256 * h : 256 * h + 128] = first.astype(bf16)
            kept["gqp"][:, 256 * h + 128 : 256 * h + 256] = second.astype(bf16)
            grad_key += crossed(gs, q_rot[loop, h])
            grad_value += crossed(p.astype(bf16), go)
            return grad_key, grad_value

        sums_of_heads = (jnp.zeros((256, 256), f32), jnp.zeros((256, 256), f32))
        for h in range(4):
            sums_of_heads = head(h, sums_of_heads)
        grad_key, grad_value = sums_of_heads
        grad_key = grad_key * scale
        first, second = rotated(grad_key[:, :128], grad_key[:, 128:], -1.0)
        kept["gkvp"][:, :128] = first.astype(bf16)
        kept["gkvp"][:, 128:256] = second.astype(bf16)
        kept["gkvp"][:, 256:] = grad_value.astype(bf16)
        need("qkv")
        kept["gu1a"][...] = against(kept["gqp"][...], a_qkv[:, :1024]).astype(bf16)
        kept["gu1b"][...] = against(kept["gkvp"][...], a_qkv[:, 1024:]).astype(bf16)
        to_hbm(attention_names, loop)

    def backward_stream(loop):
        normed[...] = (
            product(kept["gqp"][...], q_all())
            + product(kept["gkvp"][...], kv_all())
            + against(kept["gu1a"][...], a_in[0])
            + against(kept["gu1b"][...], a_in[1])
        )
        norm_back(stream.at[loop], 0)

    sums = Sums(me, LATE_STEPS, ADAPTER_GROUPS, late[:4], late[4:])

    def summing(name):
        adapter_products(sums, kept, name)
        sums.send_pair(LATE_STEPS.index(name))

    forward(0)
    forward(1)
    block_out[...] = stream[2].astype(bf16)
    backward_ffn(1)
    summing("ffn")
    summing("down")
    backward_hidden(1)
    sums.combine(0)
    backward_attention(1)
    sums.combine(1)
    summing("mix")
    sums.relay(0)
    backward_stream(1)
    for name in ("back", "down", "ffn", "in", "attn", "qkv"):
        load(name, 0)
    sums.combine(2)
    summing("attn")
    sums.relay(1)
    summing("back")
    backward_ffn(0)
    sums.combine(3)
    sums.combine(4)
    sums.relay(2)
    backward_hidden(0)
    sums.relay(3)
    sums.relay(4)
    backward_attention(0)
    backward_stream(0)
    token_grad[...] = grad[...]
    gain_tile[...] = jnp.zeros_like(gain_tile)
    for i in range(2):
        for t in range(5):
            gain_tile[5 * i + t : 5 * i + t + 1, :] = gain_sum[i : i + 1, 128 * t : 128 * t + 128]
    for g in range(3):
        sums.first_sum(g)
    slab_copies = []
    for part in range(3):
        slab_copies.append(pltpu.make_async_copy(sums.slab(part), slab_out.at[part], slab_sem.at[part]))
        slab_copies[-1].start()
    sums.finish()
    for item in items:
        item.close()
    for copy in slab_copies:
        copy.wait()
    for names in (first_names, second_names, ffn_names, attention_names):
        for loop in range(2):
            drained(names, loop)


def block_pass(tokens, cotangent, doc_ids, doc_source, mixing, norm_gains, shards, adapters):
    vmem = pl.BlockSpec(memory_space=pltpu.VMEM)
    smem = pl.BlockSpec(memory_space=pltpu.SMEM)
    anywhere = pl.BlockSpec(memory_space=pl.ANY)
    dma = pltpu.SemaphoreType.DMA
    return pl.pallas_call(
        block_kernel,
        out_shape=[
            jax.ShapeDtypeStruct((256, 640), bf16),
            jax.ShapeDtypeStruct((256, 640), f32),
            jax.ShapeDtypeStruct((16, 128), f32),
            jax.ShapeDtypeStruct((3, 4, 4, 5, 16, 128), bf16),
        ]
        + [
            jax.ShapeDtypeStruct((2, 256, width) if name in BOTH else (256, width), bf16)
            for name, width in NAMES
        ],
        in_specs=[vmem, vmem, vmem, smem, smem, vmem] + [anywhere] * 12,
        out_specs=[vmem] * 3 + [anywhere] * (1 + len(NAMES)),
        scratch_shapes=[pltpu.VMEM((256, width), bf16) for _, width in NAMES]
        + [pltpu.VMEM((4, 2, 4, 2, 2, 16, 640), bf16)] * 4
        + [pltpu.VMEM((4, 2, 4, 2, 2, 16, 128), bf16)] * 2
        + [pltpu.VMEM((64, 640), bf16)]
        + [pltpu.VMEM(shape, bf16) for shape in ADAPTERS]
        + [
            pltpu.VMEM((256, 128), f32),
            pltpu.VMEM((256, 128), f32),
            pltpu.VMEM((256, 256), f32),
            pltpu.VMEM((3, 256, 640), f32),
            pltpu.VMEM((2, 256, 640), f32),
            pltpu.VMEM((2, 4, 256, 256), bf16),
            pltpu.VMEM((2, 256, 256), bf16),
            pltpu.VMEM((2, 256, 256), bf16),
            pltpu.VMEM((2, 4, 256, 256), f32),
            pltpu.VMEM((2, 256, 2048), f32),
            pltpu.VMEM((2, 256, 2048), f32),
            pltpu.VMEM((256, 640), f32),
            pltpu.VMEM((256, 640), f32),
            pltpu.VMEM((2, 640), f32),
            dma((len(NAMES),)),
            dma((6,)),
            dma((2,)),
        ]
        + gather_sems(len(WEIGHT_ITEMS))
        + [dma((3,))]
        + sums_scratch(5, 4, len(LATE_STEPS), len(ADAPTER_GROUPS), later=False),
        compiler_params=pltpu.CompilerParams(
            collective_id=1, has_side_effects=True, vmem_limit_bytes=60 * 2**20
        ),
        name="block",
    )(tokens, cotangent, doc_ids, doc_source, mixing, norm_gains, *shards, *adapters)


NEEDS = {
    "attn": ("o", "guo"),
    "mix": ("n1", "n2", "gu1a", "gu1b", "gu2a", "gu2b", "u1a", "gqp", "u1b", "gkvp"),
    "ffn": ("u2a", "ggate", "u2b", "gup"),
    "down": ("m", "gud"),
    "back": ("uo", "ga", "ud", "gf"),
}
LOAD_ORDER = tuple(name for step in STEPS[:5] for name in NEEDS[step])
SHARED_OPERANDS = {
    "gate": ("ggate", "n2"),
    "up": ("gup", "n2"),
    "wdown": ("m", "gf"),
    "q": ("gqp", "n1"),
    "o": ("o", "ga"),
    "kv": ("gkvp", "n1"),
}


def shared_products(sums, held, name):
    slot = sums.slot(name)
    order = ORDERS[CHUNKS[name][0]]
    left, right = (held[operand] for operand in SHARED_OPERANDS[name])
    right = right[...].reshape(512, 640)

    if name in ("gate", "up", "wdown"):

        @pl.loop(0, 2)
        def _(i):
            value = crossed(left[:, :, block(i, 1024)].reshape(512, 1024), right)
            for x in range(2):
                for high in range(2):
                    for y in range(4):
                        for low in range(2):
                            row = 512 * x + 256 * high + 64 * y + 32 * low
                            for t in range(5):
                                lanes = slice(128 * t, 128 * t + 128)
                                sums.put(
                                    name,
                                    chip_spot(order, 2 * i + x, y, high * 2 + low),
                                    slot,
                                    t,
                                    value[row : row + 16, lanes],
                                    value[row + 16 : row + 32, lanes],
                                )

    elif name in ("q", "o"):
        value = crossed(left[...].reshape(512, 1024), right)
        for x in range(4):
            for high in range(2):
                for y in range(4):
                    for low in range(2):
                        row = 256 * x + 128 * high + 32 * y + 16 * low
                        tiles = [value[row : row + 16, 128 * t : 128 * t + 128] for t in range(5)]
                        for t in range(3):
                            sums.put(
                                name,
                                chip_spot(order, x, y, high * 2 + low),
                                slot,
                                t,
                                tiles[t],
                                tiles[min(t + 3, 4)],
                            )
    else:
        value = crossed(left[...].reshape(512, 512), right)
        for k in range(32):
            tiles = [value[16 * k : 16 * k + 16, 128 * t : 128 * t + 128] for t in range(5)]
            for low, ends in enumerate((((0, 3), (1, 3)), ((2, 4), (2, 4)))):
                for t, (zero, one) in enumerate(ends):
                    sums.put(
                        name,
                        chip_spot(order, k // 8, k % 4, (k // 4) % 2 * 2 + low),
                        slot,
                        t,
                        tiles[zero],
                        tiles[one],
                    )


def grads_kernel(*refs):
    count = len(NAMES)
    given = dict(zip((name for name, _ in NAMES), refs[:count]))
    gain_ref, slab_ref = refs[count : count + 2]
    all_ref, share_ref = refs[count + 2 : count + 4]
    rest = refs[count + 4 :]
    held = dict(zip((name for name, _ in NAMES), rest[:count]))
    load_sem, share_send, share_recv, share_local = rest[count : count + 4]
    gather = rest[count + 4 : count + 9]
    me = place()
    slab, slab_sem = rest[count + 9 : count + 11]
    after = rest[count + 11 :]
    late_sums = LateSums(me, ADAPTER_GROUPS, slab, after[:2], after[2:6])
    sums = Sums(me, STEPS, GROUPS, after[6:12], after[12:])

    slab_copy = pltpu.make_async_copy(slab_ref, slab, slab_sem)
    slab_copy.start()

    loads = {}
    for i, name in enumerate(LOAD_ORDER):
        loads[name] = pltpu.make_async_copy(given[name], held[name], load_sem.at[i])
        loads[name].start()
    greet(chip_peers(me) + [other_core(me), other_core(other_low(me))])

    def spreading(loop, g, piece):
        part, first, tiles = GROUPS[g]
        order = ORDERS[part]

        def region(fixed, core):
            spot = tuple(fixed.get(axis, slice(None)) for axis in order)
            return all_ref.at[(loop, core, part, *spot, pl.ds(first, tiles))]

        item = Gather(me, loop * 3 + part, order[::-1], piece, region, gather)
        item.start()
        return item

    def near(items):
        for item in items:
            item.arrive(0)
            item.spread(1)

    def ring(items):
        for item in items:
            item.arrive(1)
            item.begin_ring()

    def turn(items):
        for item in items:
            item.turn_ring()

    def end(items):
        for item in items:
            item.end_ring()

    shares = []

    def share(g):
        part, first, tiles = GROUPS[g]
        mine = sums.last(g)
        low = me["z"] % 2

        def spot(low, core):
            return share_ref.at[low * 2 + core, part, pl.ds(0, tiles)]

        local = pltpu.make_async_copy(mine, spot(low, me["c"]), share_local.at[part])
        local.start()
        shares.append(local.wait)
        for k, peer in enumerate(
            (other_low(me), other_core(me), other_core(other_low(me)))
        ):
            copy = sending(
                mine, spot(low, me["c"]), share_send.at[part, k], share_recv.at[part, k], peer
            )
            copy.start()
            sums.sent.append(copy)
            there = spot(peer["z"] % 2, peer["c"])
            shares.append(
                sending(there, there, share_send.at[part, k], share_recv.at[part, k], peer).wait_recv
            )

    def summing(k):
        name = STEPS[k]
        if name in NEEDS:
            for operand in NEEDS[name]:
                loads[operand].wait()
            first_loop = {n: held[n].at[0] if n in BOTH else held[n] for n in held}
            adapter_products(sums, first_loop, name, gain_ref[...])
        else:
            shared_products(sums, held, name)
        sums.send_pair(k)

    def each(task, groups):
        for g in groups:
            task(g)

    slab_copy.wait()
    each(late_sums.send_second, range(3))
    late, early = [], []
    adapter_groups, shared_groups = range(3), range(3, 6)
    summing(0)
    summing(1)
    summing(2)
    summing(3)
    sums.combine(0)
    summing(4)
    each(late_sums.third, adapter_groups)
    sums.combine(2)
    sums.combine(1)
    sums.combine(3)
    sums.combine(4)
    late.extend(spreading(1, g, late_sums.last(g)) for g in adapter_groups)
    summing(5)
    summing(6)
    sums.relay(0)
    summing(7)
    sums.relay(2)
    sums.relay(4)
    sums.relay(3)
    sums.relay(1)
    summing(8)
    near(late)
    sums.combine(6)
    each(sums.second, adapter_groups)
    sums.combine(7)
    ring(late)
    sums.combine(5)
    summing(9)
    summing(10)
    each(sums.third, adapter_groups)
    sums.combine(8)
    sums.combine(9)
    sums.combine(10)
    early.extend(spreading(0, g, sums.last(g)) for g in adapter_groups)
    sums.relay(8)
    sums.relay(9)
    sums.relay(7)
    sums.relay(10)
    sums.relay(6)
    sums.relay(5)
    turn(late)
    near(early)
    each(sums.second, shared_groups)
    ring(early)
    each(sums.third, shared_groups)
    turn(early)
    end(late)
    each(share, shared_groups)
    end(early)
    for item in late + early:
        item.finish()
    for item in late + early:
        item.close()
    sums.finish()
    late_sums.finish()
    for wait in shares:
        wait()


def summed_gradients(kept, gain_tile, slab):
    anywhere = pl.BlockSpec(memory_space=pl.ANY)
    vmem = pl.BlockSpec(memory_space=pltpu.VMEM)
    dma = pltpu.SemaphoreType.DMA
    more, more_sems = late_scratch(5, len(ADAPTER_GROUPS))
    return pl.pallas_call(
        grads_kernel,
        out_shape=[
            jax.ShapeDtypeStruct((2, 2, 3, 4, 4, 4, 5, 16, 128), bf16),
            jax.ShapeDtypeStruct((4, 3, 8, 16, 128), bf16),
        ],
        in_specs=[anywhere] * len(NAMES) + [vmem, anywhere],
        out_specs=[anywhere] * 2,
        scratch_shapes=[
            pltpu.VMEM((2, 256, width) if name in BOTH else (256, width), bf16)
            for name, width in NAMES
        ]
        + [
            dma((len(NAMES),)),
            dma((3, 3)),
            dma((3, 3)),
            dma((3,)),
        ]
        + gather_sems(6)
        + [pltpu.VMEM((3, 4, 4, 5, 16, 128), bf16), dma]
        + more
        + more_sems
        + sums_scratch(12, 5, len(STEPS), len(GROUPS)),
        compiler_params=pltpu.CompilerParams(
            collective_id=2, has_side_effects=True, vmem_limit_bytes=60 * 2**20
        ),
        name="grads",
    )(*kept, gain_tile, slab)


def unpack_kernel(all_ref, share_ref, *outs):
    (gain, wq, wkv, wo, wgate, wup, wdown, w_in, w_qkv, w_ffn, w_attn, w_down, w_back) = outs
    loop, step = pl.program_id(0), pl.program_id(1)

    for q in range(16):
        for core in range(2):
            row = slice(32 * (q % 8) + 16 * core, 32 * (q % 8) + 16 * core + 16)
            for j in range(2):
                for t in range(2):
                    lanes = slice(256 * (q // 8) + 128 * t, 256 * (q // 8) + 128 * t + 128)
                    w_ffn[0, j, row, lanes] = all_ref[0, core, 0, q, 2 * j + t].astype(f32)
            rows = slice(16 * q, 16 * q + 16)
            w_attn[0, rows, 128 * core : 128 * core + 128] = all_ref[0, core, 2, q, 0].astype(f32)
            for t in range(2):
                w_down[0, 32 * q + 16 * core : 32 * q + 16 * core + 16, 128 * t : 128 * t + 128] = all_ref[
                    0, core, 2, q, 1 + t
                ].astype(f32)
    for g in range(8):
        rows = slice(16 * g, 16 * g + 16)
        for t, (more, core, tile) in enumerate(((0, 0, 3), (0, 0, 4), (0, 1, 3), (0, 1, 4), (1, 0, 3))):
            w_back[0, 0, rows, 128 * t : 128 * t + 128] = all_ref[0, core, 2, 2 * g + more, tile].astype(f32)
    for core in range(2):
        for r in range(40):
            w_in[0, 0, 16 * r : 16 * r + 16, 128 * core : 128 * core + 128] = all_ref[
                0, core, 1, r // 4, r % 4
            ].astype(f32)
        for t in range(3):
            for h in range(8):
                w_qkv[0, 32 * h + 16 * core : 32 * h + 16 * core + 16, 128 * t : 128 * t + 128] = all_ref[
                    0, core, 1, 10 + 2 * t + h // 4, h % 4
                ].astype(f32)

    @pl.when((loop == 0) & (step == 0))
    def _():
        tile = all_ref[0, 1, 2, 1, 3].astype(f32)
        for i in range(2):
            for t in range(5):
                gain[i : i + 1, 128 * t : 128 * t + 128] = tile[5 * i + t : 5 * i + t + 1, :]

        def mine(low, core, part, t):
            return share_ref[low * 2 + core, part, t].astype(f32)

        def wide(part, first):
            rows = []
            for low in range(2):
                for core in range(2):
                    rows.append(jnp.concatenate([mine(low, core, part, first + t) for t in range(5)], axis=1))
            return jnp.concatenate(rows, axis=0)

        def narrow(part, first):
            rows = []
            for low in range(2):
                tiles = [mine(low, 0, part, first + t) for t in range(3)]
                tiles += [mine(low, 1, part, first + t) for t in range(2)]
                rows.append(jnp.concatenate(tiles, axis=1))
            return jnp.concatenate(rows, axis=0)

        wgate[...] = wide(0, 0)
        wup[...] = wide(1, 0)
        wdown[...] = wide(2, 0)
        wq[...] = narrow(0, 5)
        wo[...] = narrow(1, 5)
        kv = [mine(0, 0, 2, 5), mine(0, 0, 2, 6), mine(1, 0, 2, 5), mine(0, 1, 2, 5), mine(1, 1, 2, 5)]
        wkv[...] = jnp.concatenate(kv, axis=1)


def unpacked(everything, shares):
    def whole(*shape):
        return jax.ShapeDtypeStruct(shape, f32), pl.BlockSpec(shape, lambda l, s: (0,) * len(shape))

    def cut(shape, size, index):
        return jax.ShapeDtypeStruct(shape, f32), pl.BlockSpec(size, index)

    outs = [
        whole(2, 640),
        whole(32, 640),
        whole(16, 640),
        whole(32, 640),
        whole(64, 640),
        whole(64, 640),
        whole(64, 640),
        cut((2, 4, 640, 256), (1, 1, 640, 256), lambda l, s: (l, s, 0, 0)),
        cut((2, 256, 1536), (1, 256, 384), lambda l, s: (l, 0, s)),
        cut((2, 2, 256, 2048), (1, 2, 256, 512), lambda l, s: (l, 0, 0, s)),
        cut((2, 1024, 256), (1, 256, 256), lambda l, s: (l, s, 0)),
        cut((2, 2048, 256), (1, 512, 256), lambda l, s: (l, s, 0)),
        cut((2, 2, 256, 640), (1, 1, 128, 640), lambda l, s: (l, s // 2, s % 2, 0)),
    ]
    everything = everything.reshape(2, 2, 3, 64, 5, 16, 128)
    return pl.pallas_call(
        unpack_kernel,
        grid=(2, 4),
        out_shape=[shape for shape, _ in outs],
        in_specs=[
            pl.BlockSpec((1, 2, 3, 16, 5, 16, 128), lambda l, s: (l, 0, 0, s, 0, 0, 0)),
            pl.BlockSpec((4, 3, 8, 16, 128), lambda l, s: (0, 0, 0, 0, 0)),
        ],
        out_specs=[spec for _, spec in outs],
        compiler_params=pltpu.CompilerParams(vmem_limit_bytes=60 * 2**20),
        name="unpack",
    )(everything, shares)


def body(
    tokens,
    cotangent,
    doc_ids,
    doc_source,
    mixing,
    norm_gains,
    wq,
    wkv,
    wo,
    wgate,
    wup,
    wdown,
    *adapters,
):
    shards = (wq.T, wkv.T, wo, wgate.T, wup.T, wdown)
    block_out, token_grad, gain_tile, slab, *kept = block_pass(
        tokens, cotangent, doc_ids, doc_source, mixing, norm_gains, shards, adapters
    )
    everything, shares = summed_gradients(kept, gain_tile, slab)
    gain, wq_sum, wkv_sum, wo_sum, wgate_sum, wup_sum, wdown_sum, *sums = unpacked(everything, shares)
    return (
        block_out,
        token_grad,
        gain,
        wq_sum.T,
        wkv_sum.T,
        wo_sum,
        wgate_sum.T,
        wup_sum.T,
        wdown_sum,
        *sums,
    )


def solution(mesh):
    rows = P(("loop", "dp"), None)
    columns = P(None, "dp")
    placed = (
        *(rows,) * 4,
        P(),
        P(),
        columns,
        columns,
        P("dp", None),
        columns,
        columns,
        P("dp", None),
        *(P(),) * 6,
    )
    return jax.shard_map(
        body,
        mesh=mesh,
        in_specs=placed,
        out_specs=(
            rows,
            rows,
            P(),
            columns,
            columns,
            P("dp", None),
            columns,
            columns,
            P("dp", None),
            *(P(),) * 6,
        ),
        check_vma=False,
    )
```

```python
import jax
import jax.numpy as jnp
from jax import lax
from jax.experimental import pallas as pl
from jax.experimental.pallas import tpu as pltpu
from jax.sharding import PartitionSpec as P

eps = 1e-06
rope_base = 10000.0
masked = -1e30
MESH = pl.DeviceIdType.MESH
bf16 = jnp.bfloat16
f32 = jnp.float32

ORDERS = (("x", "y", "z"), ("y", "z", "x"), ("z", "x", "y"))

ADAPTER_CHUNKS = {
    "ffn": (0, 0, 4),
    "mix": (1, 0, 4),
    "attn": (2, 0, 1),
    "down": (2, 1, 2),
    "back": (2, 3, 2),
}
SHARED_CHUNKS = {
    "gate": (0, 4, 5),
    "q": (0, 9, 3),
    "up": (1, 4, 5),
    "o": (1, 9, 3),
    "wdown": (2, 5, 5),
    "kv": (2, 10, 2),
}
CHUNKS = {**ADAPTER_CHUNKS, **SHARED_CHUNKS}
ADAPTER_GROUPS = ((0, 0, 4), (1, 0, 4), (2, 0, 5))
GROUPS = ADAPTER_GROUPS + ((0, 4, 8), (1, 4, 8), (2, 5, 7))
LATE_STEPS = ("ffn", "down", "mix", "attn", "back")
STEPS = ("attn", "mix", "ffn", "down", "back", "q", "o", "kv", "wdown", "gate", "up")

HALVES = (slice(0, 2), slice(2, 4))


def place():
    lo = lax.axis_index("loop")
    dp = lax.axis_index("dp")
    return {"x": dp // 8, "y": dp % 4, "z": (dp // 4) % 2 * 2 + lo // 2, "c": lo % 2}


def device(at):
    return ((at["z"] % 2) * 2 + at["c"], at["x"] * 8 + (at["z"] // 2) * 4 + at["y"])


def moved(me, axis, by):
    return {**me, axis: (me[axis] + by) % 4}


def other_core(me):
    return {**me, "c": 1 - me["c"]}


def other_low(me):
    return {**me, "z": me["z"] + 1 - 2 * (me["z"] % 2)}


def greet(peers):
    barrier = pltpu.get_barrier_semaphore()
    for peer in peers:
        pl.semaphore_signal(barrier, inc=1, device_id=device(peer), device_id_type=MESH)
    pl.semaphore_wait(barrier, len(peers))


def sending(src, dst, send, recv, peer):
    return pltpu.make_async_remote_copy(
        src_ref=src,
        dst_ref=dst,
        send_sem=send,
        recv_sem=recv,
        device_id=device(peer),
        device_id_type=MESH,
    )


class Gather:
    def __init__(self, me, index, order, piece, region, sems):
        self.me, self.index, self.order, self.piece, self.region = me, index, order, piece, region
        self.send, self.recv, self.core_send, self.core_recv, self.local = sems
        self.sent = []

    def spot(self, stage, by):
        fixed = {axis: self.me[axis] for axis in self.order[stage:]}
        fixed[self.order[stage]] = (self.me[self.order[stage]] + by) % 4
        return fixed

    def to_core(self, source, fixed):
        i, me = self.index, self.me
        sending(
            source,
            self.region(fixed, me["c"]),
            self.core_send.at[i],
            self.core_recv.at[i],
            other_core(me),
        ).start()

    def half(self, by, which):
        return {**self.spot(2, by), self.order[0]: HALVES[which]}

    def pass_on(self, by, which, step, slot):
        here = self.region(self.half(by, which), self.me["c"])
        copy = sending(
            here,
            here,
            self.send.at[self.index, 6 + slot],
            self.recv.at[self.index, 6 + slot],
            moved(self.me, self.order[2], step),
        )
        copy.start()
        self.sent.append(copy)

    def take(self, by, which, slot):
        fixed = self.half(by, which)
        there = self.region(fixed, self.me["c"])
        sending(
            there,
            there,
            self.send.at[self.index, 6 + slot],
            self.recv.at[self.index, 6 + slot],
            moved(self.me, self.order[2], by),
        ).wait_recv()
        return there, fixed

    def begin_ring(self):
        self.pass_on(0, 0, 1, 0)
        self.pass_on(0, 1, 3, 3)
        self.pass_on(0, 1, 1, 1)
        self.pass_on(0, 0, 3, 2)

    def turn_ring(self):
        left = self.take(3, 0, 0)
        self.pass_on(3, 0, 1, 4)
        right = self.take(1, 1, 3)
        self.pass_on(1, 1, 3, 5)
        self.to_core(*left)
        self.to_core(*right)

    def end_ring(self):
        self.to_core(*self.take(3, 1, 1))
        self.to_core(*self.take(1, 0, 2))
        self.to_core(*self.take(2, 0, 4))
        self.to_core(*self.take(2, 1, 5))

    def start(self):
        fixed = self.spot(0, 0)
        self.kept = pltpu.make_async_copy(
            self.piece, self.region(fixed, self.me["c"]), self.local.at[self.index]
        )
        self.kept.start()
        self.spread(0, self.piece)
        self.to_core(self.piece, fixed)

    def spread(self, stage, source=None):
        if stage == 1:
            self.kept.wait()
        here = self.region(self.spot(stage, 0), self.me["c"])
        for by in (2, 1, 3):
            copy = sending(
                here if source is None else source,
                here,
                self.send.at[self.index, 3 * stage + by - 1],
                self.recv.at[self.index, 3 * stage + 3 - by],
                moved(self.me, self.order[stage], by),
            )
            copy.start()
            self.sent.append(copy)

    def arrive(self, stage):
        for by in (1, 3, 2):
            fixed = self.spot(stage, by)
            there = self.region(fixed, self.me["c"])
            sending(
                there,
                there,
                self.send.at[self.index, 3 * stage + by - 1],
                self.recv.at[self.index, 3 * stage + by - 1],
                moved(self.me, self.order[stage], by),
            ).wait_recv()
            self.to_core(there, fixed)

    def finish(self):
        i, me = self.index, self.me
        theirs = self.region({}, 1 - me["c"])
        sending(theirs, theirs, self.core_send.at[i], self.core_recv.at[i], other_core(me)).wait_recv()

    def close(self):
        i, me = self.index, self.me
        mine = self.region({}, me["c"])
        sending(mine, mine, self.core_send.at[i], self.core_recv.at[i], other_core(me)).wait_send()
        for copy in self.sent:
            copy.wait_send()


def gather_sems(items):
    return [
        pltpu.SemaphoreType.DMA((items, 12)),
        pltpu.SemaphoreType.DMA((items, 12)),
        pltpu.SemaphoreType.DMA((items,)),
        pltpu.SemaphoreType.DMA((items,)),
        pltpu.SemaphoreType.DMA((items,)),
    ]


def chip_peers(me):
    return [moved(me, axis, by) for axis in ("x", "y", "z") for by in (1, 2, 3)]


def chip_spot(order, x, y, z):
    at = {"x": x, "y": y, "z": z}
    return tuple(at[axis] for axis in order)


def split_spot(q):
    return (q // 16, (q // 4) % 4, q % 4)


class Sums:
    def __init__(self, me, steps, groups, buffers, sems):
        self.me, self.steps, self.groups = me, steps, groups
        self.total, self.from_core, self.to_core, self.got_one = buffers[:4]
        self.pair_send, self.pair_recv, self.one_send, self.one_recv = sems[:4]
        if len(sems) > 4:
            self.got_two, self.got_three = buffers[4:]
            self.two_send, self.two_recv, self.three_send, self.three_recv = sems[4:]
        self.pair = []
        self.sent = []

    def slot(self, name):
        k = self.steps.index(name)
        if k >= 2:
            self.pair[k - 2].wait_send()
        return k % 2

    def put(self, name, spot, slot, tile, zero, one):
        part, first, _ = CHUNKS[name]
        i, j, k = spot
        core = self.me["c"]
        self.total[part, i, j, k, first + tile] = jnp.where(core == 0, zero, one).astype(bf16)
        self.to_core[slot, i, j, k, tile] = jnp.where(core == 0, one, zero).astype(bf16)

    def send_pair(self, k):
        part, first, tiles = CHUNKS[self.steps[k]]
        self.pair.append(sending(
            self.to_core.at[k % 2, :, :, :, pl.ds(0, tiles)],
            self.from_core.at[part, :, :, :, pl.ds(first, tiles)],
            self.pair_send.at[k],
            self.pair_recv.at[k],
            other_core(self.me),
        ))
        self.pair[k].start()

    def combine(self, k):
        part, first, tiles = CHUNKS[self.steps[k]]
        self.pair[k].wait_recv()

        @pl.loop(0, 16)
        def _(i):
            for j in range(4):
                at = (part, i // 4, i % 4, j, pl.ds(first, tiles))
                self.total[at] = (self.total[at].astype(f32) + self.from_core[at].astype(f32)).astype(bf16)

        self.first_hop(k, 2, 0, 1, 1, 0)
        self.first_hop(k, 2, 1, 3, 1, 1)
        self.first_hop(k, 1, 1, 1, 2, 3)
        self.first_hop(k, 3, 0, 3, 0, 4)

    def half_slab(self, ref, k, slot, which):
        part, first, tiles = CHUNKS[self.steps[k]]
        return ref.at[part, slot, HALVES[which], :, pl.ds(first, tiles)]

    def axis(self, k):
        return ORDERS[CHUNKS[self.steps[k]][0]][0]

    def first_hop(self, k, by, which, step, slot, sem):
        axis = self.axis(k)
        copy = sending(
            self.half_slab(self.total, k, (self.me[axis] + by) % 4, which),
            self.half_slab(self.got_one, k, slot, which),
            self.one_send.at[k, sem],
            self.one_recv.at[k, sem],
            moved(self.me, axis, step),
        )
        copy.start()
        self.sent.append(copy)

    def first_got(self, k, which, slot, sem):
        there = self.half_slab(self.got_one, k, slot, which)
        sending(
            there,
            there,
            self.one_send.at[k, sem],
            self.one_recv.at[k, sem],
            moved(self.me, self.axis(k), 1),
        ).wait_recv()

    def relay(self, k):
        part, first, tiles = CHUNKS[self.steps[k]]
        for which, step, slot, sem in ((0, 1, 2, 2), (1, 3, 0, 5)):
            self.first_got(k, which, 1, which)
            to = (self.me[self.axis(k)] + step) % 4

            @pl.loop(0, 2)
            def _(i, which=which, to=to):
                for j in range(4):
                    at = (part, to, 2 * which + i, j, pl.ds(first, tiles))
                    more = self.got_one[part, 1, 2 * which + i, j, pl.ds(first, tiles)].astype(f32)
                    self.total[at] = (self.total[at].astype(f32) + more).astype(bf16)

            self.first_hop(k, step, which, step, slot, sem)

    def slab(self, part):
        return self.total.at[part, self.me[ORDERS[part][0]]]

    def first_sum(self, g):
        part, first, tiles = self.groups[g]
        slab, got = self.slab(part), self.got_one
        for k, name in enumerate(self.steps):
            if CHUNKS[name][0] == part and first <= CHUNKS[name][1] < first + tiles:
                self.first_got(k, 0, 2, 2)
                self.first_got(k, 1, 2, 3)
                self.first_got(k, 0, 0, 4)
                self.first_got(k, 1, 0, 5)

        @pl.loop(0, 16)
        def _(i):
            at = (i // 4, i % 4, pl.ds(first, tiles))
            value = slab[at].astype(f32)
            for s in (0, 2):
                value += got[part, s, i // 4, i % 4, pl.ds(first, tiles)].astype(f32)
            slab[at] = value.astype(bf16)

    def second(self, g):
        self.first_sum(g)
        self.send_second(g)

    def send_second(self, g):
        part, first, tiles = self.groups[g]
        two = ORDERS[part][1]
        for by in (2, 1, 3):
            copy = sending(
                self.slab(part).at[(self.me[two] + by) % 4, :, pl.ds(first, tiles)],
                self.got_two.at[part, 3 - by, :, pl.ds(first, tiles)],
                self.two_send.at[g, by - 1],
                self.two_recv.at[g, 3 - by],
                moved(self.me, two, by),
            )
            copy.start()
            self.sent.append(copy)

    def third(self, g):
        part, first, tiles = self.groups[g]
        _, two, three = ORDERS[part]
        me, got = self.me, self.got_two
        slab = self.slab(part).at[me[two]]
        for by in (1, 3, 2):
            there = got.at[part, by - 1, :, pl.ds(first, tiles)]
            sending(
                there, there, self.two_send.at[g, by - 1], self.two_recv.at[g, by - 1], moved(me, two, by)
            ).wait_recv()

        @pl.loop(0, 4)
        def _(i):
            at = (i, pl.ds(first, tiles))
            value = slab[at].astype(f32)
            for s in range(3):
                value += got[part, s, i, pl.ds(first, tiles)].astype(f32)
            slab[at] = value.astype(bf16)

        for by in (2, 1, 3):
            copy = sending(
                slab.at[(me[three] + by) % 4, pl.ds(first, tiles)],
                self.got_three.at[part, 3 - by, pl.ds(first, tiles)],
                self.three_send.at[g, by - 1],
                self.three_recv.at[g, 3 - by],
                moved(me, three, by),
            )
            copy.start()
            self.sent.append(copy)

    def last(self, g):
        part, first, tiles = self.groups[g]
        _, two, three = ORDERS[part]
        me, got = self.me, self.got_three
        for by in (1, 3, 2):
            there = got.at[part, by - 1, pl.ds(first, tiles)]
            sending(
                there, there, self.three_send.at[g, by - 1], self.three_recv.at[g, by - 1], moved(me, three, by)
            ).wait_recv()
        mine = self.slab(part).at[me[two], me[three], pl.ds(first, tiles)]
        value = mine[...].astype(f32)
        for s in range(3):
            value += got[part, s, pl.ds(first, tiles)].astype(f32)
        mine[...] = value.astype(bf16)
        return mine

    def finish(self):
        for copy in self.pair[-2:]:
            copy.wait_send()
        for copy in self.sent:
            copy.wait_send()


class LateSums(Sums):
    def __init__(self, me, groups, slab, buffers, sems):
        self.me, self.groups, self.kept = me, groups, slab
        self.got_two, self.got_three = buffers
        self.two_send, self.two_recv, self.three_send, self.three_recv = sems
        self.pair = []
        self.sent = []

    def slab(self, part):
        return self.kept.at[part]


def sums_scratch(tiles, widest, steps, groups, later=True):
    dma = pltpu.SemaphoreType.DMA
    buffers = [
        pltpu.VMEM((3, 4, 4, 4, tiles, 16, 128), bf16),
        pltpu.VMEM((3, 4, 4, 4, tiles, 16, 128), bf16),
        pltpu.VMEM((2, 4, 4, 4, widest, 16, 128), bf16),
        pltpu.VMEM((3, 3, 4, 4, tiles, 16, 128), bf16),
    ]
    sems = [dma((steps,)), dma((steps,)), dma((steps, 6)), dma((steps, 6))]
    if not later:
        return buffers + sems
    more, more_sems = late_scratch(tiles, groups)
    return buffers + more + sems + more_sems


def late_scratch(tiles, groups):
    return [
        pltpu.VMEM((3, 3, 4, tiles, 16, 128), bf16),
        pltpu.VMEM((3, 3, tiles, 16, 128), bf16),
    ], [pltpu.SemaphoreType.DMA((groups, 3))] * 4


def product(left, right):
    return lax.dot_general(left, right, (((1,), (0,)), ((), ())), preferred_element_type=f32)


def against(left, right):
    return lax.dot_general(left, right, (((1,), (1,)), ((), ())), preferred_element_type=f32)


def crossed(left, right):
    return lax.dot_general(left, right, (((0,), (0,)), ((), ())), preferred_element_type=f32)


def block(i, width=256):
    return pl.ds(pl.multiple_of(i * width, width), width)


def adapter_products(sums, held, name, gain=None):
    slot = sums.slot(name)

    def put(spot, tile, zero, one):
        sums.put(name, spot, slot, tile, zero, one)

    if name == "ffn":
        for j, (left, right) in enumerate((("u2a", "ggate"), ("u2b", "gup"))):

            @pl.loop(0, 2)
            def _(i, j=j, left=left, right=right):
                value = crossed(held[left][...], held[right][:, block(i, 1024)])
                for b in range(4):
                    for h in range(8):
                        for t in range(2):
                            lanes = slice(256 * b + 128 * t, 256 * b + 128 * t + 128)
                            put(
                                (2 * i + b // 2, (b % 2) * 2 + h // 4, h % 4),
                                j * 2 + t,
                                value[32 * h : 32 * h + 16, lanes],
                                value[32 * h + 16 : 32 * h + 32, lanes],
                            )

    elif name == "mix":
        for j, right in enumerate(("gu1a", "gu1b", "gu2a", "gu2b")):
            value = crossed(held["n1" if j < 2 else "n2"][...], held[right][...])
            for r in range(40):
                rows = slice(16 * r, 16 * r + 16)
                put(split_spot(16 * j + r // 4), r % 4, value[rows, :128], value[rows, 128:])
        for k in range(3):
            if k < 2:
                value = crossed(held["u1a"][...], held["gqp"][:, 512 * k : 512 * k + 512])
            else:
                value = crossed(held["u1b"][...], held["gkvp"][...])
            for t in range(4):
                lanes = slice(128 * t, 128 * t + 128)
                for h in range(8):
                    put(
                        split_spot((4 * k + t) // 3 * 16 + 10 + (4 * k + t) % 3 * 2 + h // 4),
                        h % 4,
                        value[32 * h : 32 * h + 16, lanes],
                        value[32 * h + 16 : 32 * h + 32, lanes],
                    )
    elif name == "attn":
        value = crossed(held["o"][...], held["guo"][...])
        for q in range(64):
            rows = slice(16 * q, 16 * q + 16)
            put(split_spot(q), 0, value[rows, :128], value[rows, 128:])
    elif name == "down":

        @pl.loop(0, 2)
        def _(i):
            value = crossed(held["m"][:, block(i, 1024)], held["gud"][...])
            for b in range(4):
                for h in range(8):
                    row = 256 * b + 32 * h
                    for t in range(2):
                        lanes = slice(128 * t, 128 * t + 128)
                        put(
                            (2 * i + b // 2, (b % 2) * 2 + h // 4, h % 4),
                            t,
                            value[row : row + 16, lanes],
                            value[row + 16 : row + 32, lanes],
                        )

    else:
        for b, (left, right) in enumerate((("uo", "ga"), ("ud", "gf"))):
            value = crossed(held[left][...], held[right][...])
            for g in range(16):
                tiles = [value[16 * g : 16 * g + 16, 128 * t : 128 * t + 128] for t in range(5)]
                q = 2 * (16 * b + g)
                put(split_spot(q), 0, tiles[0], tiles[2])
                put(split_spot(q), 1, tiles[1], tiles[3])
                more = tiles[4] if gain is None or q else gain
                put(split_spot(q + 1), 0, tiles[4], more)
                put(split_spot(q + 1), 1, tiles[4], tiles[4])


WEIGHT_ITEMS = (
    (1, 3, 0, 256),
    (2, 3, 256, 640),
    (0, 4, 0, 128),
    (0, 5, 0, 128),
    (0, 0, 0, 640),
    (1, 1, 0, 640),
    (2, 2, 0, 640),
)

NAMES = (
    ("m", 2048),
    ("gf", 640),
    ("gud", 256),
    ("ud", 256),
    ("n2", 640),
    ("ggate", 2048),
    ("gup", 2048),
    ("gu2a", 256),
    ("gu2b", 256),
    ("u2a", 256),
    ("u2b", 256),
    ("o", 1024),
    ("ga", 640),
    ("guo", 256),
    ("uo", 256),
    ("n1", 640),
    ("gqp", 1024),
    ("gkvp", 512),
    ("gu1a", 256),
    ("gu1b", 256),
    ("u1a", 256),
    ("u1b", 256),
)
BOTH = ("m", "gf", "n2", "ggate", "gup", "o", "ga", "n1", "gqp", "gkvp")
ORDER = {name: i for i, (name, _) in enumerate(NAMES)}
ADAPTERS = ((4, 640, 256), (256, 1536), (2, 256, 2048), (1024, 256), (2048, 256), (2, 256, 640))


CURVE = 0.7978845608028654
CUBE = 0.044715


def block_kernel(*refs):
    (tokens, cotangent, doc_row, doc_source, mixing, gains) = refs[:6]
    shards = refs[6:12]
    adapters_in = refs[12:18]
    outs = refs[18:]
    block_out, token_grad, gain_tile, slab_out = outs[:4]
    kept_out = dict(zip((name for name, _ in NAMES), outs[4 : 4 + len(NAMES)]))
    rest = outs[4 + len(NAMES) :]
    kept = dict(zip((name for name, _ in NAMES), rest[: len(NAMES)]))
    rest = rest[len(NAMES) :]
    whole = rest[:6]
    both_piece = rest[6]
    a_in, a_qkv, a_ffn, a_attn, a_down, a_back = rest[7:13]
    (cosine, sine, mask, stream, hidden, q_rot, k_rot, value, probs, gate, up, grad, normed, gain_sum) = rest[13:27]
    kept_sem, adapter_sem, piece_sem = rest[27:30]
    gather = rest[30:35]
    slab_sem = rest[35]
    late = rest[36:]

    me = place()
    quarter = (me["z"] % 2) * 2 + me["c"]
    w_gate, w_up, w_down, w_both, w_kv, w_kv_last = whole

    fetch = [
        pltpu.make_async_copy(shards[0], both_piece.at[:32], piece_sem.at[0]),
        pltpu.make_async_copy(shards[2], both_piece.at[32:], piece_sem.at[1]),
    ]
    for copy in fetch:
        copy.start()
    adapter_names = ("in", "qkv", "ffn", "attn", "down", "back")
    waiting = {}

    def load(name, loop):
        i = adapter_names.index(name)
        target = (a_in, a_qkv, a_ffn, a_attn, a_down, a_back)[i]
        waiting[name] = pltpu.make_async_copy(adapters_in[i].at[loop], target, adapter_sem.at[i])
        waiting[name].start()

    def need(name):
        if name in waiting:
            waiting.pop(name).wait()

    for name in adapter_names:
        load(name, 0)
    greet(chip_peers(me) + [other_core(me)])
    for copy in fetch:
        copy.wait()
    own = pl.ds(pl.multiple_of(quarter * 16, 16), 16)
    sources = (shards[3].at[own], shards[4].at[own], shards[5].at[own], both_piece.at[own])
    lanes_of_kv = pl.ds(pl.multiple_of(quarter * 128, 128), 128)
    sources += (shards[1].at[:, lanes_of_kv], shards[1].at[:, pl.ds(512, 128)])
    items = []
    for i, (part, array, low, high) in enumerate(WEIGHT_ITEMS):

        def region(fixed, core, array=array, low=low, high=high):
            every = slice(None)
            zh, zl = every, every
            if isinstance(fixed.get("z"), slice):
                zh = fixed["z"].start // 2
            elif "z" in fixed:
                zh, zl = fixed["z"] // 2, fixed["z"] % 2
            return whole[array].at[
                fixed.get("x", every), zh, fixed.get("y", every), zl, core, :, pl.ds(low, high - low)
            ]

        items.append(
            Gather(me, i, ORDERS[part][::-1], sources[array].at[:, pl.ds(low, high - low)], region, gather)
        )
    for item in items:
        item.start()

    rows_of = lax.broadcasted_iota(jnp.int32, (256, 256), 0)
    columns_of = lax.broadcasted_iota(jnp.int32, (256, 256), 1)
    along = jnp.broadcast_to(doc_row[...], (256, 256))
    down = jnp.sum(jnp.where(rows_of == columns_of, along, 0), axis=1, keepdims=True)
    before = jnp.sum(jnp.where(along < down, 1, 0), axis=1, keepdims=True)
    mask[...] = jnp.where((along == down) & (columns_of <= rows_of), 1.0, 0.0)
    position = (lax.broadcasted_iota(jnp.int32, (256, 1), 0) - before).astype(f32)
    lanes = lax.broadcasted_iota(jnp.int32, (1, 128), 1).astype(f32)
    frequency = jnp.exp(lanes * (-2.0 / 256) * jnp.log(f32(rope_base)))
    angle = position * frequency
    cosine[...] = jnp.cos(angle)
    sine[...] = jnp.sin(angle)
    ratios = jnp.float32(0)
    for i in range(8):
        ratios += mixing[i].astype(f32)
    weight = jnp.zeros((256, 1), f32)
    for i in range(4):
        scale = mixing[doc_source[0, i]].astype(f32) * 8.0 / ratios
        weight = jnp.where(down == i, scale, weight)
    stream[0] = tokens[...].astype(f32)
    grad[...] = cotangent[...].astype(f32) * weight
    gain_sum[...] = jnp.zeros_like(gain_sum)
    soon, later = items[:4], items[4:]
    for item in items:
        item.arrive(0)
        item.spread(1)
    for item in soon:
        item.arrive(1)
        item.begin_ring()
    for item in later:
        item.arrive(1)
    for item in soon:
        item.turn_ring()
    for item in later:
        item.begin_ring()
    for item in soon:
        item.end_ring()

    def first_weights():
        for item in soon:
            item.finish()

    def turn_weights():
        for item in later:
            item.turn_ring()

    def rest_of_weights():
        for item in later:
            item.end_ring()
        for item in later:
            item.finish()

    def wide_rows(array, i):
        return array[i].reshape(512, 640)

    def q_rows(i):
        return w_both[i, :, :, 0].reshape(256, 640)

    def o_rows(i):
        return w_both[i, :, :, 1].reshape(256, 640)

    def kv_rows(i):
        return kv_of(slice(2 * i, 2 * i + 2), 256)

    def kv_of(x, rows):
        tiles = [w_kv[x, :, :, low, core].reshape(rows, 128) for low in range(2) for core in range(2)]
        return jnp.concatenate([*tiles, w_kv_last[x, :, :, 0, 0].reshape(rows, 128)], axis=1)

    def q_all():
        return w_both[:, :, :, 0].reshape(1024, 640)

    def o_all():
        return w_both[:, :, :, 1].reshape(1024, 640)

    def kv_all():
        return kv_of(slice(0, 4), 512)

    def all_rows(array):
        return array[...].reshape(2048, 640)

    scale = 256 ** (-0.5)

    def rotated(first, second, sign):
        c = cosine[...]
        s = sine[...] * sign
        return first * c - second * s, second * c + first * s

    def out_of(name, loop):
        target = kept_out[name].at[loop] if name in BOTH else kept_out[name]
        return pltpu.make_async_copy(kept[name], target, kept_sem.at[ORDER[name]])

    leaving = set()

    def to_hbm(names, loop):
        for name in names:
            if loop == 0 or name in BOTH:
                out_of(name, loop).start()
                leaving.add((name, loop))

    def drained(names, loop):
        for name in names:
            if (name, loop) in leaving:
                leaving.discard((name, loop))
                out_of(name, loop).wait()

    def norm(source, gain, target):
        for i in range(4):
            rows = slice(64 * i, 64 * i + 64)
            x = source[rows, :]
            inverse = lax.rsqrt(jnp.mean(x * x, axis=-1, keepdims=True) + eps)
            target[rows, :] = (x * inverse * gain).astype(bf16)

    first_names = ("n1", "u1a", "u1b", "o", "uo")
    second_names = ("n2", "u2a", "u2b", "m", "ud")

    def forward(loop):
        drained(first_names, 0)
        need("in")
        norm(stream.at[loop], gains[0:1, :], kept["n1"])
        kept["u1a"][...] = product(kept["n1"][...], a_in[0]).astype(bf16)
        kept["u1b"][...] = product(kept["n1"][...], a_in[1]).astype(bf16)

        need("qkv")
        if loop == 0:
            first_weights()
        k_pre = against(kept["n1"][...], kv_rows(0)) + product(kept["u1b"][...], a_qkv[:, 1024:1280])
        first, second = rotated(k_pre[:, :128], k_pre[:, 128:], 1.0)
        k_rot[loop, :, :128] = first.astype(bf16)
        k_rot[loop, :, 128:] = second.astype(bf16)
        value[loop] = (
            against(kept["n1"][...], kv_rows(1)) + product(kept["u1b"][...], a_qkv[:, 1280:1536])
        ).astype(bf16)

        if loop == 0:
            turn_weights()
        for h in range(4):
            at = slice(256 * h, 256 * h + 256)
            q_pre = against(kept["n1"][...], q_rows(h)) + product(kept["u1a"][...], a_qkv[:, at])
            first, second = rotated(q_pre[:, :128], q_pre[:, 128:], 1.0)
            q_rot[loop, h, :, :128] = first.astype(bf16)
            q_rot[loop, h, :, 128:] = second.astype(bf16)
            scores = against(q_rot[loop, h], k_rot[loop]) * scale
            scores = jnp.where(mask[...] > 0.5, scores, masked)
            expo = jnp.exp(scores - jnp.max(scores, axis=-1, keepdims=True))
            p = expo * (1.0 / jnp.sum(expo, axis=-1, keepdims=True))
            probs[loop, h] = p
            kept["o"][:, at] = product(p.astype(bf16), value[loop]).astype(bf16)

        if loop == 0:
            load("qkv", 1)
        need("attn")
        need("back")
        kept["uo"][...] = product(kept["o"][...], a_attn[...]).astype(bf16)
        hidden[loop] = stream[loop] + (
            product(kept["o"][...], o_all()) + product(kept["uo"][...], a_back[0])
        )
        to_hbm(first_names, loop)
        if loop == 0:
            load("attn", 1)
        drained(second_names, 0)
        if loop == 0:
            rest_of_weights()
        norm(hidden.at[loop], gains[1:2, :], kept["n2"])
        kept["u2a"][...] = product(kept["n2"][...], a_in[2]).astype(bf16)
        kept["u2b"][...] = product(kept["n2"][...], a_in[3]).astype(bf16)
        if loop == 0:
            load("in", 1)
        need("ffn")

        for i in range(4):
            at = slice(512 * i, 512 * i + 512)
            g = against(kept["n2"][...], wide_rows(w_gate, i)) + product(
                kept["u2a"][...], a_ffn[0, :, at]
            )
            u = against(kept["n2"][...], wide_rows(w_up, i)) + product(
                kept["u2b"][...], a_ffn[1, :, at]
            )
            gate[loop, :, at] = g
            up[loop, :, at] = u
            bend = jnp.tanh(CURVE * (g + CUBE * g * g * g))
            kept["m"][:, at] = (0.5 * g * (1.0 + bend) * u).astype(bf16)

        if loop == 0:
            load("ffn", 1)
        need("down")
        kept["ud"][...] = product(kept["m"][...], a_down[...]).astype(bf16)
        stream[loop + 1] = hidden[loop] + (
            product(kept["m"][...], all_rows(w_down)) + product(kept["ud"][...], a_back[1])
        )
        to_hbm(second_names, loop)
        if loop == 0:
            load("down", 1)
            load("back", 1)

    def norm_back(source, which):
        gain = gains[which : which + 1, :]

        for i in range(4):
            rows = slice(64 * i, 64 * i + 64)
            x = source[rows, :]
            g = normed[rows, :]
            inverse = lax.rsqrt(jnp.mean(x * x, axis=-1, keepdims=True) + eps)
            scaled = g * gain
            step = inverse * (
                scaled - x * inverse * inverse * jnp.mean(scaled * x, axis=-1, keepdims=True)
            )
            grad[rows, :] = grad[rows, :] + step
            gain_sum[which : which + 1, :] += jnp.sum(g * x * inverse, axis=0, keepdims=True)

    ffn_names = ("gf", "gud", "ggate", "gup", "gu2a", "gu2b")
    attention_names = ("ga", "guo", "gqp", "gkvp", "gu1a", "gu1b")

    def backward_ffn(loop):
        drained(ffn_names, 1)
        need("back")
        need("down")
        kept["gf"][...] = grad[...].astype(bf16)
        kept["gud"][...] = against(kept["gf"][...], a_back[1]).astype(bf16)

        for i in range(4):
            at = slice(512 * i, 512 * i + 512)
            gm = against(kept["gf"][...], wide_rows(w_down, i)) + against(
                kept["gud"][...], a_down[at, :]
            )
            g = gate[loop, :, at]
            u = up[loop, :, at]
            square = g * g
            bend = jnp.tanh(CURVE * (g + CUBE * g * square))
            half = 0.5 * (1.0 + bend)
            slope = half + 0.5 * g * (1.0 - bend * bend) * (CURVE * (1.0 + 3.0 * CUBE * square))
            kept["ggate"][:, at] = (gm * u * slope).astype(bf16)
            kept["gup"][:, at] = (gm * (g * half)).astype(bf16)

        need("ffn")
        kept["gu2a"][...] = against(kept["ggate"][...], a_ffn[0]).astype(bf16)
        kept["gu2b"][...] = against(kept["gup"][...], a_ffn[1]).astype(bf16)
        to_hbm(ffn_names, loop)

    def backward_hidden(loop):
        need("in")
        normed[...] = (
            product(kept["ggate"][...], all_rows(w_gate))
            + product(kept["gup"][...], all_rows(w_up))
            + against(kept["gu2a"][...], a_in[2])
            + against(kept["gu2b"][...], a_in[3])
        )
        norm_back(hidden.at[loop], 1)

    def backward_attention(loop):
        drained(attention_names, 1)
        need("attn")
        kept["ga"][...] = grad[...].astype(bf16)
        kept["guo"][...] = against(kept["ga"][...], a_back[0]).astype(bf16)

        def head(h, carry):
            grad_key, grad_value = carry
            at = slice(256 * h, 256 * h + 256)
            go = (
                against(kept["ga"][...], o_rows(h)) + against(kept["guo"][...], a_attn[at, :])
            ).astype(bf16)
            p = probs[loop, h]
            gp = against(go, value[loop])
            gs = (p * (gp - jnp.sum(p * gp, axis=-1, keepdims=True))).astype(bf16)
            gq = product(gs, k_rot[loop]) * scale
            first, second = rotated(gq[:, :128], gq[:, 128:], -1.0)
            kept["gqp"][:, 256 * h : 256 * h + 128] = first.astype(bf16)
            kept["gqp"][:, 256 * h + 128 : 256 * h + 256] = second.astype(bf16)
            grad_key += crossed(gs, q_rot[loop, h])
            grad_value += crossed(p.astype(bf16), go)
            return grad_key, grad_value

        sums_of_heads = (jnp.zeros((256, 256), f32), jnp.zeros((256, 256), f32))
        for h in range(4):
            sums_of_heads = head(h, sums_of_heads)
        grad_key, grad_value = sums_of_heads
        grad_key = grad_key * scale
        first, second = rotated(grad_key[:, :128], grad_key[:, 128:], -1.0)
        kept["gkvp"][:, :128] = first.astype(bf16)
        kept["gkvp"][:, 128:256] = second.astype(bf16)
        kept["gkvp"][:, 256:] = grad_value.astype(bf16)
        need("qkv")
        kept["gu1a"][...] = against(kept["gqp"][...], a_qkv[:, :1024]).astype(bf16)
        kept["gu1b"][...] = against(kept["gkvp"][...], a_qkv[:, 1024:]).astype(bf16)
        to_hbm(attention_names, loop)

    def backward_stream(loop):
        normed[...] = (
            product(kept["gqp"][...], q_all())
            + product(kept["gkvp"][...], kv_all())
            + against(kept["gu1a"][...], a_in[0])
            + against(kept["gu1b"][...], a_in[1])
        )
        norm_back(stream.at[loop], 0)

    sums = Sums(me, LATE_STEPS, ADAPTER_GROUPS, late[:4], late[4:])

    def summing(name):
        adapter_products(sums, kept, name)
        sums.send_pair(LATE_STEPS.index(name))

    forward(0)
    forward(1)
    block_out[...] = stream[2].astype(bf16)
    backward_ffn(1)
    summing("ffn")
    summing("down")
    backward_hidden(1)
    sums.combine(0)
    backward_attention(1)
    sums.combine(1)
    summing("mix")
    sums.relay(0)
    backward_stream(1)
    for name in ("back", "down", "ffn", "in", "attn", "qkv"):
        load(name, 0)
    sums.combine(2)
    summing("attn")
    sums.relay(1)
    summing("back")
    backward_ffn(0)
    sums.combine(3)
    sums.combine(4)
    sums.relay(2)
    backward_hidden(0)
    sums.relay(3)
    sums.relay(4)
    backward_attention(0)
    backward_stream(0)
    token_grad[...] = grad[...]
    gain_tile[...] = jnp.zeros_like(gain_tile)
    for i in range(2):
        for t in range(5):
            gain_tile[5 * i + t : 5 * i + t + 1, :] = gain_sum[i : i + 1, 128 * t : 128 * t + 128]
    for g in range(3):
        sums.first_sum(g)
    slab_copies = []
    for part in range(3):
        slab_copies.append(pltpu.make_async_copy(sums.slab(part), slab_out.at[part], slab_sem.at[part]))
        slab_copies[-1].start()
    sums.finish()
    for item in items:
        item.close()
    for copy in slab_copies:
        copy.wait()
    for names in (first_names, second_names, ffn_names, attention_names):
        for loop in range(2):
            drained(names, loop)


def block_pass(tokens, cotangent, doc_ids, doc_source, mixing, norm_gains, shards, adapters):
    vmem = pl.BlockSpec(memory_space=pltpu.VMEM)
    smem = pl.BlockSpec(memory_space=pltpu.SMEM)
    anywhere = pl.BlockSpec(memory_space=pl.ANY)
    dma = pltpu.SemaphoreType.DMA
    return pl.pallas_call(
        block_kernel,
        out_shape=[
            jax.ShapeDtypeStruct((256, 640), bf16),
            jax.ShapeDtypeStruct((256, 640), f32),
            jax.ShapeDtypeStruct((16, 128), f32),
            jax.ShapeDtypeStruct((3, 4, 4, 5, 16, 128), bf16),
        ]
        + [
            jax.ShapeDtypeStruct((2, 256, width) if name in BOTH else (256, width), bf16)
            for name, width in NAMES
        ],
        in_specs=[vmem, vmem, vmem, smem, smem, vmem] + [anywhere] * 12,
        out_specs=[vmem] * 3 + [anywhere] * (1 + len(NAMES)),
        scratch_shapes=[pltpu.VMEM((256, width), bf16) for _, width in NAMES]
        + [pltpu.VMEM((4, 2, 4, 2, 2, 16, 640), bf16)] * 4
        + [pltpu.VMEM((4, 2, 4, 2, 2, 16, 128), bf16)] * 2
        + [pltpu.VMEM((64, 640), bf16)]
        + [pltpu.VMEM(shape, bf16) for shape in ADAPTERS]
        + [
            pltpu.VMEM((256, 128), f32),
            pltpu.VMEM((256, 128), f32),
            pltpu.VMEM((256, 256), f32),
            pltpu.VMEM((3, 256, 640), f32),
            pltpu.VMEM((2, 256, 640), f32),
            pltpu.VMEM((2, 4, 256, 256), bf16),
            pltpu.VMEM((2, 256, 256), bf16),
            pltpu.VMEM((2, 256, 256), bf16),
            pltpu.VMEM((2, 4, 256, 256), f32),
            pltpu.VMEM((2, 256, 2048), f32),
            pltpu.VMEM((2, 256, 2048), f32),
            pltpu.VMEM((256, 640), f32),
            pltpu.VMEM((256, 640), f32),
            pltpu.VMEM((2, 640), f32),
            dma((len(NAMES),)),
            dma((6,)),
            dma((2,)),
        ]
        + gather_sems(len(WEIGHT_ITEMS))
        + [dma((3,))]
        + sums_scratch(5, 4, len(LATE_STEPS), len(ADAPTER_GROUPS), later=False),
        compiler_params=pltpu.CompilerParams(
            collective_id=1, has_side_effects=True, vmem_limit_bytes=60 * 2**20
        ),
        name="block",
    )(tokens, cotangent, doc_ids, doc_source, mixing, norm_gains, *shards, *adapters)


NEEDS = {
    "attn": ("o", "guo"),
    "mix": ("n1", "n2", "gu1a", "gu1b", "gu2a", "gu2b", "u1a", "gqp", "u1b", "gkvp"),
    "ffn": ("u2a", "ggate", "u2b", "gup"),
    "down": ("m", "gud"),
    "back": ("uo", "ga", "ud", "gf"),
}
LOAD_ORDER = tuple(name for step in STEPS[:5] for name in NEEDS[step])
SHARED_OPERANDS = {
    "gate": ("ggate", "n2"),
    "up": ("gup", "n2"),
    "wdown": ("m", "gf"),
    "q": ("gqp", "n1"),
    "o": ("o", "ga"),
    "kv": ("gkvp", "n1"),
}


def shared_products(sums, held, name):
    slot = sums.slot(name)
    order = ORDERS[CHUNKS[name][0]]
    left, right = (held[operand] for operand in SHARED_OPERANDS[name])
    right = right[...].reshape(512, 640)

    if name in ("gate", "up", "wdown"):

        @pl.loop(0, 2)
        def _(i):
            value = crossed(left[:, :, block(i, 1024)].reshape(512, 1024), right)
            for x in range(2):
                for high in range(2):
                    for y in range(4):
                        for low in range(2):
                            row = 512 * x + 256 * high + 64 * y + 32 * low
                            for t in range(5):
                                lanes = slice(128 * t, 128 * t + 128)
                                sums.put(
                                    name,
                                    chip_spot(order, 2 * i + x, y, high * 2 + low),
                                    slot,
                                    t,
                                    value[row : row + 16, lanes],
                                    value[row + 16 : row + 32, lanes],
                                )

    elif name in ("q", "o"):
        value = crossed(left[...].reshape(512, 1024), right)
        for x in range(4):
            for high in range(2):
                for y in range(4):
                    for low in range(2):
                        row = 256 * x + 128 * high + 32 * y + 16 * low
                        tiles = [value[row : row + 16, 128 * t : 128 * t + 128] for t in range(5)]
                        for t in range(3):
                            sums.put(
                                name,
                                chip_spot(order, x, y, high * 2 + low),
                                slot,
                                t,
                                tiles[t],
                                tiles[min(t + 3, 4)],
                            )
    else:
        value = crossed(left[...].reshape(512, 512), right)
        for k in range(32):
            tiles = [value[16 * k : 16 * k + 16, 128 * t : 128 * t + 128] for t in range(5)]
            for low, ends in enumerate((((0, 3), (1, 3)), ((2, 4), (2, 4)))):
                for t, (zero, one) in enumerate(ends):
                    sums.put(
                        name,
                        chip_spot(order, k // 8, k % 4, (k // 4) % 2 * 2 + low),
                        slot,
                        t,
                        tiles[zero],
                        tiles[one],
                    )


def grads_kernel(*refs):
    count = len(NAMES)
    given = dict(zip((name for name, _ in NAMES), refs[:count]))
    gain_ref, slab_ref = refs[count : count + 2]
    all_ref, share_ref = refs[count + 2 : count + 4]
    rest = refs[count + 4 :]
    held = dict(zip((name for name, _ in NAMES), rest[:count]))
    load_sem, share_send, share_recv, share_local = rest[count : count + 4]
    gather = rest[count + 4 : count + 9]
    me = place()
    slab, slab_sem = rest[count + 9 : count + 11]
    after = rest[count + 11 :]
    late_sums = LateSums(me, ADAPTER_GROUPS, slab, after[:2], after[2:6])
    sums = Sums(me, STEPS, GROUPS, after[6:12], after[12:])

    slab_copy = pltpu.make_async_copy(slab_ref, slab, slab_sem)
    slab_copy.start()

    loads = {}
    for i, name in enumerate(LOAD_ORDER):
        loads[name] = pltpu.make_async_copy(given[name], held[name], load_sem.at[i])
        loads[name].start()
    greet(chip_peers(me) + [other_core(me), other_core(other_low(me))])

    def spreading(loop, g, piece):
        part, first, tiles = GROUPS[g]
        order = ORDERS[part]

        def region(fixed, core):
            spot = tuple(fixed.get(axis, slice(None)) for axis in order)
            return all_ref.at[(loop, core, part, *spot, pl.ds(first, tiles))]

        item = Gather(me, loop * 3 + part, order[::-1], piece, region, gather)
        item.start()
        return item

    def near(items):
        for item in items:
            item.arrive(0)
            item.spread(1)

    def ring(items):
        for item in items:
            item.arrive(1)
            item.begin_ring()

    def turn(items):
        for item in items:
            item.turn_ring()

    def end(items):
        for item in items:
            item.end_ring()

    shares = []

    def share(g):
        part, first, tiles = GROUPS[g]
        mine = sums.last(g)
        low = me["z"] % 2

        def spot(low, core):
            return share_ref.at[low * 2 + core, part, pl.ds(0, tiles)]

        local = pltpu.make_async_copy(mine, spot(low, me["c"]), share_local.at[part])
        local.start()
        shares.append(local.wait)
        for k, peer in enumerate(
            (other_low(me), other_core(me), other_core(other_low(me)))
        ):
            copy = sending(
                mine, spot(low, me["c"]), share_send.at[part, k], share_recv.at[part, k], peer
            )
            copy.start()
            sums.sent.append(copy)
            there = spot(peer["z"] % 2, peer["c"])
            shares.append(
                sending(there, there, share_send.at[part, k], share_recv.at[part, k], peer).wait_recv
            )

    def summing(k):
        name = STEPS[k]
        if name in NEEDS:
            for operand in NEEDS[name]:
                loads[operand].wait()
            first_loop = {n: held[n].at[0] if n in BOTH else held[n] for n in held}
            adapter_products(sums, first_loop, name, gain_ref[...])
        else:
            shared_products(sums, held, name)
        sums.send_pair(k)

    def each(task, groups):
        for g in groups:
            task(g)

    slab_copy.wait()
    each(late_sums.send_second, range(3))
    late, early = [], []
    adapter_groups, shared_groups = range(3), range(3, 6)
    summing(0)
    summing(1)
    summing(2)
    sums.combine(0)
    summing(3)
    summing(4)
    each(late_sums.third, adapter_groups)
    sums.combine(2)
    sums.relay(0)
    sums.combine(3)
    sums.combine(1)
    summing(5)
    summing(6)
    sums.combine(4)
    late.extend(spreading(1, g, late_sums.last(g)) for g in adapter_groups)
    summing(7)
    sums.relay(1)
    sums.relay(2)
    sums.combine(7)
    sums.relay(4)
    sums.combine(5)
    sums.combine(6)
    sums.relay(3)
    summing(8)
    near(late)
    sums.combine(8)
    summing(9)
    each(sums.second, adapter_groups)
    sums.relay(7)
    sums.relay(6)
    sums.relay(5)
    summing(10)
    sums.combine(9)
    sums.combine(10)
    sums.relay(8)
    each(sums.third, adapter_groups)
    ring(late)
    early.extend(spreading(0, g, sums.last(g)) for g in adapter_groups)
    sums.relay(9)
    sums.relay(10)
    turn(late)
    near(early)
    each(sums.second, shared_groups)
    ring(early)
    each(sums.third, shared_groups)
    turn(early)
    end(late)
    each(share, shared_groups)
    end(early)
    for item in late + early:
        item.finish()
    for item in late + early:
        item.close()
    sums.finish()
    late_sums.finish()
    for wait in shares:
        wait()


def summed_gradients(kept, gain_tile, slab):
    anywhere = pl.BlockSpec(memory_space=pl.ANY)
    vmem = pl.BlockSpec(memory_space=pltpu.VMEM)
    dma = pltpu.SemaphoreType.DMA
    more, more_sems = late_scratch(5, len(ADAPTER_GROUPS))
    return pl.pallas_call(
        grads_kernel,
        out_shape=[
            jax.ShapeDtypeStruct((2, 2, 3, 4, 4, 4, 5, 16, 128), bf16),
            jax.ShapeDtypeStruct((4, 3, 8, 16, 128), bf16),
        ],
        in_specs=[anywhere] * len(NAMES) + [vmem, anywhere],
        out_specs=[anywhere] * 2,
        scratch_shapes=[
            pltpu.VMEM((2, 256, width) if name in BOTH else (256, width), bf16)
            for name, width in NAMES
        ]
        + [
            dma((len(NAMES),)),
            dma((3, 3)),
            dma((3, 3)),
            dma((3,)),
        ]
        + gather_sems(6)
        + [pltpu.VMEM((3, 4, 4, 5, 16, 128), bf16), dma]
        + more
        + more_sems
        + sums_scratch(12, 5, len(STEPS), len(GROUPS)),
        compiler_params=pltpu.CompilerParams(
            collective_id=2, has_side_effects=True, vmem_limit_bytes=60 * 2**20
        ),
        name="grads",
    )(*kept, gain_tile, slab)


def unpack_kernel(all_ref, share_ref, *outs):
    (gain, wq, wkv, wo, wgate, wup, wdown, w_in, w_qkv, w_ffn, w_attn, w_down, w_back) = outs
    loop, step = pl.program_id(0), pl.program_id(1)

    for q in range(16):
        for core in range(2):
            row = slice(32 * (q % 8) + 16 * core, 32 * (q % 8) + 16 * core + 16)
            for j in range(2):
                for t in range(2):
                    lanes = slice(256 * (q // 8) + 128 * t, 256 * (q // 8) + 128 * t + 128)
                    w_ffn[0, j, row, lanes] = all_ref[0, core, 0, q, 2 * j + t].astype(f32)
            rows = slice(16 * q, 16 * q + 16)
            w_attn[0, rows, 128 * core : 128 * core + 128] = all_ref[0, core, 2, q, 0].astype(f32)
            for t in range(2):
                w_down[0, 32 * q + 16 * core : 32 * q + 16 * core + 16, 128 * t : 128 * t + 128] = all_ref[
                    0, core, 2, q, 1 + t
                ].astype(f32)
    for g in range(8):
        rows = slice(16 * g, 16 * g + 16)
        for t, (more, core, tile) in enumerate(((0, 0, 3), (0, 0, 4), (0, 1, 3), (0, 1, 4), (1, 0, 3))):
            w_back[0, 0, rows, 128 * t : 128 * t + 128] = all_ref[0, core, 2, 2 * g + more, tile].astype(f32)
    for core in range(2):
        for r in range(40):
            w_in[0, 0, 16 * r : 16 * r + 16, 128 * core : 128 * core + 128] = all_ref[
                0, core, 1, r // 4, r % 4
            ].astype(f32)
        for t in range(3):
            for h in range(8):
                w_qkv[0, 32 * h + 16 * core : 32 * h + 16 * core + 16, 128 * t : 128 * t + 128] = all_ref[
                    0, core, 1, 10 + 2 * t + h // 4, h % 4
                ].astype(f32)

    @pl.when((loop == 0) & (step == 0))
    def _():
        tile = all_ref[0, 1, 2, 1, 3].astype(f32)
        for i in range(2):
            for t in range(5):
                gain[i : i + 1, 128 * t : 128 * t + 128] = tile[5 * i + t : 5 * i + t + 1, :]

        def mine(low, core, part, t):
            return share_ref[low * 2 + core, part, t].astype(f32)

        def wide(part, first):
            rows = []
            for low in range(2):
                for core in range(2):
                    rows.append(jnp.concatenate([mine(low, core, part, first + t) for t in range(5)], axis=1))
            return jnp.concatenate(rows, axis=0)

        def narrow(part, first):
            rows = []
            for low in range(2):
                tiles = [mine(low, 0, part, first + t) for t in range(3)]
                tiles += [mine(low, 1, part, first + t) for t in range(2)]
                rows.append(jnp.concatenate(tiles, axis=1))
            return jnp.concatenate(rows, axis=0)

        wgate[...] = wide(0, 0)
        wup[...] = wide(1, 0)
        wdown[...] = wide(2, 0)
        wq[...] = narrow(0, 5)
        wo[...] = narrow(1, 5)
        kv = [mine(0, 0, 2, 5), mine(0, 0, 2, 6), mine(1, 0, 2, 5), mine(0, 1, 2, 5), mine(1, 1, 2, 5)]
        wkv[...] = jnp.concatenate(kv, axis=1)


def unpacked(everything, shares):
    def whole(*shape):
        return jax.ShapeDtypeStruct(shape, f32), pl.BlockSpec(shape, lambda l, s: (0,) * len(shape))

    def cut(shape, size, index):
        return jax.ShapeDtypeStruct(shape, f32), pl.BlockSpec(size, index)

    outs = [
        whole(2, 640),
        whole(32, 640),
        whole(16, 640),
        whole(32, 640),
        whole(64, 640),
        whole(64, 640),
        whole(64, 640),
        cut((2, 4, 640, 256), (1, 1, 640, 256), lambda l, s: (l, s, 0, 0)),
        cut((2, 256, 1536), (1, 256, 384), lambda l, s: (l, 0, s)),
        cut((2, 2, 256, 2048), (1, 2, 256, 512), lambda l, s: (l, 0, 0, s)),
        cut((2, 1024, 256), (1, 256, 256), lambda l, s: (l, s, 0)),
        cut((2, 2048, 256), (1, 512, 256), lambda l, s: (l, s, 0)),
        cut((2, 2, 256, 640), (1, 1, 128, 640), lambda l, s: (l, s // 2, s % 2, 0)),
    ]
    everything = everything.reshape(2, 2, 3, 64, 5, 16, 128)
    return pl.pallas_call(
        unpack_kernel,
        grid=(2, 4),
        out_shape=[shape for shape, _ in outs],
        in_specs=[
            pl.BlockSpec((1, 2, 3, 16, 5, 16, 128), lambda l, s: (l, 0, 0, s, 0, 0, 0)),
            pl.BlockSpec((4, 3, 8, 16, 128), lambda l, s: (0, 0, 0, 0, 0)),
        ],
        out_specs=[spec for _, spec in outs],
        compiler_params=pltpu.CompilerParams(vmem_limit_bytes=60 * 2**20),
        name="unpack",
    )(everything, shares)


def body(
    tokens,
    cotangent,
    doc_ids,
    doc_source,
    mixing,
    norm_gains,
    wq,
    wkv,
    wo,
    wgate,
    wup,
    wdown,
    *adapters,
):
    shards = (wq.T, wkv.T, wo, wgate.T, wup.T, wdown)
    block_out, token_grad, gain_tile, slab, *kept = block_pass(
        tokens, cotangent, doc_ids, doc_source, mixing, norm_gains, shards, adapters
    )
    everything, shares = summed_gradients(kept, gain_tile, slab)
    gain, wq_sum, wkv_sum, wo_sum, wgate_sum, wup_sum, wdown_sum, *sums = unpacked(everything, shares)
    return (
        block_out,
        token_grad,
        gain,
        wq_sum.T,
        wkv_sum.T,
        wo_sum,
        wgate_sum.T,
        wup_sum.T,
        wdown_sum,
        *sums,
    )


def solution(mesh):
    rows = P(("loop", "dp"), None)
    columns = P(None, "dp")
    placed = (
        *(rows,) * 4,
        P(),
        P(),
        columns,
        columns,
        P("dp", None),
        columns,
        columns,
        P("dp", None),
        *(P(),) * 6,
    )
    return jax.shard_map(
        body,
        mesh=mesh,
        in_specs=placed,
        out_specs=(
            rows,
            rows,
            P(),
            columns,
            columns,
            P("dp", None),
            columns,
            columns,
            P("dp", None),
            *(P(),) * 6,
        ),
        check_vma=False,
    )
```
